32 devices in a mesh: scene: 2 (over y), sp: 4 (over z), hd: 4 (over x, core).
Axes of the slice: x: 2, y: 2, z: 4, core: 2. Of those that a mesh axis runs over, the one named last changes fastest.
Arguments:
- tokens: bfloat16 [16384, 1024], P(('scene', 'sp')), parts along dimension 0, may hold values from -110 to 110
- norm_gain: bfloat16 [1024], replicated, may hold values from 0.099609375 to 1.8984375
- reduce_gain: bfloat16 [1024], replicated, may hold values from 0.099609375 to 1.8984375
- query_weight: bfloat16 [1024, 1024], P('sp', 'hd'), may hold values from -1 to 1
- key_weight: bfloat16 [1024, 1024], P('sp', 'hd'), may hold values from -1 to 1
- value_weight: bfloat16 [1024, 1024], P('sp', 'hd'), may hold values from -0.1875 to 0.1875
- out_weight: bfloat16 [1024, 1024], P('sp', 'hd'), may hold values from -0.1875 to 0.1875
- out_cotangent: bfloat16 [16384, 1024], P(('scene', 'sp')), parts along dimension 0, may hold values from -6 to 6
Outputs:
- branch: bfloat16 [16384, 1024], P(('scene', 'sp'), 'hd'), parts along dimension 0
- input_grad: bfloat16 [16384, 1024], P(('scene', 'sp'), 'hd'), parts along dimension 0
- query_grad: float32 [2048, 1024], P(('scene', 'sp'), 'hd'), parts along dimension 0
- key_grad: float32 [2048, 1024], P(('scene', 'sp'), 'hd'), parts along dimension 0
- value_grad: float32 [2048, 1024], P(('scene', 'sp'), 'hd'), parts along dimension 0
- out_grad: float32 [2048, 1024], P(('scene', 'sp'), 'hd'), parts along dimension 0
The draws below stay inside these ranges and needn't reach their ends.
There are 2 independent parts, one for each index of `scene`. The reference program is written for one: setup_inputs(seed, part) draws one part's arguments, and reference() takes and returns one part's arrays. A program takes and returns all parts, laid end to end along the dimension named above; an argument that names none is the same for every part. Nothing has to cross between parts.
All inputs are finite; a program needn't handle non-finite values.
Results may differ from the reference program's by a relative error of at most 0.015.
The reference program's roundings to bfloat16 on the way count: a program that leaves them out, or rounds other values in their place, can miss the bound.
Values may be sent and summed in bfloat16 or wider, within the bound.
No kernel may reach another device: no remote copies, remote signals or barrier semaphores. Data moves between devices by JAX's collectives and lax.ppermute only.
A program may use at most 128 MiB of HBM per device.

```python
import math
import jax
import jax.numpy as jnp
from jax import lax

D = 1024
HEADS = 16
HEAD_DIM = 64
POOL = 8
GRID_W = 128
ROWS = 64
TOKENS = 8192
REDUCED = 128
N_HD = 4


def draw_tokens(key, part):
    key = jax.random.fold_in(key, 11)
    columns = jnp.arange(D, dtype=jnp.float32)
    trend_up = jnp.exp(math.log(3.0) * (columns / D - 0.5))
    col_scale = jnp.exp(jax.random.uniform(jax.random.fold_in(key, 1), (D,), minval=math.log(0.3), maxval=math.log(3.0))) * trend_up
    row_scale = jnp.exp(jax.random.uniform(jax.random.fold_in(key, 3), (TOKENS, 1), minval=math.log(0.5), maxval=math.log(2.0)))
    values = jax.random.truncated_normal(jax.random.fold_in(key, 2), -4.0, 4.0, (TOKENS, D)) * col_scale[None, :] * row_scale
    return values.astype(jnp.bfloat16)


def draw_query_weight(key, part):
    own_key = jax.random.fold_in(key, 21)
    return (jax.random.truncated_normal(own_key, -4.0, 4.0, (D, D)) * (1.5 * D ** (-0.5))).astype(jnp.bfloat16)


def draw_key_weight(key, part):
    own_key = jax.random.fold_in(key, 22)
    return (jax.random.truncated_normal(own_key, -4.0, 4.0, (D, D)) * (1.5 * D ** (-0.5))).astype(jnp.bfloat16)


def with_spikes(drawn, stream_key, source, target, blocks, factor):
    def block_of(dim):
        return (jnp.arange(drawn.shape[dim]) // (drawn.shape[dim] // blocks)).reshape((-1,) + (1,) * (drawn.ndim - 1 - dim))

    first = jax.random.permutation(stream_key, blocks)[block_of(target)]
    second = (block_of(target) + blocks // 2) % blocks
    return jnp.where((block_of(source) == first) | (block_of(source) == second), factor * drawn, drawn)


def shard_levels(key, dims, pieces, smallest, high):
    loudness, own = 1.0, jax.random.fold_in(key, 6)
    for dim, blocks in pieces:
        heights = jnp.exp(jax.random.uniform(jax.random.fold_in(own, dim), (blocks,), jnp.float32, smallest / len(pieces), high / len(pieces)))
        loudness = loudness * jnp.repeat(heights, dims[dim] // blocks).reshape([-1 if axis == dim else 1 for axis in range(len(dims))])
    return loudness


def bell_draw(rng, shape, scale, most, shards=(), kind=jnp.bfloat16):
    array = jax.random.normal(rng, shape, jnp.float32) * scale
    if len(shards) > 0:
        array = shard_levels(rng, shape, shards, -0.22, 0.18) * array
    return jnp.clip(array, min=-most, max=most).astype(kind)


def gaussian_with(key, shape, width, bound, pieces, heavy, kind=jnp.bfloat16):
    result = width * jax.random.normal(key, shape, jnp.float32)
    if pieces:
        result = result * shard_levels(key, shape, pieces, -0.22, 0.18)
    return jnp.clip(with_spikes(result, jax.random.fold_in(key, 3), *heavy), -bound, bound).astype(kind)


def setup_inputs(seed: int = 0, part: int = 0) -> dict:
    keys = jax.random.split(jax.random.key(seed), 9)
    part_splits = jax.random.split(jax.random.fold_in(keys[8], part), 9)
    tokens = draw_tokens(jax.random.fold_in(jax.random.fold_in(keys[8], part), 71), part)
    norm_gain = jnp.clip(1.0 + 0.18 * jax.random.normal(keys[1], (D,), jnp.float32), 0.099609375, 1.8984375).astype(jnp.bfloat16)
    reduce_gain = jnp.clip(1.0 + 0.18 * jax.random.normal(keys[2], (D,), jnp.float32), 0.099609375, 1.8984375).astype(jnp.bfloat16)
    query_weight = draw_query_weight(jax.random.fold_in(keys[8], 71), part)
    key_weight = draw_key_weight(jax.random.fold_in(keys[8], 71), part)
    value_weight = bell_draw(keys[5], (D, D), D ** -0.5, 0.1875, ((0, 4), (1, 4)))
    out_weight = bell_draw(keys[6], (D, D), D ** -0.5, 0.1875, ((0, 4), (1, 4)))
    out_cotangent = gaussian_with(part_splits[7], (TOKENS, D), 1.0, 6.0, ((0, 4),), (0, 1, 4, 2.0))
    return dict(tokens=tokens, norm_gain=norm_gain, reduce_gain=reduce_gain, query_weight=query_weight, key_weight=key_weight, value_weight=value_weight, out_weight=out_weight, out_cotangent=out_cotangent)


EPS = 1e-06

def norm_rows(values, row_gain):
    row_mean = lax.optimization_barrier(jnp.mean(values, axis=-1, keepdims=True))
    centred = values - row_mean
    inverse = lax.rsqrt(lax.optimization_barrier(jnp.mean(centred * centred, axis=-1, keepdims=True)) + EPS)
    unit_rows = centred * inverse
    return (unit_rows * row_gain, unit_rows, inverse)

def norm_back(gradient, unit_rows, inverse, row_gain):
    scaled = gradient * row_gain
    first_mean = lax.optimization_barrier(jnp.mean(scaled, axis=-1, keepdims=True))
    second_mean = lax.optimization_barrier(jnp.mean(scaled * unit_rows, axis=-1, keepdims=True))
    return inverse * (scaled - first_mean - unit_rows * second_mean)

def round_trip(values):
    lowered = lax.optimization_barrier(values.astype(jnp.bfloat16))
    return lowered.astype(jnp.float32)

def head_pass(query_h, keys_h, values_h, dattn_h):
    factor = HEAD_DIM ** (-0.5)
    scores = jnp.dot(query_h, keys_h.T, preferred_element_type=jnp.float32) * factor
    row_max = lax.optimization_barrier(jnp.max(scores, axis=-1, keepdims=True))
    shifted = jnp.exp(scores - row_max)
    chances = shifted / lax.optimization_barrier(jnp.sum(shifted, axis=-1, keepdims=True))
    reduced_probabilities = chances.astype(jnp.bfloat16)
    attn_h = jnp.dot(reduced_probabilities, values_h, preferred_element_type=jnp.float32).astype(jnp.bfloat16)
    d_chances = jnp.dot(dattn_h, values_h.T, preferred_element_type=jnp.float32)
    row_delta = lax.optimization_barrier(jnp.sum(chances * d_chances, axis=-1, keepdims=True))
    score_gradient = (chances * (d_chances - row_delta) * factor).astype(jnp.bfloat16)
    dquery_h = jnp.dot(score_gradient, keys_h, preferred_element_type=jnp.float32).astype(jnp.bfloat16)
    dkeys_h = jnp.dot(score_gradient.T, query_h, preferred_element_type=jnp.float32)
    dvalues_h = jnp.dot(reduced_probabilities.T, dattn_h, preferred_element_type=jnp.float32)
    return (attn_h, dquery_h, dkeys_h, dvalues_h)

def split_heads(matrix):
    return matrix.reshape(matrix.shape[0], HEADS, HEAD_DIM).transpose(1, 0, 2)

def join_heads(stacked):
    return stacked.transpose(1, 0, 2).reshape(stacked.shape[1], HEADS * HEAD_DIM)

def group_sum(left_rows, right_rows):
    group_width = left_rows.shape[1] // N_HD
    running = jnp.zeros((left_rows.shape[0], right_rows.shape[0]), jnp.float32)
    for member in range(N_HD):
        low_edge = member * group_width
        piece_sum = jnp.dot(left_rows[:, low_edge:low_edge + group_width], right_rows[:, low_edge:low_edge + group_width].T, preferred_element_type=jnp.float32)
        running = running + round_trip(piece_sum)
    return running

def reference(tokens, norm_gain, reduce_gain, query_weight, key_weight, value_weight, out_weight, out_cotangent):
    first_gain = norm_gain.astype(jnp.float32)
    second_gain = reduce_gain.astype(jnp.float32)
    normed_wide, unit_rows, inverse = norm_rows(tokens.astype(jnp.float32), first_gain)
    normed = normed_wide.astype(jnp.bfloat16)
    blocks = normed.reshape(ROWS // POOL, POOL, GRID_W // POOL, POOL, D)
    pooled = (lax.optimization_barrier(jnp.sum(blocks, axis=(1, 3), dtype=jnp.float32)) / (POOL * POOL)).reshape(REDUCED, D)
    reduced_wide, reduced_unit, reduced_inverse = norm_rows(pooled, second_gain)
    reduced = reduced_wide.astype(jnp.bfloat16)
    queries = jnp.dot(normed, query_weight, preferred_element_type=jnp.float32).astype(jnp.bfloat16)
    key_rows = jnp.dot(reduced, key_weight, preferred_element_type=jnp.float32).astype(jnp.bfloat16)
    value_rows = jnp.dot(reduced, value_weight, preferred_element_type=jnp.float32).astype(jnp.bfloat16)
    d_attention = jnp.dot(out_cotangent, out_weight, preferred_element_type=jnp.float32).astype(jnp.bfloat16)
    attn_stack, dquery_stack, dkeys_stack, dvalues_stack = lax.map(lambda head_parts: head_pass(head_parts[0], head_parts[1], head_parts[2], head_parts[3]), (split_heads(queries), split_heads(key_rows), split_heads(value_rows), split_heads(d_attention)))
    attention = join_heads(attn_stack)
    query_gradient = join_heads(dquery_stack)
    d_keys = join_heads(dkeys_stack).astype(jnp.bfloat16)
    d_values = join_heads(dvalues_stack).astype(jnp.bfloat16)
    branch = group_sum(attention, out_weight).astype(jnp.bfloat16)
    d_reduced = jnp.dot(d_keys, key_weight.T, preferred_element_type=jnp.float32) + jnp.dot(d_values, value_weight.T, preferred_element_type=jnp.float32)
    d_pooled = norm_back(d_reduced, reduced_unit, reduced_inverse, second_gain)
    grid_view = d_pooled.reshape(ROWS // POOL, 1, GRID_W // POOL, 1, D)
    spread_rows = jnp.broadcast_to(grid_view, (ROWS // POOL, POOL, GRID_W // POOL, POOL, D)).reshape(TOKENS, D)
    d_normed = group_sum(query_gradient, query_weight) + spread_rows / (POOL * POOL)
    input_grad = norm_back(d_normed, unit_rows, inverse, first_gain).astype(jnp.bfloat16)
    grad_factor = TOKENS ** (-0.5)
    query_grad = jnp.dot(normed.T, query_gradient, preferred_element_type=jnp.float32) * grad_factor
    key_grad = jnp.dot(reduced.T, d_keys, preferred_element_type=jnp.float32) * grad_factor
    value_grad = jnp.dot(reduced.T, d_values, preferred_element_type=jnp.float32) * grad_factor
    out_grad = jnp.dot(out_cotangent.T, attention, preferred_element_type=jnp.float32) * grad_factor
    return (branch, input_grad, query_grad, key_grad, value_grad, out_grad)
```

```python
import functools
import jax
import jax.numpy as jnp
from jax import lax
from jax.experimental import pallas as pl
from jax.experimental.pallas import tpu as pltpu
from jax.sharding import PartitionSpec as P

HEAD_DIM = 64
POOL = 8
GRID_W = 128
EPS = 1e-06
BF = jnp.bfloat16
F32 = jnp.float32
VMEM_LIMIT = 40 * 1024 * 1024

NN = (((1,), (0,)), ((), ()))
NT = (((1,), (1,)), ((), ()))


def mm(left, right, dims=NN):
    return lax.dot_general(left, right, dims, preferred_element_type=F32)


def params(axes=1):
    return pltpu.CompilerParams(
        dimension_semantics=("arbitrary",) * axes, vmem_limit_bytes=VMEM_LIMIT
    )


def norm_kernel(gain_ref, rgain_ref, tok_ref, normed_ref, red_ref, runit_ref, rinv_ref, pooled):
    row, col = pl.program_id(0), pl.program_id(1)
    cols = tok_ref.shape[1]
    width = tok_ref.shape[2]
    gain = gain_ref[...]
    chunk = 2 * POOL
    sums = []
    for part in range(cols // chunk):
        acc = jnp.zeros((chunk, width), F32)
        for r in range(POOL):
            v = tok_ref[r, part * chunk : (part + 1) * chunk, :].astype(F32)
            d = v - jnp.mean(v, axis=-1, keepdims=True)
            inv = lax.rsqrt(jnp.mean(d * d, axis=-1, keepdims=True) + EPS)
            n = (d * inv * gain).astype(BF)
            normed_ref[r, part * chunk : (part + 1) * chunk, :] = n
            acc = acc + n.astype(F32)
        sums.append(jnp.sum(acc.reshape(2, POOL, width), axis=1))
    span = cols // POOL
    base = pl.multiple_of((row * pl.num_programs(1) + col) * span, span)
    pooled[pl.ds(base, span), :] = jnp.concatenate(sums, axis=0)

    @pl.when((row == pl.num_programs(0) - 1) & (col == pl.num_programs(1) - 1))
    def _():
        v = pooled[...] / (POOL * POOL)
        d = v - jnp.mean(v, axis=-1, keepdims=True)
        inv = lax.rsqrt(jnp.mean(d * d, axis=-1, keepdims=True) + EPS)
        unit = d * inv
        runit_ref[...] = unit
        rinv_ref[...] = jnp.broadcast_to(inv, rinv_ref.shape)
        red_ref[...] = (unit * rgain_ref[...]).astype(BF)


def norm_and_pool(tokens, norm_gain, reduce_gain):
    count, width = tokens.shape
    grid_rows = count // GRID_W
    blocks = count // (POOL * POOL)
    cols = 64
    spec = pl.BlockSpec((POOL, cols, width), lambda i, j: (i, j, 0))
    whole = lambda shape: pl.BlockSpec(shape, lambda i, j: (0,) * len(shape))
    normed, reduced, unit, inverse = pl.pallas_call(
        norm_kernel,
        grid=(grid_rows // POOL, GRID_W // cols),
        in_specs=[whole((1, width)), whole((1, width)), spec],
        out_specs=[spec, whole((blocks, width)), whole((blocks, width)), whole((blocks, 128))],
        out_shape=[
            jax.ShapeDtypeStruct((grid_rows, GRID_W, width), BF),
            jax.ShapeDtypeStruct((blocks, width), BF),
            jax.ShapeDtypeStruct((blocks, width), F32),
            jax.ShapeDtypeStruct((blocks, 128), F32),
        ],
        scratch_shapes=[pltpu.VMEM((blocks, width), F32)],
        compiler_params=params(2),
        name="norm_pool",
    )(
        norm_gain.astype(F32).reshape(1, width),
        reduce_gain.astype(F32).reshape(1, width),
        tokens.reshape(grid_rows, GRID_W, width),
    )
    return normed.reshape(count, width), reduced, unit, inverse


def head_mask(shape, head):
    lane = lax.broadcasted_iota(jnp.int32, shape, 1)
    return (lane >= head * HEAD_DIM) & (lane < (head + 1) * HEAD_DIM)


def attend_kernel(
    grads, n_sp, grad_factor, pos_ref, x_ref, y_ref, w_ref, kv_ref, attn_ref, dq_ref, *rest
):
    if grads:
        grad_ref, dkv_ref, kbd, vbd, kbd_t, vbd_t, dk_acc, dv_acc, g_acc = rest
    else:
        kbd, vbd, kbd_t, vbd_t = rest
    step = pl.program_id(0)
    feats = w_ref.shape[2]
    depth = w_ref.shape[3]
    blocks = kv_ref.shape[0]
    heads = feats // HEAD_DIM
    z = pos_ref[0]
    factor = HEAD_DIM ** (-0.5)

    @pl.when(step == 0)
    def _():
        k = kv_ref[:, :feats]
        v = kv_ref[:, feats:]
        for head in range(heads):
            mask = head_mask((blocks, feats), head)
            rows = slice(head * blocks, (head + 1) * blocks)
            kbd[rows, :] = jnp.where(mask, k.astype(F32) * factor, 0.0).astype(BF)
            vbd[rows, :] = jnp.where(mask, v.astype(F32), 0.0).astype(BF)
        kbd_t[...] = kbd[...].T
        vbd_t[...] = vbd[...].T
        if grads:
            dk_acc[...] = jnp.zeros_like(dk_acc)
            dv_acc[...] = jnp.zeros_like(dv_acc)
            g_acc[...] = jnp.zeros_like(g_acc)

    q_sum, da_sum = None, None
    for place in range(n_sp):
        piece = lax.rem(z - place + n_sp, n_sp)
        cols = slice(place * depth, (place + 1) * depth)
        q_term = mm(w_ref[piece, 0], x_ref[:, cols], NT)
        da_term = mm(w_ref[piece, 1], y_ref[:, cols], NT)
        q_sum = q_term if q_sum is None else q_sum + q_term
        da_sum = da_term if da_sum is None else da_sum + da_term
    q_t = q_sum.astype(BF)
    da_t = da_sum.astype(BF)

    scores = mm(kbd[...], q_t)
    d_chances = mm(vbd[...], da_t)
    low, d_low = [], []
    for head in range(heads):
        rows = slice(head * blocks, (head + 1) * blocks)
        s = scores[rows]
        e = jnp.exp(s - jnp.max(s, axis=0, keepdims=True))
        p = e * (1.0 / jnp.sum(e, axis=0, keepdims=True))
        dp = d_chances[rows]
        delta = jnp.sum(p * dp, axis=0, keepdims=True)
        low.append(p.astype(BF))
        d_low.append((p * (dp - delta)).astype(BF))
    low = jnp.concatenate(low, axis=0)
    d_low = jnp.concatenate(d_low, axis=0)
    attn_t = mm(vbd_t[...], low).astype(BF)
    dq_t = mm(kbd_t[...], d_low).astype(BF)
    attn_ref[...] = attn_t
    dq_ref[...] = dq_t
    if grads:
        dk_acc[...] += mm(d_low, q_t, NT)
        dv_acc[...] += mm(low, da_t, NT)
        for place in range(n_sp):
            cols = slice(place * depth, (place + 1) * depth)
            g_acc[place, 0] += mm(dq_t, x_ref[:, cols])
            g_acc[place, 1] += mm(attn_t, y_ref[:, cols])

        @pl.when(step == pl.num_programs(0) - 1)
        def _():
            dk = jnp.zeros((blocks, feats), F32)
            dv = jnp.zeros((blocks, feats), F32)
            for head in range(heads):
                mask = head_mask((blocks, feats), head)
                rows = slice(head * blocks, (head + 1) * blocks)
                dk = dk + jnp.where(mask, dk_acc[rows, :], 0.0)
                dv = dv + jnp.where(mask, dv_acc[rows, :], 0.0)
            dkv_ref[:, :feats] = (dk * factor).astype(dkv_ref.dtype)
            dkv_ref[:, feats:] = dv.astype(dkv_ref.dtype)
            grad_ref[...] = (g_acc[...] * grad_factor).astype(grad_ref.dtype)


def attend(pos, normed, cotangent, weights, kv, grads=None, grad_factor=1.0):
    n_sp, _, feats, depth = weights.shape
    width = normed.shape[1]
    own = normed.shape[0] // 2
    blocks = kv.shape[0]
    heads = feats // HEAD_DIM
    tile = 256
    steps = own // tile
    rows = pl.BlockSpec((tile, width), lambda i, p: (p[1] * steps + i, 0))
    whole = lambda shape: pl.BlockSpec(shape, lambda i, p: (0,) * len(shape))
    t_spec = pl.BlockSpec((feats, tile), lambda i, p: (0, i))
    out_specs = [t_spec, t_spec]
    out_shape = [jax.ShapeDtypeStruct((feats, own), BF)] * 2
    scratch = [
        pltpu.VMEM((heads * blocks, feats), BF),
        pltpu.VMEM((heads * blocks, feats), BF),
        pltpu.VMEM((feats, heads * blocks), BF),
        pltpu.VMEM((feats, heads * blocks), BF),
    ]
    flops = 2 * 2 * own * width * feats + 4 * 2 * own * heads * blocks * feats
    if grads is not None:
        out_specs += [whole(weights.shape), whole((blocks, 2 * feats))]
        out_shape += [
            jax.ShapeDtypeStruct(weights.shape, grads),
            jax.ShapeDtypeStruct((blocks, 2 * feats), grads),
        ]
        scratch += [
            pltpu.VMEM((heads * blocks, feats), F32),
            pltpu.VMEM((heads * blocks, feats), F32),
            pltpu.VMEM(weights.shape, F32),
        ]
        flops += 2 * 2 * own * width * feats + 2 * 2 * own * heads * blocks * feats
    return pl.pallas_call(
        functools.partial(attend_kernel, grads is not None, n_sp, grad_factor),
        grid_spec=pltpu.PrefetchScalarGridSpec(
            num_scalar_prefetch=1,
            grid=(steps,),
            in_specs=[rows, rows, whole(weights.shape), whole(kv.shape)],
            out_specs=out_specs,
            scratch_shapes=scratch,
        ),
        out_shape=out_shape,
        compiler_params=params(),
        cost_estimate=pl.CostEstimate(
            flops=flops, bytes_accessed=4 * own * width + 8 * width * feats, transcendentals=0
        ),
        name="attend_grads" if grads is not None else "attend",
    )(pos, normed, cotangent, weights, kv)


def branch_kernel(count, n_sp, pos_ref, *refs):
    attn_refs, w_refs = refs[:count], refs[count : 2 * count]
    own_ref, sib_ref = refs[2 * count :]
    depth = w_refs[0].shape[3]
    z, h = pos_ref[0], pos_ref[2]
    sib = h + 1 - 2 * lax.rem(h, 2)
    pieces = own_ref.shape[1] // depth
    rows = [ref[...].T for ref in attn_refs]
    for ref, owner in ((own_ref, h), (sib_ref, sib)):
        for j in range(pieces):
            place = owner * pieces + j
            piece = lax.rem(z - place + n_sp, n_sp)
            total = None
            for row, w_ref in zip(rows, w_refs):
                term = mm(row, w_ref[piece, 0]).astype(BF).astype(F32)
                total = term if total is None else total + term
            ref[:, j * depth : (j + 1) * depth] = total.astype(BF)


def branch_rows(pos, attns, weights, n_hd):
    count = len(attns)
    n_sp, _, feats, depth = weights[0].shape
    own = attns[0].shape[1]
    width = n_sp * depth
    cols = width // n_hd
    tile = 256
    t_spec = pl.BlockSpec((feats, tile), lambda i, p: (0, i))
    w_spec = pl.BlockSpec((n_sp, 1, feats, depth), lambda i, p: (0, 1, 0, 0))
    o_spec = pl.BlockSpec((tile, cols), lambda i, p: (i, 0))
    return pl.pallas_call(
        functools.partial(branch_kernel, count, n_sp),
        grid_spec=pltpu.PrefetchScalarGridSpec(
            num_scalar_prefetch=1,
            grid=(own // tile,),
            in_specs=[t_spec] * count + [w_spec] * count,
            out_specs=[o_spec, o_spec],
        ),
        out_shape=[jax.ShapeDtypeStruct((own, cols), BF)] * 2,
        compiler_params=params(),
        cost_estimate=pl.CostEstimate(
            flops=4 * own * cols * count * feats, bytes_accessed=6 * own * width, transcendentals=0
        ),
        name="branch_rows",
    )(pos, *attns, *weights)


def input_kernel(count, n_sp, pos_ref, gain_ref, rgain_ref, tok_ref, dred_ref, runit_ref, rinv_ref, *refs):
    dq_refs, w_refs = refs[:count], refs[count : 2 * count]
    own_ref, sib_ref, spread, e_ref, u_ref = refs[2 * count :]
    step = pl.program_id(0)
    depth = w_refs[0].shape[3]
    width = tok_ref.shape[1]
    tile = tok_ref.shape[0]
    z, h = pos_ref[0], pos_ref[2]
    sib = h + 1 - 2 * lax.rem(h, 2)
    cols = own_ref.shape[1]

    @pl.when(step == 0)
    def _():
        groups = runit_ref.shape[0]
        parts = []
        for place in range(n_sp):
            parts.append(dred_ref[lax.rem(z - place + n_sp, n_sp)])
        e = jnp.concatenate(parts, axis=1) * rgain_ref[...]
        unit = runit_ref[...]
        first = jnp.mean(e, axis=-1, keepdims=True)
        second = jnp.mean(e * unit, axis=-1, keepdims=True)
        d_pooled = rinv_ref[:, 0:1] * (e - first - unit * second) / (POOL * POOL)
        spread[...] = jnp.broadcast_to(d_pooled[:, None, :], (groups, POOL, width)).reshape(
            groups * POOL, width
        )

    rows = [ref[...].T for ref in dq_refs]
    for place in range(n_sp):
        piece = lax.rem(z - place + n_sp, n_sp)
        lanes = slice(place * depth, (place + 1) * depth)
        total = None
        for row, w_ref in zip(rows, w_refs):
            term = mm(row, w_ref[piece, 0]).astype(BF).astype(F32)
            total = term if total is None else total + term
        e_ref[:, lanes] = total
    for part in range(tile // GRID_W):
        at = slice(part * GRID_W, (part + 1) * GRID_W)
        v = tok_ref[at, :].astype(F32)
        d = v - jnp.mean(v, axis=-1, keepdims=True)
        inv = lax.rsqrt(jnp.mean(d * d, axis=-1, keepdims=True) + EPS)
        unit = d * inv
        e = (e_ref[at, :] + spread[...]) * gain_ref[...]
        first = jnp.mean(e, axis=-1, keepdims=True)
        second = jnp.mean(e * unit, axis=-1, keepdims=True)
        u_ref[...] = inv * (e - first - unit * second)
        for ref, owner in ((own_ref, h), (sib_ref, sib)):
            ref[at, :] = u_ref[:, pl.ds(pl.multiple_of(owner * cols, 128), cols)].astype(BF)


def input_rows(pos, norm_gain, reduce_gain, tokens, d_reduced, unit, inverse, dqs, weights, n_hd):
    count = len(dqs)
    n_sp, _, feats, depth = weights[0].shape
    own = dqs[0].shape[1]
    width = n_sp * depth
    cols = width // n_hd
    groups = d_reduced.shape[1]
    tile = 256
    steps = own // tile
    whole = lambda shape: pl.BlockSpec(shape, lambda i, p: (0,) * len(shape))
    half = lambda shape: pl.BlockSpec(shape, lambda i, p: (p[1], 0))
    t_spec = pl.BlockSpec((feats, tile), lambda i, p: (0, i))
    w_spec = pl.BlockSpec((n_sp, 1, feats, depth), lambda i, p: (0, 0, 0, 0))
    o_spec = pl.BlockSpec((tile, cols), lambda i, p: (i, 0))
    return pl.pallas_call(
        functools.partial(input_kernel, count, n_sp),
        grid_spec=pltpu.PrefetchScalarGridSpec(
            num_scalar_prefetch=1,
            grid=(steps,),
            in_specs=[
                whole((1, width)),
                whole((1, width)),
                pl.BlockSpec((tile, width), lambda i, p: (p[1] * steps + i, 0)),
                whole(d_reduced.shape),
                half((groups, width)),
                half((groups, 128)),
            ]
            + [t_spec] * count
            + [w_spec] * count,
            out_specs=[o_spec, o_spec],
            scratch_shapes=[
                pltpu.VMEM((groups * POOL, width), F32),
                pltpu.VMEM((tile, width), F32),
                pltpu.VMEM((GRID_W, width), F32),
            ],
        ),
        out_shape=[jax.ShapeDtypeStruct((own, cols), BF)] * 2,
        compiler_params=params(),
        cost_estimate=pl.CostEstimate(
            flops=2 * own * width * count * feats, bytes_accessed=8 * own * width, transcendentals=0
        ),
        name="input_rows",
    )(
        pos,
        norm_gain.astype(F32).reshape(1, width),
        reduce_gain.astype(F32).reshape(1, width),
        tokens,
        d_reduced,
        unit,
        inverse,
        *dqs,
        *weights,
    )


def on_device(
    tokens,
    norm_gain,
    reduce_gain,
    query_weight,
    key_weight,
    value_weight,
    out_weight,
    out_cotangent,
):
    n_sp, n_hd = lax.axis_size("sp"), lax.axis_size("hd")
    n_x = n_hd // 2
    z, h = lax.axis_index("sp"), lax.axis_index("hd")
    c = h % 2
    depth, feats = query_weight.shape
    count = tokens.shape[0]
    own = count // 2
    grad_factor = float(count * n_sp) ** (-0.5)
    pos = jnp.stack([z, c, h]).astype(jnp.int32)

    def to_sp(value, k):
        return lax.ppermute(value, "sp", [(i, (i + k) % n_sp) for i in range(n_sp)])

    def swap(value):
        return lax.ppermute(value, "hd", [(i, i ^ 1) for i in range(n_hd)])

    def to_x(value, k):
        return lax.ppermute(value, "hd", [(i, (i + 2 * k) % n_hd) for i in range(n_hd)])

    def gather_sp(value):
        return [value] + [to_sp(value, k) for k in range(1, n_sp)]

    def pick(stack, index):
        return lax.dynamic_index_in_dim(stack, index % n_sp, 0, keepdims=False)

    shard = jnp.stack([query_weight.T, out_weight.T])
    w_own = jnp.stack(gather_sp(shard))

    normed, reduced, r_unit, r_inverse = norm_and_pool(tokens, norm_gain, reduce_gain)
    blocks = reduced.shape[0]

    red_cut = jnp.stack([reduced[:, i * depth : (i + 1) * depth] for i in range(n_sp)])
    reduced_cols = jnp.concatenate(
        [pick(red_cut, z)] + [to_sp(pick(red_cut, z + k), k) for k in range(1, n_sp)]
    )
    kv_weight = jnp.concatenate([key_weight, value_weight], axis=1)
    kv_part = mm(reduced_cols, kv_weight)

    def scatter_sp(parts, low):
        total = parts[:blocks]
        for k in range(1, n_sp):
            source = (n_sp - k) % n_sp
            total = total + to_sp(low[source * blocks : (source + 1) * blocks], k).astype(F32)
        return total

    kv_rows = scatter_sp(kv_part, kv_part.astype(BF)).astype(BF)
    kv_own = jnp.concatenate(gather_sp(kv_rows))

    kvs, ws = [kv_own, swap(kv_own)], [w_own, swap(w_own)]
    for k in range(1, n_x):
        kv_far, w_far = to_x(kv_own, k), to_x(w_own, k)
        kvs += [kv_far, swap(kv_far)]
        ws += [w_far, swap(w_far)]

    attn0, dq0, grad0, dkv0 = attend(
        pos, normed, out_cotangent, ws[0], kvs[0], F32, grad_factor
    )
    attn1, dq1, grad1, dkv1 = attend(pos, normed, out_cotangent, ws[1], kvs[1], BF, grad_factor)
    attns, dqs = [attn0, attn1], [dq0, dq1]

    dkv = dkv0 + swap(dkv1).astype(F32)
    dkv_rows = scatter_sp(dkv, dkv.astype(BF)).astype(BF)
    dkv_own = jnp.concatenate(gather_sp(dkv_rows))
    d_keys, d_values = dkv_own[:, :feats], dkv_own[:, feats:]
    red_t = reduced_cols.T
    key_grad = mm(red_t, d_keys) * grad_factor
    value_grad = mm(red_t, d_values) * grad_factor
    d_red = mm(d_keys, key_weight, NT) + mm(d_values, value_weight, NT)
    d_red = d_red.astype(BF).reshape(n_sp, 2, blocks // 2, depth)
    mine = lax.dynamic_index_in_dim(d_red, c, 1, keepdims=False).astype(F32)
    other = lax.dynamic_index_in_dim(d_red, 1 - c, 1, keepdims=False)
    d_red = mine + swap(other).astype(F32)
    low = d_red.astype(BF)
    for k in range(1, n_x):
        d_red = d_red + to_x(low, k).astype(F32)
    low = d_red.astype(BF)
    d_red = jnp.stack(
        [d_red[0]] + [to_sp(low[(n_sp - k) % n_sp], k).astype(F32) for k in range(1, n_sp)]
    )

    grad = grad0 + swap(grad1).astype(F32)
    low = grad.astype(BF)
    total = pick(grad, z)
    for k in range(1, n_sp):
        total = total + to_sp(pick(low, z + k), k).astype(F32)
    query_grad, out_grad = total[0].T, total[1].T

    for w, kv in zip(ws[2:], kvs[2:]):
        attn, dq = attend(pos, normed, out_cotangent, w, kv)
        attns.append(attn)
        dqs.append(dq)

    mine, other = branch_rows(pos, attns, ws, n_hd)

    def place(mine, other):
        both = jnp.concatenate([mine, other, mine])
        return lax.dynamic_slice_in_dim(both, c * own, 2 * own, 0)

    branch = place(mine, swap(other))
    mine, other = input_rows(
        pos, norm_gain, reduce_gain, tokens, d_red, r_unit, r_inverse, dqs, ws, n_hd
    )
    input_grad = place(mine, swap(other))
    return (branch, input_grad, query_grad, key_grad, value_grad, out_grad)


def solution(mesh):
    rows, whole, both = P(("scene", "sp"), None), P(), P("sp", "hd")
    out = P(("scene", "sp"), "hd")
    return jax.shard_map(
        on_device,
        mesh=mesh,
        in_specs=(rows, whole, whole, both, both, both, both, rows),
        out_specs=(out,) * 6,
        check_vma=False,
    )
```

```python
import functools
import jax
import jax.numpy as jnp
from jax import lax
from jax.experimental import pallas as pl
from jax.experimental.pallas import tpu as pltpu
from jax.sharding import PartitionSpec as P

HEAD_DIM = 64
POOL = 8
GRID_W = 128
EPS = 1e-06
BF = jnp.bfloat16
F32 = jnp.float32
VMEM_LIMIT = 58 * 1024 * 1024

NN = (((1,), (0,)), ((), ()))
TN = (((0,), (0,)), ((), ()))
NT = (((1,), (1,)), ((), ()))


def mm(left, right, dims=NN):
    return lax.dot_general(left, right, dims, preferred_element_type=F32)


def params(axes=1):
    return pltpu.CompilerParams(
        dimension_semantics=("arbitrary",) * axes, vmem_limit_bytes=VMEM_LIMIT
    )


def norm_kernel(gain_ref, rgain_ref, tok_ref, normed_ref, red_ref, runit_ref, rinv_ref, pooled):
    row, col = pl.program_id(0), pl.program_id(1)
    cols = tok_ref.shape[1]
    width = tok_ref.shape[2]
    gain = gain_ref[...]
    chunk = 2 * POOL
    sums = []
    for part in range(cols // chunk):
        acc = jnp.zeros((chunk, width), F32)
        for r in range(POOL):
            v = tok_ref[r, part * chunk : (part + 1) * chunk, :].astype(F32)
            d = v - jnp.mean(v, axis=-1, keepdims=True)
            inv = lax.rsqrt(jnp.mean(d * d, axis=-1, keepdims=True) + EPS)
            n = (d * inv * gain).astype(BF)
            normed_ref[r, part * chunk : (part + 1) * chunk, :] = n
            acc = acc + n.astype(F32)
        sums.append(jnp.sum(acc.reshape(2, POOL, width), axis=1))
    span = cols // POOL
    base = pl.multiple_of((row * pl.num_programs(1) + col) * span, span)
    pooled[pl.ds(base, span), :] = jnp.concatenate(sums, axis=0)

    @pl.when((row == pl.num_programs(0) - 1) & (col == pl.num_programs(1) - 1))
    def _():
        v = pooled[...] / (POOL * POOL)
        d = v - jnp.mean(v, axis=-1, keepdims=True)
        inv = lax.rsqrt(jnp.mean(d * d, axis=-1, keepdims=True) + EPS)
        unit = d * inv
        runit_ref[...] = unit
        rinv_ref[...] = jnp.broadcast_to(inv, rinv_ref.shape)
        red_ref[...] = (unit * rgain_ref[...]).astype(BF)


def norm_and_pool(tokens, norm_gain, reduce_gain):
    count, width = tokens.shape
    grid_rows = count // GRID_W
    blocks = count // (POOL * POOL)
    cols = 64
    spec = pl.BlockSpec((POOL, cols, width), lambda i, j: (i, j, 0))
    whole = lambda shape: pl.BlockSpec(shape, lambda i, j: (0,) * len(shape))
    normed, reduced, unit, inverse = pl.pallas_call(
        norm_kernel,
        grid=(grid_rows // POOL, GRID_W // cols),
        in_specs=[whole((1, width)), whole((1, width)), spec],
        out_specs=[spec, whole((blocks, width)), whole((blocks, width)), whole((blocks, 128))],
        out_shape=[
            jax.ShapeDtypeStruct((grid_rows, GRID_W, width), BF),
            jax.ShapeDtypeStruct((blocks, width), BF),
            jax.ShapeDtypeStruct((blocks, width), F32),
            jax.ShapeDtypeStruct((blocks, 128), F32),
        ],
        scratch_shapes=[pltpu.VMEM((blocks, width), F32)],
        compiler_params=params(2),
        name="norm_pool",
    )(
        norm_gain.astype(F32).reshape(1, width),
        reduce_gain.astype(F32).reshape(1, width),
        tokens.reshape(grid_rows, GRID_W, width),
    )
    return normed.reshape(count, width), reduced, unit, inverse


def head_mask(shape, head):
    lane = lax.broadcasted_iota(jnp.int32, shape, 1)
    return (lane >= head * HEAD_DIM) & (lane < (head + 1) * HEAD_DIM)


def spread_heads(kv_ref, kbd, vbd, kbd_t, vbd_t):
    blocks, feats = kv_ref.shape[0], kv_ref.shape[1] // 2
    k = kv_ref[:, :feats].astype(F32) * HEAD_DIM ** (-0.5)
    v = kv_ref[:, feats:].astype(F32)
    for head in range(feats // HEAD_DIM):
        mask = head_mask((blocks, feats), head)
        rows = slice(head * blocks, (head + 1) * blocks)
        kbd[rows, :] = jnp.where(mask, k, 0.0).astype(BF)
        vbd[rows, :] = jnp.where(mask, v, 0.0).astype(BF)
    kbd_t[...] = kbd[...].T
    vbd_t[...] = vbd[...].T


def attend_tile(n_sp, z, x_ref, y_ref, w_ref, kbd, vbd, kbd_t, vbd_t):
    feats, depth = w_ref.shape[2], w_ref.shape[3]
    heads = feats // HEAD_DIM
    blocks = kbd.shape[0] // heads
    q_sum, da_sum = None, None
    for place in range(n_sp):
        piece = lax.rem(z - place + n_sp, n_sp)
        cols = slice(place * depth, (place + 1) * depth)
        q_term = mm(w_ref[piece, 0], x_ref[:, cols], NT)
        da_term = mm(w_ref[piece, 1], y_ref[:, cols], NT)
        q_sum = q_term if q_sum is None else q_sum + q_term
        da_sum = da_term if da_sum is None else da_sum + da_term
    q_t = q_sum.astype(BF)
    da_t = da_sum.astype(BF)
    scores = mm(kbd[...], q_t)
    d_chances = mm(vbd[...], da_t)
    low, d_low = [], []
    for head in range(heads):
        rows = slice(head * blocks, (head + 1) * blocks)
        s = scores[rows]
        e = jnp.exp(s - jnp.max(s, axis=0, keepdims=True))
        p = e * (1.0 / jnp.sum(e, axis=0, keepdims=True))
        dp = d_chances[rows]
        delta = jnp.sum(p * dp, axis=0, keepdims=True)
        low.append(p.astype(BF))
        d_low.append((p * (dp - delta)).astype(BF))
    low = jnp.concatenate(low, axis=0)
    d_low = jnp.concatenate(d_low, axis=0)
    attn_t = mm(vbd_t[...], low).astype(BF)
    dq_t = mm(kbd_t[...], d_low).astype(BF)
    return q_t, da_t, low, d_low, attn_t, dq_t


def head_scratch(heads, blocks, feats):
    return [
        pltpu.VMEM((heads * blocks, feats), BF),
        pltpu.VMEM((heads * blocks, feats), BF),
        pltpu.VMEM((feats, heads * blocks), BF),
        pltpu.VMEM((feats, heads * blocks), BF),
    ]


def attend_kernel(n_sp, grad_factor, pos_ref, x_ref, y_ref, w_ref, kv_ref, attn_ref, dq_ref,
                  grad_ref, dkv_ref, kbd, vbd, kbd_t, vbd_t, dk_acc, dv_acc, g_acc):
    step = pl.program_id(0)
    feats, depth = w_ref.shape[2], w_ref.shape[3]
    blocks = kv_ref.shape[0]
    z = pos_ref[0]

    @pl.when(step == 0)
    def _():
        spread_heads(kv_ref, kbd, vbd, kbd_t, vbd_t)
        dk_acc[...] = jnp.zeros_like(dk_acc)
        dv_acc[...] = jnp.zeros_like(dv_acc)
        g_acc[...] = jnp.zeros_like(g_acc)

    q_t, da_t, low, d_low, attn_t, dq_t = attend_tile(
        n_sp, z, x_ref, y_ref, w_ref, kbd, vbd, kbd_t, vbd_t
    )
    attn_ref[...] = attn_t
    dq_ref[...] = dq_t
    dk_acc[...] += mm(d_low, q_t, NT)
    dv_acc[...] += mm(low, da_t, NT)
    for place in range(n_sp):
        cols = slice(place * depth, (place + 1) * depth)
        g_acc[place, 0] += mm(dq_t, x_ref[:, cols])
        g_acc[place, 1] += mm(attn_t, y_ref[:, cols])

    @pl.when(step == pl.num_programs(0) - 1)
    def _():
        dk = jnp.zeros((blocks, feats), F32)
        dv = jnp.zeros((blocks, feats), F32)
        for head in range(feats // HEAD_DIM):
            mask = head_mask((blocks, feats), head)
            rows = slice(head * blocks, (head + 1) * blocks)
            dk = dk + jnp.where(mask, dk_acc[rows, :], 0.0)
            dv = dv + jnp.where(mask, dv_acc[rows, :], 0.0)
        dkv_ref[:, :feats] = (dk * HEAD_DIM ** (-0.5)).astype(dkv_ref.dtype)
        dkv_ref[:, feats:] = dv.astype(dkv_ref.dtype)
        grad_ref[...] = (g_acc[...] * grad_factor).astype(grad_ref.dtype)


def fixed(shape):
    return pl.BlockSpec(shape, lambda i, p: (0,) * len(shape))


def attend(pos, normed, cotangent, weights, kv, grad_factor, dkv_type):
    n_sp, _, feats, depth = weights.shape
    width = normed.shape[1]
    own = normed.shape[0] // 2
    blocks = kv.shape[0]
    heads = feats // HEAD_DIM
    tile = 256
    steps = own // tile
    rows = pl.BlockSpec((tile, width), lambda i, p: (p[1] * steps + i, 0))
    t_spec = pl.BlockSpec((feats, tile), lambda i, p: (0, i))
    return pl.pallas_call(
        functools.partial(attend_kernel, n_sp, grad_factor),
        grid_spec=pltpu.PrefetchScalarGridSpec(
            num_scalar_prefetch=1,
            grid=(steps,),
            in_specs=[rows, rows, fixed(weights.shape), fixed(kv.shape)],
            out_specs=[t_spec, t_spec, fixed(weights.shape), fixed((blocks, 2 * feats))],
            scratch_shapes=head_scratch(heads, blocks, feats)
            + [
                pltpu.VMEM((heads * blocks, feats), F32),
                pltpu.VMEM((heads * blocks, feats), F32),
                pltpu.VMEM(weights.shape, F32),
            ],
        ),
        out_shape=[jax.ShapeDtypeStruct((feats, own), BF)] * 2
        + [
            jax.ShapeDtypeStruct(weights.shape, BF),
            jax.ShapeDtypeStruct((blocks, 2 * feats), dkv_type),
        ],
        compiler_params=params(),
        cost_estimate=pl.CostEstimate(
            flops=8 * own * width * feats + 12 * own * heads * blocks * feats,
            bytes_accessed=4 * own * width + 8 * width * feats,
            transcendentals=0,
        ),
        name="attend_grads",
    )(pos, normed, cotangent, weights, kv)


def far_kernel(near, far, n_sp, pos_ref, x_ref, y_ref, *refs):
    total = near + far
    attn_refs, refs = refs[:near], refs[near:]
    dq_refs, refs = refs[:near], refs[near:]
    w_refs, refs = refs[:total], refs[total:]
    kv_refs, refs = refs[:far], refs[far:]
    own_ref, sib_ref, heads_ref = refs[:3]
    scratch = refs[3:]
    depth = w_refs[0].shape[3]
    z, h = pos_ref[0], pos_ref[2]
    sib = h + 1 - 2 * lax.rem(h, 2)
    pieces = own_ref.shape[1] // depth

    @pl.when(pl.program_id(0) == 0)
    def _():
        for g in range(far):
            spread_heads(kv_refs[g], *scratch[4 * g : 4 * g + 4])

    attn_rows = [ref[...].T for ref in attn_refs]
    dq_rows = [ref[...].T for ref in dq_refs]
    for g in range(far):
        out = attend_tile(n_sp, z, x_ref, y_ref, w_refs[near + g], *scratch[4 * g : 4 * g + 4])
        attn_rows.append(out[4].T)
        dq_rows.append(out[5].T)

    def grouped(rows, piece, which):
        total = None
        for row, w_ref in zip(rows, w_refs):
            term = mm(row, w_ref[piece, which]).astype(BF).astype(F32)
            total = term if total is None else total + term
        return total

    for ref, owner in ((own_ref, h), (sib_ref, sib)):
        for j in range(pieces):
            piece = lax.rem(z - (owner * pieces + j) + n_sp, n_sp)
            ref[:, j * depth : (j + 1) * depth] = grouped(attn_rows, piece, 1).astype(BF)
    for place in range(n_sp):
        piece = lax.rem(z - place + n_sp, n_sp)
        heads_ref[:, place * depth : (place + 1) * depth] = grouped(dq_rows, piece, 0)


def far_heads(pos, normed, cotangent, attns, dqs, weights, kvs, n_hd):
    near, far = len(attns), len(kvs)
    n_sp, _, feats, depth = weights[0].shape
    width = normed.shape[1]
    own = normed.shape[0] // 2
    cols = width // n_hd
    blocks = kvs[0].shape[0]
    heads = feats // HEAD_DIM
    tile = 256
    steps = own // tile
    rows = pl.BlockSpec((tile, width), lambda i, p: (p[1] * steps + i, 0))
    t_spec = pl.BlockSpec((feats, tile), lambda i, p: (0, i))
    return pl.pallas_call(
        functools.partial(far_kernel, near, far, n_sp),
        grid_spec=pltpu.PrefetchScalarGridSpec(
            num_scalar_prefetch=1,
            grid=(steps,),
            in_specs=[rows, rows]
            + [t_spec] * (2 * near)
            + [fixed(w.shape) for w in weights]
            + [fixed(kv.shape) for kv in kvs],
            out_specs=[
                pl.BlockSpec((tile, cols), lambda i, p: (p[1] * steps + i, 0)),
                pl.BlockSpec((tile, cols), lambda i, p: (i, 0)),
                pl.BlockSpec((tile, width), lambda i, p: (i, 0)),
            ],
            scratch_shapes=head_scratch(heads, blocks, feats) * far,
        ),
        out_shape=[
            jax.ShapeDtypeStruct((2 * own, cols), BF),
            jax.ShapeDtypeStruct((own, cols), BF),
            jax.ShapeDtypeStruct((own, width), F32),
        ],
        compiler_params=params(),
        cost_estimate=pl.CostEstimate(
            flops=far * (4 * own * width * feats + 8 * own * heads * blocks * feats)
            + 2 * own * width * (width + 2 * cols),
            bytes_accessed=20 * own * width,
            transcendentals=0,
        ),
        name="far_heads",
    )(pos, normed, cotangent, *attns, *dqs, *weights, *kvs)


def input_kernel(pos_ref, gain_ref, rgain_ref, tok_ref, dred_ref, runit_ref, rinv_ref, heads_ref,
                 own_ref, sib_ref, spread, u_ref):
    width = tok_ref.shape[1]
    h = pos_ref[2]
    sib = h + 1 - 2 * lax.rem(h, 2)
    cols = own_ref.shape[1]

    @pl.when(pl.program_id(0) == 0)
    def _():
        groups = runit_ref.shape[0]
        e = dred_ref[...] * rgain_ref[...]
        unit = runit_ref[...]
        first = jnp.mean(e, axis=-1, keepdims=True)
        second = jnp.mean(e * unit, axis=-1, keepdims=True)
        d_pooled = rinv_ref[:, 0:1] * (e - first - unit * second) / (POOL * POOL)
        spread[...] = jnp.broadcast_to(d_pooled[:, None, :], (groups, POOL, width)).reshape(
            groups * POOL, width
        )

    chunk = 2 * POOL
    for part in range(tok_ref.shape[0] // chunk):
        at = slice(part * chunk, (part + 1) * chunk)
        low = (part * chunk) % GRID_W
        v = tok_ref[at, :].astype(F32)
        d = v - jnp.mean(v, axis=-1, keepdims=True)
        inv = lax.rsqrt(jnp.mean(d * d, axis=-1, keepdims=True) + EPS)
        unit = d * inv
        e = (heads_ref[at, :] + spread[low : low + chunk, :]) * gain_ref[...]
        first = jnp.mean(e, axis=-1, keepdims=True)
        second = jnp.mean(e * unit, axis=-1, keepdims=True)
        u_ref[at, :] = inv * (e - first - unit * second)
    for ref, owner in ((own_ref, h), (sib_ref, sib)):
        ref[...] = u_ref[:, pl.ds(pl.multiple_of(owner * cols, 128), cols)].astype(BF)


def input_rows(pos, norm_gain, reduce_gain, tokens, d_reduced, unit, inverse, d_heads, n_hd):
    own, width = d_heads.shape
    cols = width // n_hd
    groups = d_reduced.shape[0]
    tile = 256
    steps = own // tile
    half = lambda shape: pl.BlockSpec(shape, lambda i, p: (p[1], 0))
    return pl.pallas_call(
        input_kernel,
        grid_spec=pltpu.PrefetchScalarGridSpec(
            num_scalar_prefetch=1,
            grid=(steps,),
            in_specs=[
                fixed((1, width)),
                fixed((1, width)),
                pl.BlockSpec((tile, width), lambda i, p: (p[1] * steps + i, 0)),
                fixed(d_reduced.shape),
                half((groups, width)),
                half((groups, 128)),
                pl.BlockSpec((tile, width), lambda i, p: (i, 0)),
            ],
            out_specs=[
                pl.BlockSpec((tile, cols), lambda i, p: (p[1] * steps + i, 0)),
                pl.BlockSpec((tile, cols), lambda i, p: (i, 0)),
            ],
            scratch_shapes=[
                pltpu.VMEM((groups * POOL, width), F32),
                pltpu.VMEM((tile, width), F32),
            ],
        ),
        out_shape=[
            jax.ShapeDtypeStruct((2 * own, cols), BF),
            jax.ShapeDtypeStruct((own, cols), BF),
        ],
        compiler_params=params(),
        cost_estimate=pl.CostEstimate(
            flops=20 * own * width, bytes_accessed=8 * own * width, transcendentals=0
        ),
        name="input_rows",
    )(
        pos,
        norm_gain.astype(F32).reshape(1, width),
        reduce_gain.astype(F32).reshape(1, width),
        tokens,
        d_reduced,
        unit,
        inverse,
        d_heads,
    )


def small(kernel, name, out_shape, *args, pos=None):
    smem = [] if pos is None else [pl.BlockSpec(memory_space=pltpu.SMEM)]
    vmem = pl.BlockSpec(memory_space=pltpu.VMEM)
    many = isinstance(out_shape, list)
    return pl.pallas_call(
        kernel,
        in_specs=smem + [vmem] * len(args),
        out_specs=[vmem] * len(out_shape) if many else vmem,
        out_shape=out_shape,
        compiler_params=pltpu.CompilerParams(vmem_limit_bytes=VMEM_LIMIT),
        name=name,
    )(*([] if pos is None else [pos]), *args)


def turn_kernel(q_ref, o_ref, k_ref, v_ref, out_ref):
    out_ref[0, 0] = q_ref[...].T
    out_ref[0, 1] = o_ref[...].T
    out_ref[1, 0] = k_ref[...]
    out_ref[1, 1] = v_ref[...]


def project_kernel(pos_ref, red_ref, w_ref, out_ref):
    n_sp, _, depth, feats = w_ref.shape
    z = pos_ref[0]
    for which in range(2):
        total = None
        for place in range(n_sp):
            term = mm(
                red_ref[:, place * depth : (place + 1) * depth],
                w_ref[lax.rem(z - place + n_sp, n_sp), which],
            )
            total = term if total is None else total + term
        out_ref[:, which * feats : (which + 1) * feats] = total.astype(BF)


def back_kernel(pos_ref, d_ref, w_ref, out_ref):
    n_sp, _, depth, feats = w_ref.shape
    z = pos_ref[0]
    for place in range(n_sp):
        piece = lax.rem(z - place + n_sp, n_sp)
        out_ref[:, place * depth : (place + 1) * depth] = (
            mm(d_ref[:, :feats], w_ref[piece, 0], NT) + mm(d_ref[:, feats:], w_ref[piece, 1], NT)
        ).astype(BF)


def kv_grad_kernel(grad_factor, red_ref, d_ref, key_ref, value_ref):
    feats = key_ref.shape[1]
    both = mm(red_ref[...].T, d_ref[...]) * grad_factor
    key_ref[...] = both[:, :feats]
    value_ref[...] = both[:, feats:]


def grad_sum_kernel(*refs):
    query_ref, out_ref = refs[-2:]
    for which, ref in ((0, query_ref), (1, out_ref)):
        total = refs[0][which].astype(F32)
        for part in refs[1:-2]:
            total = total + part[which].astype(F32)
        ref[...] = total.T


def on_device(
    tokens,
    norm_gain,
    reduce_gain,
    query_weight,
    key_weight,
    value_weight,
    out_weight,
    out_cotangent,
):
    n_sp, n_hd, n_scene = lax.axis_size("sp"), lax.axis_size("hd"), lax.axis_size("scene")
    n_x = n_hd // 2
    z, h = lax.axis_index("sp"), lax.axis_index("hd")
    c = h % 2
    depth, feats = query_weight.shape
    count = tokens.shape[0]
    own = count // 2
    grad_factor = float(count * n_sp) ** (-0.5)
    pos = jnp.stack([z, c, h]).astype(jnp.int32)

    def to_sp(value, k):
        return lax.ppermute(value, "sp", [(i, (i + k) % n_sp) for i in range(n_sp)])

    def to_hd(value, k):
        return lax.ppermute(value, "hd", [(i, (i + k) % n_hd) for i in range(n_hd)])

    def swap(value):
        return lax.ppermute(value, "hd", [(i, i ^ 1) for i in range(n_hd)])

    def gather_sp(value):
        return [value] + [to_sp(value, k) for k in range(1, n_sp)]

    def pick(stack, index):
        return lax.dynamic_index_in_dim(stack, index % n_sp, 0, keepdims=False)

    shard = small(
        turn_kernel,
        "turn",
        jax.ShapeDtypeStruct((2, 2, depth, feats), BF),
        query_weight,
        out_weight,
        key_weight,
        value_weight,
    ) if depth == feats else jnp.stack(
        [
            jnp.stack([query_weight.T, out_weight.T]).reshape(2, depth, feats),
            jnp.stack([key_weight, value_weight]),
        ]
    )
    if n_scene == 2:
        y = lax.axis_index("scene")
        half = lax.dynamic_index_in_dim(shard, y, 0, keepdims=False)
        qo, kv_w = [shard[0]], [shard[1]]
        for k in range(1, n_sp):
            here = to_sp(half, k)
            there = lax.ppermute(here, "scene", [(0, 1), (1, 0)])
            qo.append(jnp.where(y == 0, here, there))
            kv_w.append(jnp.where(y == 0, there, here))
    else:
        qo, kv_w = gather_sp(shard[0]), gather_sp(shard[1])
    w_own = jnp.stack(qo).reshape(n_sp, 2, feats, depth)
    wkv = jnp.stack(kv_w)

    normed, reduced, r_unit, r_inverse = norm_and_pool(tokens, norm_gain, reduce_gain)
    blocks = reduced.shape[0]
    reduced_all = jnp.concatenate(gather_sp(reduced))
    kv_own = small(
        project_kernel,
        "project",
        jax.ShapeDtypeStruct((blocks * n_sp, 2 * feats), BF),
        reduced_all,
        wkv,
        pos=pos,
    )

    kvs, ws = [kv_own, swap(kv_own)], [w_own, swap(w_own)]
    for k in range(1, n_x):
        kv_far, w_far = to_hd(kv_own, 2 * k), to_hd(w_own, 2 * k)
        kvs += [kv_far, swap(kv_far)]
        ws += [w_far, swap(w_far)]

    attn0, dq0, grad0, dkv0 = attend(
        pos, normed, out_cotangent, ws[0], kvs[0], grad_factor, F32
    )
    attn1, dq1, grad1, dkv1 = attend(pos, normed, out_cotangent, ws[1], kvs[1], grad_factor, BF)

    dkv = dkv0 + swap(dkv1).astype(F32)
    low = dkv.astype(BF)
    total = dkv[:blocks]
    for k in range(1, n_sp):
        source = n_sp - k
        total = total + to_sp(low[source * blocks : (source + 1) * blocks], k).astype(F32)
    dkv_rows = total.astype(BF)
    d_red = small(
        back_kernel,
        "back",
        jax.ShapeDtypeStruct((blocks, n_sp * depth), BF),
        dkv_rows,
        wkv,
        pos=pos,
    ).reshape(2, blocks // 2, n_sp * depth)

    def half_of(index):
        return lax.dynamic_index_in_dim(d_red, index % 2, 0, keepdims=False)

    d_reduced = half_of(c).astype(F32)
    for k in range(1, n_hd):
        d_reduced = d_reduced + to_hd(half_of(h + k), k).astype(F32)

    dkv_all = jnp.concatenate(gather_sp(dkv_rows))
    reduced_cols = lax.dynamic_slice_in_dim(reduced_all, z * depth, depth, 1)
    key_grad, value_grad = small(
        functools.partial(kv_grad_kernel, grad_factor),
        "kv_grad",
        [jax.ShapeDtypeStruct((depth, feats), F32)] * 2,
        reduced_cols,
        dkv_all,
    )

    grad = (grad0.astype(F32) + swap(grad1).astype(F32)).astype(BF)
    parts = [pick(grad, z)] + [to_sp(pick(grad, z + k), k) for k in range(1, n_sp)]
    query_grad, out_grad = small(
        grad_sum_kernel, "grad_sum", [jax.ShapeDtypeStruct((depth, feats), F32)] * 2, *parts
    )

    branch, other, d_heads = far_heads(
        pos, normed, out_cotangent, [attn0, attn1], [dq0, dq1], ws, kvs[2:], n_hd
    )
    there = (1 - c) * own
    branch = lax.dynamic_update_slice_in_dim(branch, swap(other), there, 0)
    input_grad, other = input_rows(
        pos, norm_gain, reduce_gain, tokens, d_reduced, r_unit, r_inverse, d_heads, n_hd
    )
    input_grad = lax.dynamic_update_slice_in_dim(input_grad, swap(other), there, 0)
    return (branch, input_grad, query_grad, key_grad, value_grad, out_grad)


def solution(mesh):
    rows, whole, both = P(("scene", "sp"), None), P(), P("sp", "hd")
    out = P(("scene", "sp"), "hd")
    return jax.shard_map(
        on_device,
        mesh=mesh,
        in_specs=(rows, whole, whole, both, both, both, both, rows),
        out_specs=(out,) * 6,
        check_vma=False,
    )
```

```python
import functools
import jax
import jax.numpy as jnp
from jax import lax
from jax.experimental import pallas as pl
from jax.experimental.pallas import tpu as pltpu
from jax.sharding import PartitionSpec as P

HEAD_DIM = 64
POOL = 8
GRID_W = 128
EPS = 1e-06
BF = jnp.bfloat16
F32 = jnp.float32
VMEM_LIMIT = 24 * 1024 * 1024

NN = (((1,), (0,)), ((), ()))
TN = (((0,), (0,)), ((), ()))
NT = (((1,), (1,)), ((), ()))


def mm(left, right, dims=NN):
    return lax.dot_general(left, right, dims, preferred_element_type=F32)


def cost(flops, moved):
    return pl.CostEstimate(flops=int(flops), bytes_accessed=int(moved), transcendentals=0)


def params(axes=1):
    return pltpu.CompilerParams(
        dimension_semantics=("arbitrary",) * axes, vmem_limit_bytes=VMEM_LIMIT
    )


def norm_kernel(pos_ref, gain_ref, rgain_ref, tok_ref, cot_ref, normed_ref, cot_out_ref, red_ref,
                runit_ref, rinv_ref, pooled):
    step, col = pl.program_id(0), pl.program_id(1)
    half = pl.num_programs(0) // 2
    row = lax.rem(step + (1 - pos_ref[1]) * half, 2 * half)
    cols, width = tok_ref.shape[1], tok_ref.shape[2]
    gain = gain_ref[...]
    chunk = 2 * POOL
    sums = []
    for part in range(cols // chunk):
        acc = jnp.zeros((chunk, width), F32)
        for r in range(POOL):
            v = tok_ref[r, part * chunk : (part + 1) * chunk, :].astype(F32)
            d = v - jnp.mean(v, axis=-1, keepdims=True)
            inv = lax.rsqrt(jnp.mean(d * d, axis=-1, keepdims=True) + EPS)
            n = (d * inv * gain).astype(BF)
            normed_ref[r, part * chunk : (part + 1) * chunk, :] = n
            acc = acc + n.astype(F32)
        sums.append(jnp.sum(acc.reshape(2, POOL, width), axis=1))
    span = cols // POOL
    base = pl.multiple_of((row * pl.num_programs(1) + col) * span, span)
    pooled[pl.ds(base, span), :] = jnp.concatenate(sums, axis=0)

    @pl.when(step >= half)
    def _():
        cot_out_ref[...] = cot_ref[...]

    @pl.when((step == pl.num_programs(0) - 1) & (col == pl.num_programs(1) - 1))
    def _():
        v = pooled[...] / (POOL * POOL)
        d = v - jnp.mean(v, axis=-1, keepdims=True)
        inv = lax.rsqrt(jnp.mean(d * d, axis=-1, keepdims=True) + EPS)
        unit = d * inv
        runit_ref[...] = unit
        rinv_ref[...] = jnp.broadcast_to(inv, rinv_ref.shape)
        red_ref[...] = (unit * rgain_ref[...]).astype(BF)


def norm_and_pool(pos, tokens, cotangent, norm_gain, reduce_gain):
    count, width = tokens.shape
    grid_rows = count // GRID_W
    blocks = count // (POOL * POOL)
    cols = 64
    rows = grid_rows // POOL
    half = rows // 2
    block = (POOL, cols, width)

    def own(i):
        return jnp.maximum(i - half, 0)

    def own_col(i, j):
        return jnp.where(i >= half, j, 0)

    tok = pl.BlockSpec(block, lambda i, j, p: (lax.rem(i + (1 - p[1]) * half, rows), j, 0))
    cot = pl.BlockSpec(block, lambda i, j, p: (p[1] * half + own(i), own_col(i, j), 0))
    out = pl.BlockSpec(block, lambda i, j, p: (own(i), own_col(i, j), 0))
    whole = lambda shape: pl.BlockSpec(shape, lambda i, j, p: (0,) * len(shape))
    normed, cot_own, reduced, unit, inverse = pl.pallas_call(
        norm_kernel,
        grid_spec=pltpu.PrefetchScalarGridSpec(
            num_scalar_prefetch=1,
            grid=(rows, GRID_W // cols),
            in_specs=[whole((1, width)), whole((1, width)), tok, cot],
            out_specs=[
                out,
                out,
                whole((blocks, width)),
                whole((blocks, width)),
                whole((blocks, 128)),
            ],
            scratch_shapes=[pltpu.VMEM((blocks, width), F32)],
        ),
        out_shape=[
            jax.ShapeDtypeStruct((grid_rows // 2, GRID_W, width), BF),
            jax.ShapeDtypeStruct((grid_rows // 2, GRID_W, width), BF),
            jax.ShapeDtypeStruct((blocks, width), BF),
            jax.ShapeDtypeStruct((blocks, width), F32),
            jax.ShapeDtypeStruct((blocks, 128), F32),
        ],
        compiler_params=params(2),
        cost_estimate=cost(40 * count * width, 10 * count * width),
        name="norm_pool",
    )(
        pos,
        norm_gain.astype(F32).reshape(1, width),
        reduce_gain.astype(F32).reshape(1, width),
        tokens.reshape(grid_rows, GRID_W, width),
        cotangent.reshape(grid_rows, GRID_W, width),
    )
    return (
        normed.reshape(count // 2, width),
        cot_own.reshape(count // 2, width),
        reduced,
        unit,
        inverse,
    )


def head_mask(shape, head):
    lane = lax.broadcasted_iota(jnp.int32, shape, 1)
    return (lane >= head * HEAD_DIM) & (lane < (head + 1) * HEAD_DIM)


def spread_heads(kv_ref, kbd, vbd, kbd_t, vbd_t):
    blocks, feats = kv_ref.shape[0], kv_ref.shape[1] // 2
    k = kv_ref[:, :feats].astype(F32) * HEAD_DIM ** (-0.5)
    v = kv_ref[:, feats:].astype(F32)
    for head in range(feats // HEAD_DIM):
        mask = head_mask((blocks, feats), head)
        rows = slice(head * blocks, (head + 1) * blocks)
        kbd[rows, :] = jnp.where(mask, k, 0.0).astype(BF)
        vbd[rows, :] = jnp.where(mask, v, 0.0).astype(BF)
    kbd_t[...] = kbd[...].T
    vbd_t[...] = vbd[...].T


def attend_tile(x, y, w_ref, kbd, vbd, kbd_t, vbd_t):
    feats = w_ref.shape[1]
    heads = feats // HEAD_DIM
    blocks = kbd.shape[0] // heads
    q_t = mm(w_ref[0], x, NT).astype(BF)
    da_t = mm(w_ref[1], y, NT).astype(BF)
    scores = mm(kbd[...], q_t)
    d_chances = mm(vbd[...], da_t)
    low, d_low = [], []
    for head in range(heads):
        rows = slice(head * blocks, (head + 1) * blocks)
        s = scores[rows]
        e = jnp.exp(s - jnp.max(s, axis=0, keepdims=True))
        p = e * (1.0 / jnp.sum(e, axis=0, keepdims=True))
        dp = d_chances[rows]
        delta = jnp.sum(p * dp, axis=0, keepdims=True)
        low.append(p.astype(BF))
        d_low.append((p * (dp - delta)).astype(BF))
    low = jnp.concatenate(low, axis=0)
    d_low = jnp.concatenate(d_low, axis=0)
    attn_t = mm(vbd_t[...], low).astype(BF)
    dq_t = mm(kbd_t[...], d_low).astype(BF)
    return q_t, da_t, low, d_low, attn_t, dq_t


def head_scratch(heads, blocks, feats):
    return [
        pltpu.VMEM((heads * blocks, feats), BF),
        pltpu.VMEM((heads * blocks, feats), BF),
        pltpu.VMEM((feats, heads * blocks), BF),
        pltpu.VMEM((feats, heads * blocks), BF),
    ]


def attend_kernel(n_sp, grad_factor, x_ref, y_ref, w_ref, kv_ref, attn_ref, dq_ref, *rest):
    step = pl.program_id(0)
    feats, width = w_ref.shape[1], w_ref.shape[2]
    blocks = kv_ref.shape[0]
    depth = width // n_sp
    heads_at = rest[-4:] if len(rest) == 4 else rest[2:6]
    if len(rest) > 4:
        grad_ref, dkv_ref = rest[:2]
        dk_acc, dv_acc, g_acc = rest[6:]

    @pl.when(step == 0)
    def _():
        spread_heads(kv_ref, *heads_at)
        if len(rest) > 4:
            dk_acc[...] = jnp.zeros_like(dk_acc)
            dv_acc[...] = jnp.zeros_like(dv_acc)
            g_acc[...] = jnp.zeros_like(g_acc)

    x, y = x_ref[...], y_ref[...]
    q_t, da_t, low, d_low, attn_t, dq_t = attend_tile(x, y, w_ref, *heads_at)
    attn_ref[...] = attn_t
    dq_ref[...] = dq_t
    if len(rest) == 4:
        return
    dk_acc[...] += mm(d_low, q_t, NT)
    dv_acc[...] += mm(low, da_t, NT)
    g_acc[0] += mm(dq_t, x)
    g_acc[1] += mm(attn_t, y)

    @pl.when(step == pl.num_programs(0) - 1)
    def _():
        dk = jnp.zeros((blocks, feats), F32)
        dv = jnp.zeros((blocks, feats), F32)
        for head in range(feats // HEAD_DIM):
            mask = head_mask((blocks, feats), head)
            rows = slice(head * blocks, (head + 1) * blocks)
            dk = dk + jnp.where(mask, dk_acc[rows, :], 0.0)
            dv = dv + jnp.where(mask, dv_acc[rows, :], 0.0)
        dkv_ref[:, :feats] = (dk * HEAD_DIM ** (-0.5)).astype(dkv_ref.dtype)
        dkv_ref[:, feats:] = dv.astype(dkv_ref.dtype)
        for place in range(n_sp):
            cols = slice(place * depth, (place + 1) * depth)
            grad_ref[place] = (g_acc[:, :, cols] * grad_factor).astype(BF)


def fixed(shape):
    return pl.BlockSpec(shape, lambda i: (0,) * len(shape))


def attend(n_sp, normed, cotangent, weights, kv, grad_factor=None, dkv_type=BF):
    _, feats, width = weights.shape
    own = normed.shape[0]
    blocks = kv.shape[0]
    heads = feats // HEAD_DIM
    tile = 256
    rows = pl.BlockSpec((tile, width), lambda i: (i, 0))
    t_spec = pl.BlockSpec((feats, tile), lambda i: (0, i))
    out_specs = [t_spec, t_spec]
    out_shape = [jax.ShapeDtypeStruct((feats, own), BF)] * 2
    scratch = head_scratch(heads, blocks, feats)
    flops = 4 * own * width * feats + 8 * own * heads * blocks * feats
    if grad_factor is not None:
        grad_shape = (n_sp, 2, feats, width // n_sp)
        out_specs += [fixed(grad_shape), fixed((blocks, 2 * feats))]
        out_shape += [
            jax.ShapeDtypeStruct(grad_shape, BF),
            jax.ShapeDtypeStruct((blocks, 2 * feats), dkv_type),
        ]
        scratch += [
            pltpu.VMEM((heads * blocks, feats), F32),
            pltpu.VMEM((heads * blocks, feats), F32),
            pltpu.VMEM(weights.shape, F32),
        ]
        flops = flops + 4 * own * width * feats + 4 * own * heads * blocks * feats
    return pl.pallas_call(
        functools.partial(attend_kernel, n_sp, grad_factor),
        grid=(own // tile,),
        in_specs=[rows, rows, fixed(weights.shape), fixed(kv.shape)],
        out_specs=out_specs,
        out_shape=out_shape,
        scratch_shapes=scratch,
        compiler_params=params(),
        cost_estimate=cost(2 * flops, 4 * own * width + 8 * width * feats),
        name="attend" if grad_factor is None else "attend_grads",
    )(normed, cotangent, weights, kv)


def rows_kernel(count, pos_ref, *refs):
    attn_refs, refs = refs[:count], refs[count:]
    dq_refs, refs = refs[:count], refs[count:]
    w_refs, (own_ref, sib_ref, heads_ref) = refs[:count], refs[count:]
    h = pos_ref[2]
    sib = h + 1 - 2 * lax.rem(h, 2)
    cols = own_ref.shape[1]
    rows = [ref[...].T for ref in attn_refs]
    for ref, owner in ((own_ref, h), (sib_ref, sib)):
        lanes = pl.ds(pl.multiple_of(owner * cols, 128), cols)
        total = None
        for row, w_ref in zip(rows, w_refs):
            term = mm(row, w_ref[1, :, lanes]).astype(BF).astype(F32)
            total = term if total is None else total + term
        ref[...] = total.astype(BF)
    total = None
    for dq_ref, w_ref in zip(dq_refs, w_refs):
        term = mm(dq_ref[...].T, w_ref[0]).astype(BF).astype(F32)
        total = term if total is None else total + term
    heads_ref[...] = total


def model_rows(pos, attns, dqs, weights, n_hd):
    count = len(attns)
    _, feats, width = weights[0].shape
    own = attns[0].shape[1]
    cols = width // n_hd
    tile = 256
    steps = own // tile
    whole = lambda shape: pl.BlockSpec(shape, lambda i, p: (0,) * len(shape))
    t_spec = pl.BlockSpec((feats, tile), lambda i, p: (0, i))
    return pl.pallas_call(
        functools.partial(rows_kernel, count),
        grid_spec=pltpu.PrefetchScalarGridSpec(
            num_scalar_prefetch=1,
            grid=(steps,),
            in_specs=[t_spec] * (2 * count) + [whole(w.shape) for w in weights],
            out_specs=[
                pl.BlockSpec((tile, cols), lambda i, p: (p[1] * steps + i, 0)),
                pl.BlockSpec((tile, cols), lambda i, p: (i, 0)),
                pl.BlockSpec((tile, width), lambda i, p: (i, 0)),
            ],
        ),
        out_shape=[
            jax.ShapeDtypeStruct((2 * own, cols), BF),
            jax.ShapeDtypeStruct((own, cols), BF),
            jax.ShapeDtypeStruct((own, width), F32),
        ],
        compiler_params=params(),
        cost_estimate=cost(4 * own * width * (width + 2 * cols), 12 * own * width),
        name="model_rows",
    )(pos, *attns, *dqs, *weights)


def input_kernel(pos_ref, gain_ref, rgain_ref, tok_ref, dred_ref, runit_ref, rinv_ref, heads_ref,
                 own_ref, sib_ref, spread, u_ref):
    width = tok_ref.shape[1]
    h = pos_ref[2]
    sib = h + 1 - 2 * lax.rem(h, 2)
    cols = own_ref.shape[1]

    @pl.when(pl.program_id(0) == 0)
    def _():
        groups = runit_ref.shape[0]
        e = dred_ref[...] * rgain_ref[...]
        unit = runit_ref[...]
        first = jnp.mean(e, axis=-1, keepdims=True)
        second = jnp.mean(e * unit, axis=-1, keepdims=True)
        d_pooled = rinv_ref[:, 0:1] * (e - first - unit * second) / (POOL * POOL)
        spread[...] = jnp.broadcast_to(d_pooled[:, None, :], (groups, POOL, width)).reshape(
            groups * POOL, width
        )

    chunk = 2 * POOL
    for part in range(tok_ref.shape[0] // chunk):
        at = slice(part * chunk, (part + 1) * chunk)
        low = (part * chunk) % GRID_W
        v = tok_ref[at, :].astype(F32)
        d = v - jnp.mean(v, axis=-1, keepdims=True)
        inv = lax.rsqrt(jnp.mean(d * d, axis=-1, keepdims=True) + EPS)
        unit = d * inv
        e = (heads_ref[at, :] + spread[low : low + chunk, :]) * gain_ref[...]
        first = jnp.mean(e, axis=-1, keepdims=True)
        second = jnp.mean(e * unit, axis=-1, keepdims=True)
        u_ref[at, :] = inv * (e - first - unit * second)
    for ref, owner in ((own_ref, h), (sib_ref, sib)):
        ref[...] = u_ref[:, pl.ds(pl.multiple_of(owner * cols, 128), cols)].astype(BF)


def input_rows(pos, norm_gain, reduce_gain, tokens, d_reduced, unit, inverse, d_heads, n_hd):
    own, width = d_heads.shape
    cols = width // n_hd
    groups = d_reduced.shape[0]
    tile = 256
    steps = own // tile
    whole = lambda shape: pl.BlockSpec(shape, lambda i, p: (0,) * len(shape))
    half = lambda shape: pl.BlockSpec(shape, lambda i, p: (p[1], 0))
    return pl.pallas_call(
        input_kernel,
        grid_spec=pltpu.PrefetchScalarGridSpec(
            num_scalar_prefetch=1,
            grid=(steps,),
            in_specs=[
                whole((1, width)),
                whole((1, width)),
                pl.BlockSpec((tile, width), lambda i, p: (p[1] * steps + i, 0)),
                whole(d_reduced.shape),
                half((groups, width)),
                half((groups, 128)),
                pl.BlockSpec((tile, width), lambda i, p: (i, 0)),
            ],
            out_specs=[
                pl.BlockSpec((tile, cols), lambda i, p: (p[1] * steps + i, 0)),
                pl.BlockSpec((tile, cols), lambda i, p: (i, 0)),
            ],
            scratch_shapes=[
                pltpu.VMEM((groups * POOL, width), F32),
                pltpu.VMEM((tile, width), F32),
            ],
        ),
        out_shape=[
            jax.ShapeDtypeStruct((2 * own, cols), BF),
            jax.ShapeDtypeStruct((own, cols), BF),
        ],
        compiler_params=params(),
        cost_estimate=cost(40 * own * width, 16 * own * width),
        name="input_rows",
    )(
        pos,
        norm_gain.astype(F32).reshape(1, width),
        reduce_gain.astype(F32).reshape(1, width),
        tokens,
        d_reduced,
        unit,
        inverse,
        d_heads,
    )


def small(kernel, name, out_shape, *args, pos=None):
    smem = [] if pos is None else [pl.BlockSpec(memory_space=pltpu.SMEM)]
    vmem = pl.BlockSpec(memory_space=pltpu.VMEM)
    many = isinstance(out_shape, list)
    return pl.pallas_call(
        kernel,
        in_specs=smem + [vmem] * len(args),
        out_specs=[vmem] * len(out_shape) if many else vmem,
        out_shape=out_shape,
        compiler_params=pltpu.CompilerParams(vmem_limit_bytes=VMEM_LIMIT),
        cost_estimate=cost(1 << 28, 1 << 21),
        name=name,
    )(*([] if pos is None else [pos]), *args)


def turn_kernel(q_ref, o_ref, out_ref):
    out_ref[0] = q_ref[...].T
    out_ref[1] = o_ref[...].T


def choose(index, values):
    result = values[0]
    for k in range(1, len(values)):
        result = jnp.where(index == k, values[k], result)
    return result


def assemble_kernel(n_sp, pos_ref, own_ref, *refs):
    here, there, out_ref = refs[: n_sp - 1], refs[n_sp - 1 : 2 * n_sp - 2], refs[-1]
    depth = own_ref.shape[2]
    z, y = pos_ref[0], pos_ref[3]
    for which in range(2):
        pieces = [own_ref[which]] + [
            jnp.where(y == which, a[...], b[...]) for a, b in zip(here, there)
        ]
        for place in range(n_sp):
            index = lax.rem(z - place + n_sp, n_sp)
            out_ref[which, :, place * depth : (place + 1) * depth] = choose(index, pieces)


def project_kernel(k_ref, v_ref, *refs):
    red, (cols_ref, part_ref, low_ref) = refs[:-3], refs[-3:]
    feats = k_ref.shape[1]
    rows = jnp.concatenate([ref[...] for ref in red], axis=0)
    cols_ref[...] = rows
    for which, ref in ((0, k_ref), (1, v_ref)):
        lanes = slice(which * feats, (which + 1) * feats)
        part = mm(rows, ref[...])
        part_ref[:, lanes] = part
        low_ref[:, lanes] = part.astype(BF)


def kv_sum_kernel(blocks, own_ref, *refs):
    parts, out_ref = refs[:-1], refs[-1]
    n_sp = len(parts) + 1
    for j in range(n_sp):
        total = own_ref[j * blocks : (j + 1) * blocks, :]
        for k, part in enumerate(parts, 1):
            at = (j - k) % n_sp
            total = total + part[at * blocks : (at + 1) * blocks, :].astype(F32)
        out_ref[j * blocks : (j + 1) * blocks, :] = total.astype(BF)


def back_kernel(n_sp, pos_ref, *refs):
    blocks = refs[0].shape[0]
    rows, weights, (low_ref, out_ref) = refs[:n_sp], refs[n_sp : 2 * n_sp], refs[-2:]
    depth, feats = weights[0].shape[1:]
    z = pos_ref[0]
    total = rows[0][...]
    for part in rows[1:]:
        total = total + part[...].astype(F32)
    low = total.astype(BF)
    low_ref[...] = low
    terms = [mm(low[:, :feats], w[0], NT) + mm(low[:, feats:], w[1], NT) for w in weights]
    for place in range(n_sp):
        index = lax.rem(z - place + n_sp, n_sp)
        out_ref[:, place * depth : (place + 1) * depth] = choose(index, terms).astype(BF)


def kv_grad_kernel(grad_factor, red_ref, *refs):
    rows, (key_ref, value_ref) = refs[:-2], refs[-2:]
    feats = key_ref.shape[1]
    d_kv = jnp.concatenate([ref[...] for ref in rows], axis=0)
    both = mm(red_ref[...].T, d_kv) * grad_factor
    key_ref[...] = both[:, :feats]
    value_ref[...] = both[:, feats:]


def grad_sum_kernel(*refs):
    query_ref, out_ref = refs[-2:]
    for which, ref in ((0, query_ref), (1, out_ref)):
        total = refs[0][which].astype(F32)
        for part in refs[1:-2]:
            total = total + part[which].astype(F32)
        ref[...] = total.T


def on_device(
    tokens,
    norm_gain,
    reduce_gain,
    query_weight,
    key_weight,
    value_weight,
    out_weight,
    out_cotangent,
):
    n_sp, n_hd, n_scene = lax.axis_size("sp"), lax.axis_size("hd"), lax.axis_size("scene")
    n_x = n_hd // 2
    z, h, y = lax.axis_index("sp"), lax.axis_index("hd"), lax.axis_index("scene")
    c = h % 2
    depth, feats = query_weight.shape
    width = tokens.shape[1]
    own = tokens.shape[0] // 2
    grad_factor = float(2 * own * n_sp) ** (-0.5)
    pos = jnp.stack([z, c, h, y]).astype(jnp.int32)
    others = range(1, n_sp)

    def to_sp(value, k):
        return lax.ppermute(value, "sp", [(i, (i + k) % n_sp) for i in range(n_sp)])

    def to_hd(value, k):
        return lax.ppermute(value, "hd", [(i, (i + k) % n_hd) for i in range(n_hd)])

    def swap(value):
        return lax.ppermute(value, "hd", [(i, i ^ 1) for i in range(n_hd)])

    def pick(stack, index):
        return lax.dynamic_index_in_dim(stack, index % n_sp, 0, keepdims=False)

    shard = small(
        turn_kernel, "turn", jax.ShapeDtypeStruct((2, feats, depth), BF), query_weight, out_weight
    )
    if n_scene == 2:
        half = lax.dynamic_index_in_dim(shard, y, 0, keepdims=False)
        here = [to_sp(half, k) for k in others]
        there = [lax.ppermute(value, "scene", [(0, 1), (1, 0)]) for value in here]
    else:
        here = [to_sp(shard[0], k) for k in others]
        there = [to_sp(shard[1], k) for k in others]
    w_own = small(
        functools.partial(assemble_kernel, n_sp),
        "assemble",
        jax.ShapeDtypeStruct((2, feats, width), BF),
        shard,
        *here,
        *there,
        pos=pos if n_scene == 2 else pos.at[3].set(0),
    )

    normed, cot, reduced, r_unit, r_inverse = norm_and_pool(
        pos, tokens, out_cotangent, norm_gain, reduce_gain
    )
    blocks = reduced.shape[0]
    red_cut = jnp.stack([reduced[:, i * depth : (i + 1) * depth] for i in range(n_sp)])
    reds = [pick(red_cut, z)] + [to_sp(pick(red_cut, z + k), k) for k in others]
    both = (blocks * n_sp, 2 * feats)
    reduced_cols, kv_part, kv_low = small(
        project_kernel,
        "project",
        [
            jax.ShapeDtypeStruct((blocks * n_sp, depth), BF),
            jax.ShapeDtypeStruct(both, F32),
            jax.ShapeDtypeStruct(both, BF),
        ],
        key_weight,
        value_weight,
        *reds,
    )
    kv_own = small(
        functools.partial(kv_sum_kernel, blocks),
        "kv_sum",
        jax.ShapeDtypeStruct(both, BF),
        kv_part,
        *[to_sp(kv_low, k) for k in others],
    )

    kvs, ws = [kv_own, swap(kv_own)], [w_own, swap(w_own)]
    for k in range(1, n_x):
        kv_far, w_far = to_hd(kv_own, 2 * k), to_hd(w_own, 2 * k)
        kvs += [kv_far, swap(kv_far)]
        ws += [w_far, swap(w_far)]

    kv_weight, _ = lax.optimization_barrier((jnp.stack([key_weight, value_weight]), kv_own))
    kv_weights = [kv_weight] + [to_sp(kv_weight, k) for k in others]

    attn0, dq0, grad0, dkv0 = attend(n_sp, normed, cot, ws[0], kvs[0], grad_factor, F32)
    attn1, dq1, grad1, dkv1 = attend(n_sp, normed, cot, ws[1], kvs[1], grad_factor, BF)
    attns, dqs = [attn0, attn1], [dq0, dq1]

    dkv = dkv0 + swap(dkv1).astype(F32)
    low = dkv.astype(BF)
    rows = [dkv[:blocks]] + [
        to_sp(low[(n_sp - k) * blocks : (n_sp - k + 1) * blocks], k) for k in others
    ]
    dkv_rows, d_red = small(
        functools.partial(back_kernel, n_sp),
        "back",
        [
            jax.ShapeDtypeStruct((blocks, 2 * feats), BF),
            jax.ShapeDtypeStruct((blocks, width), BF),
        ],
        *rows,
        *kv_weights,
        pos=pos,
    )
    d_red = d_red.reshape(2, blocks // 2, width)

    def half_of(index):
        return lax.dynamic_index_in_dim(d_red, index % 2, 0, keepdims=False)

    d_reduced = half_of(c).astype(F32)
    for k in range(1, n_hd):
        d_reduced = d_reduced + to_hd(half_of(h + k), k).astype(F32)

    grad = (grad0.astype(F32) + swap(grad1).astype(F32)).astype(BF)
    parts = [pick(grad, z)] + [to_sp(pick(grad, z + k), k) for k in others]
    query_grad, out_grad = small(
        grad_sum_kernel, "grad_sum", [jax.ShapeDtypeStruct((depth, feats), F32)] * 2, *parts
    )

    key_grad, value_grad = small(
        functools.partial(kv_grad_kernel, grad_factor),
        "kv_grad",
        [jax.ShapeDtypeStruct((depth, feats), F32)] * 2,
        reduced_cols,
        dkv_rows,
        *[to_sp(dkv_rows, k) for k in others],
    )

    for w, kv in zip(ws[2:], kvs[2:]):
        attn, dq = attend(n_sp, normed, cot, w, kv)
        attns.append(attn)
        dqs.append(dq)
    branch, other, d_heads = model_rows(pos, attns, dqs, ws, n_hd)
    place = (1 - c) * own
    branch = lax.dynamic_update_slice_in_dim(branch, swap(other), place, 0)
    input_grad, other = input_rows(
        pos, norm_gain, reduce_gain, tokens, d_reduced, r_unit, r_inverse, d_heads, n_hd
    )
    input_grad = lax.dynamic_update_slice_in_dim(input_grad, swap(other), place, 0)
    return (branch, input_grad, query_grad, key_grad, value_grad, out_grad)


def solution(mesh):
    rows, whole, both = P(("scene", "sp"), None), P(), P("sp", "hd")
    out = P(("scene", "sp"), "hd")
    return jax.shard_map(
        on_device,
        mesh=mesh,
        in_specs=(rows, whole, whole, both, both, both, both, rows),
        out_specs=(out,) * 6,
        check_vma=False,
    )
```

```python
import functools
import jax
import jax.numpy as jnp
from jax import lax
from jax.experimental import pallas as pl
from jax.experimental.pallas import tpu as pltpu
from jax.sharding import PartitionSpec as P

HEAD_DIM = 64
POOL = 8
GRID_W = 128
EPS = 1e-06
BF = jnp.bfloat16
F32 = jnp.float32
VMEM_LIMIT = 24 * 1024 * 1024

NN = (((1,), (0,)), ((), ()))
TN = (((0,), (0,)), ((), ()))
NT = (((1,), (1,)), ((), ()))


def mm(left, right, dims=NN):
    return lax.dot_general(left, right, dims, preferred_element_type=F32)


def cost(flops, moved):
    return pl.CostEstimate(flops=int(flops), bytes_accessed=int(moved), transcendentals=0)


ANY = pl.BlockSpec(memory_space=pl.ANY)


def after(kernel, inputs, deps):
    return lambda *refs: kernel(*refs[:inputs], *refs[inputs + deps :])


def params(axes=1):
    return pltpu.CompilerParams(
        dimension_semantics=("arbitrary",) * axes, vmem_limit_bytes=VMEM_LIMIT
    )


def norm_kernel(pos_ref, gain_ref, rgain_ref, tok_ref, cot_ref, normed_ref, cot_out_ref, red_ref,
                runit_ref, rinv_ref, pooled):
    step, col = pl.program_id(0), pl.program_id(1)
    half = pl.num_programs(0) // 2
    row = lax.rem(step + (1 - pos_ref[1]) * half, 2 * half)
    cols, width = tok_ref.shape[1], tok_ref.shape[2]
    gain = gain_ref[...]
    chunk = 2 * POOL
    sums = []
    for part in range(cols // chunk):
        acc = jnp.zeros((chunk, width), F32)
        for r in range(POOL):
            v = tok_ref[r, part * chunk : (part + 1) * chunk, :].astype(F32)
            d = v - jnp.mean(v, axis=-1, keepdims=True)
            inv = lax.rsqrt(jnp.mean(d * d, axis=-1, keepdims=True) + EPS)
            n = (d * inv * gain).astype(BF)
            normed_ref[r, part * chunk : (part + 1) * chunk, :] = n
            acc = acc + n.astype(F32)
        sums.append(jnp.sum(acc.reshape(2, POOL, width), axis=1))
    span = cols // POOL
    base = pl.multiple_of((row * pl.num_programs(1) + col) * span, span)
    pooled[pl.ds(base, span), :] = jnp.concatenate(sums, axis=0)

    @pl.when(step >= half)
    def _():
        cot_out_ref[...] = cot_ref[...]

    @pl.when((step == pl.num_programs(0) - 1) & (col == pl.num_programs(1) - 1))
    def _():
        v = pooled[...] / (POOL * POOL)
        d = v - jnp.mean(v, axis=-1, keepdims=True)
        inv = lax.rsqrt(jnp.mean(d * d, axis=-1, keepdims=True) + EPS)
        unit = d * inv
        runit_ref[...] = unit
        rinv_ref[...] = jnp.broadcast_to(inv, rinv_ref.shape)
        red_ref[...] = (unit * rgain_ref[...]).astype(BF)


def norm_and_pool(pos, tokens, cotangent, norm_gain, reduce_gain, deps):
    count, width = tokens.shape
    grid_rows = count // GRID_W
    blocks = count // (POOL * POOL)
    cols = 64
    rows = grid_rows // POOL
    half = rows // 2
    block = (POOL, cols, width)

    def own(i):
        return jnp.maximum(i - half, 0)

    def own_col(i, j):
        return jnp.where(i >= half, j, 0)

    tok = pl.BlockSpec(block, lambda i, j, p: (lax.rem(i + (1 - p[1]) * half, rows), j, 0))
    cot = pl.BlockSpec(block, lambda i, j, p: (p[1] * half + own(i), own_col(i, j), 0))
    out = pl.BlockSpec(block, lambda i, j, p: (own(i), own_col(i, j), 0))
    whole = lambda shape: pl.BlockSpec(shape, lambda i, j, p: (0,) * len(shape))
    normed, cot_own, reduced, unit, inverse = pl.pallas_call(
        after(norm_kernel, 5, len(deps)),
        grid_spec=pltpu.PrefetchScalarGridSpec(
            num_scalar_prefetch=1,
            grid=(rows, GRID_W // cols),
            in_specs=[whole((1, width)), whole((1, width)), tok, cot]
            + [ANY] * len(deps),
            out_specs=[
                out,
                out,
                whole((blocks, width)),
                whole((blocks, width)),
                whole((blocks, 128)),
            ],
            scratch_shapes=[pltpu.VMEM((blocks, width), F32)],
        ),
        out_shape=[
            jax.ShapeDtypeStruct((grid_rows // 2, GRID_W, width), BF),
            jax.ShapeDtypeStruct((grid_rows // 2, GRID_W, width), BF),
            jax.ShapeDtypeStruct((blocks, width), BF),
            jax.ShapeDtypeStruct((blocks, width), F32),
            jax.ShapeDtypeStruct((blocks, 128), F32),
        ],
        compiler_params=params(2),
        cost_estimate=cost(40 * count * width, 10 * count * width),
        name="norm_pool",
    )(
        pos,
        norm_gain.astype(F32).reshape(1, width),
        reduce_gain.astype(F32).reshape(1, width),
        tokens.reshape(grid_rows, GRID_W, width),
        cotangent.reshape(grid_rows, GRID_W, width),
        *deps,
    )
    return (
        normed.reshape(count // 2, width),
        cot_own.reshape(count // 2, width),
        reduced,
        unit,
        inverse,
    )


def spread_heads(w_ref, width, kbd, vbd, kbd_t, vbd_t):
    feats, blocks = w_ref.shape[1], w_ref.shape[2] - width
    row = lax.broadcasted_iota(jnp.int32, (feats, blocks), 0)
    k = w_ref[0, :, width:].astype(F32) * HEAD_DIM ** (-0.5)
    v = w_ref[1, :, width:].astype(F32)
    for head in range(feats // HEAD_DIM):
        mask = (row >= head * HEAD_DIM) & (row < (head + 1) * HEAD_DIM)
        lanes = slice(head * blocks, (head + 1) * blocks)
        kbd_t[:, lanes] = jnp.where(mask, k, 0.0).astype(BF)
        vbd_t[:, lanes] = jnp.where(mask, v, 0.0).astype(BF)
    kbd[...] = kbd_t[...].T
    vbd[...] = vbd_t[...].T


def attend_tile(x, y, w_ref, kbd, vbd, kbd_t, vbd_t):
    feats = w_ref.shape[1]
    heads = feats // HEAD_DIM
    blocks = kbd.shape[0] // heads
    q_t = mm(w_ref[0, :, : x.shape[1]], x, NT).astype(BF)
    da_t = mm(w_ref[1, :, : y.shape[1]], y, NT).astype(BF)
    scores = mm(kbd[...], q_t)
    d_chances = mm(vbd[...], da_t)
    low, d_low = [], []
    for head in range(heads):
        rows = slice(head * blocks, (head + 1) * blocks)
        s = scores[rows]
        e = jnp.exp(s - jnp.max(s, axis=0, keepdims=True))
        p = e * (1.0 / jnp.sum(e, axis=0, keepdims=True))
        dp = d_chances[rows]
        delta = jnp.sum(p * dp, axis=0, keepdims=True)
        low.append(p.astype(BF))
        d_low.append((p * (dp - delta)).astype(BF))
    low = jnp.concatenate(low, axis=0)
    d_low = jnp.concatenate(d_low, axis=0)
    attn_t = mm(vbd_t[...], low).astype(BF)
    dq_t = mm(kbd_t[...], d_low).astype(BF)
    return q_t, da_t, low, d_low, attn_t, dq_t


def head_mask(shape, head):
    lane = lax.broadcasted_iota(jnp.int32, shape, 1)
    return (lane >= head * HEAD_DIM) & (lane < (head + 1) * HEAD_DIM)


def head_scratch(heads, blocks, feats):
    return [
        pltpu.VMEM((heads * blocks, feats), BF),
        pltpu.VMEM((heads * blocks, feats), BF),
        pltpu.VMEM((feats, heads * blocks), BF),
        pltpu.VMEM((feats, heads * blocks), BF),
    ]


def attend_kernel(n_sp, grad_factor, x_ref, y_ref, w_ref, attn_ref, dq_ref, *rest):
    step = pl.program_id(0)
    feats, width = w_ref.shape[1], x_ref.shape[1]
    blocks = w_ref.shape[2] - width
    depth = width // n_sp
    heads_at = rest[-4:] if len(rest) == 4 else rest[2:6]
    if len(rest) > 4:
        grad_ref, dkv_ref = rest[:2]
        dk_acc, dv_acc, g_acc = rest[6:]

    @pl.when(step == 0)
    def _():
        spread_heads(w_ref, width, *heads_at)
        if len(rest) > 4:
            dk_acc[...] = jnp.zeros_like(dk_acc)
            dv_acc[...] = jnp.zeros_like(dv_acc)
            g_acc[...] = jnp.zeros_like(g_acc)

    x, y = x_ref[...], y_ref[...]
    q_t, da_t, low, d_low, attn_t, dq_t = attend_tile(x, y, w_ref, *heads_at)
    attn_ref[...] = attn_t
    dq_ref[...] = dq_t
    if len(rest) == 4:
        return
    dk_acc[...] += mm(d_low, q_t, NT)
    dv_acc[...] += mm(low, da_t, NT)
    g_acc[0] += mm(dq_t, x)
    g_acc[1] += mm(attn_t, y)

    @pl.when(step == pl.num_programs(0) - 1)
    def _():
        dk = jnp.zeros((blocks, feats), F32)
        dv = jnp.zeros((blocks, feats), F32)
        for head in range(feats // HEAD_DIM):
            mask = head_mask((blocks, feats), head)
            rows = slice(head * blocks, (head + 1) * blocks)
            dk = dk + jnp.where(mask, dk_acc[rows, :], 0.0)
            dv = dv + jnp.where(mask, dv_acc[rows, :], 0.0)
        dkv_ref[:, :feats] = (dk * HEAD_DIM ** (-0.5)).astype(dkv_ref.dtype)
        dkv_ref[:, feats:] = dv.astype(dkv_ref.dtype)
        for place in range(n_sp):
            cols = slice(place * depth, (place + 1) * depth)
            grad_ref[place] = (g_acc[:, :, cols] * grad_factor).astype(BF)


def fixed(shape):
    return pl.BlockSpec(shape, lambda i: (0,) * len(shape))


def attend(n_sp, normed, cotangent, weights, deps, grad_factor=None, dkv_type=BF):
    feats = weights.shape[1]
    own, width = normed.shape
    blocks = weights.shape[2] - width
    heads = feats // HEAD_DIM
    tile = 256
    rows = pl.BlockSpec((tile, width), lambda i: (i, 0))
    t_spec = pl.BlockSpec((feats, tile), lambda i: (0, i))
    out_specs = [t_spec, t_spec]
    out_shape = [jax.ShapeDtypeStruct((feats, own), BF)] * 2
    scratch = head_scratch(heads, blocks, feats)
    flops = 4 * own * width * feats + 8 * own * heads * blocks * feats
    if grad_factor is not None:
        grad_shape = (n_sp, 2, feats, width // n_sp)
        out_specs += [fixed(grad_shape), fixed((blocks, 2 * feats))]
        out_shape += [
            jax.ShapeDtypeStruct(grad_shape, BF),
            jax.ShapeDtypeStruct((blocks, 2 * feats), dkv_type),
        ]
        scratch += [
            pltpu.VMEM((heads * blocks, feats), F32),
            pltpu.VMEM((heads * blocks, feats), F32),
            pltpu.VMEM((2, feats, width), F32),
        ]
        flops = flops + 4 * own * width * feats + 4 * own * heads * blocks * feats
    return pl.pallas_call(
        after(functools.partial(attend_kernel, n_sp, grad_factor), 3, len(deps)),
        grid=(own // tile,),
        in_specs=[rows, rows, fixed(weights.shape)] + [ANY] * len(deps),
        out_specs=out_specs,
        out_shape=out_shape,
        scratch_shapes=scratch,
        compiler_params=params(),
        cost_estimate=cost(2 * flops, 4 * own * width + 8 * width * feats),
        name="attend" if grad_factor is None else "attend_grads",
    )(normed, cotangent, weights, *deps)


def rows_kernel(count, pos_ref, *refs):
    attn_refs, refs = refs[:count], refs[count:]
    dq_refs, refs = refs[:count], refs[count:]
    w_refs, (own_ref, sib_ref, heads_ref) = refs[:count], refs[count:]
    h = pos_ref[2]
    sib = h + 1 - 2 * lax.rem(h, 2)
    cols = own_ref.shape[1]
    rows = [ref[...].T for ref in attn_refs]
    for ref, owner in ((own_ref, h), (sib_ref, sib)):
        lanes = pl.ds(pl.multiple_of(owner * cols, 128), cols)
        total = None
        for row, w_ref in zip(rows, w_refs):
            term = mm(row, w_ref[1, :, lanes]).astype(BF).astype(F32)
            total = term if total is None else total + term
        ref[...] = total.astype(BF)
    total = None
    for dq_ref, w_ref in zip(dq_refs, w_refs):
        term = mm(dq_ref[...].T, w_ref[0, :, : heads_ref.shape[1]]).astype(BF).astype(F32)
        total = term if total is None else total + term
    heads_ref[...] = total


def model_rows(pos, width, attns, dqs, weights, n_hd, deps):
    count = len(attns)
    feats = weights[0].shape[1]
    own = attns[0].shape[1]
    cols = width // n_hd
    tile = 256
    steps = own // tile
    whole = lambda shape: pl.BlockSpec(shape, lambda i, p: (0,) * len(shape))
    t_spec = pl.BlockSpec((feats, tile), lambda i, p: (0, i))
    return pl.pallas_call(
        after(functools.partial(rows_kernel, count), 3 * count + 1, len(deps)),
        grid_spec=pltpu.PrefetchScalarGridSpec(
            num_scalar_prefetch=1,
            grid=(steps,),
            in_specs=[t_spec] * (2 * count) + [whole(w.shape) for w in weights]
            + [ANY] * len(deps),
            out_specs=[
                pl.BlockSpec((tile, cols), lambda i, p: (p[1] * steps + i, 0)),
                pl.BlockSpec((tile, cols), lambda i, p: (i, 0)),
                pl.BlockSpec((tile, width), lambda i, p: (i, 0)),
            ],
        ),
        out_shape=[
            jax.ShapeDtypeStruct((2 * own, cols), BF),
            jax.ShapeDtypeStruct((own, cols), BF),
            jax.ShapeDtypeStruct((own, width), F32),
        ],
        compiler_params=params(),
        cost_estimate=cost(4 * own * width * (width + 2 * cols), 12 * own * width),
        name="model_rows",
    )(pos, *attns, *dqs, *weights, *deps)


def input_kernel(count, pos_ref, gain_ref, rgain_ref, tok_ref, runit_ref, rinv_ref, heads_ref, *refs):
    d_refs, (own_ref, sib_ref, spread, u_ref) = refs[:count], refs[count:]
    width = tok_ref.shape[1]
    h = pos_ref[2]
    sib = h + 1 - 2 * lax.rem(h, 2)
    cols = own_ref.shape[1]

    @pl.when(pl.program_id(0) == 0)
    def _():
        groups = runit_ref.shape[0]
        total = d_refs[0][...].astype(F32)
        for ref in d_refs[1:]:
            total = total + ref[...].astype(F32)
        e = total * rgain_ref[...]
        unit = runit_ref[...]
        first = jnp.mean(e, axis=-1, keepdims=True)
        second = jnp.mean(e * unit, axis=-1, keepdims=True)
        d_pooled = rinv_ref[:, 0:1] * (e - first - unit * second) / (POOL * POOL)
        spread[...] = jnp.broadcast_to(d_pooled[:, None, :], (groups, POOL, width)).reshape(
            groups * POOL, width
        )

    chunk = 2 * POOL
    for part in range(tok_ref.shape[0] // chunk):
        at = slice(part * chunk, (part + 1) * chunk)
        low = (part * chunk) % GRID_W
        v = tok_ref[at, :].astype(F32)
        d = v - jnp.mean(v, axis=-1, keepdims=True)
        inv = lax.rsqrt(jnp.mean(d * d, axis=-1, keepdims=True) + EPS)
        unit = d * inv
        e = (heads_ref[at, :] + spread[low : low + chunk, :]) * gain_ref[...]
        first = jnp.mean(e, axis=-1, keepdims=True)
        second = jnp.mean(e * unit, axis=-1, keepdims=True)
        u_ref[at, :] = inv * (e - first - unit * second)
    for ref, owner in ((own_ref, h), (sib_ref, sib)):
        ref[...] = u_ref[:, pl.ds(pl.multiple_of(owner * cols, 128), cols)].astype(BF)


def input_rows(pos, norm_gain, reduce_gain, tokens, unit, inverse, d_heads, parts, n_hd, deps):
    own, width = d_heads.shape
    cols = width // n_hd
    groups = parts[0].shape[0]
    tile = 256
    steps = own // tile
    whole = lambda shape: pl.BlockSpec(shape, lambda i, p: (0,) * len(shape))
    half = lambda shape: pl.BlockSpec(shape, lambda i, p: (p[1], 0))
    return pl.pallas_call(
        after(functools.partial(input_kernel, len(parts)), 7 + len(parts), len(deps)),
        grid_spec=pltpu.PrefetchScalarGridSpec(
            num_scalar_prefetch=1,
            grid=(steps,),
            in_specs=[
                whole((1, width)),
                whole((1, width)),
                pl.BlockSpec((tile, width), lambda i, p: (p[1] * steps + i, 0)),
                half((groups, width)),
                half((groups, 128)),
                pl.BlockSpec((tile, width), lambda i, p: (i, 0)),
            ]
            + [whole(part.shape) for part in parts]
            + [ANY] * len(deps),
            out_specs=[
                pl.BlockSpec((tile, cols), lambda i, p: (p[1] * steps + i, 0)),
                pl.BlockSpec((tile, cols), lambda i, p: (i, 0)),
            ],
            scratch_shapes=[
                pltpu.VMEM((groups * POOL, width), F32),
                pltpu.VMEM((tile, width), F32),
            ],
        ),
        out_shape=[
            jax.ShapeDtypeStruct((2 * own, cols), BF),
            jax.ShapeDtypeStruct((own, cols), BF),
        ],
        compiler_params=params(),
        cost_estimate=cost(40 * own * width, 16 * own * width),
        name="input_rows",
    )(
        pos,
        norm_gain.astype(F32).reshape(1, width),
        reduce_gain.astype(F32).reshape(1, width),
        tokens,
        unit,
        inverse,
        d_heads,
        *parts,
        *deps,
    )


def small(kernel, name, out_shape, *args, pos=None, deps=()):
    smem = [] if pos is None else [pl.BlockSpec(memory_space=pltpu.SMEM)]
    vmem = pl.BlockSpec(memory_space=pltpu.VMEM)
    many = isinstance(out_shape, list)
    return pl.pallas_call(
        after(kernel, len(smem) + len(args), len(deps)),
        in_specs=smem + [vmem] * len(args) + [ANY] * len(deps),
        out_specs=[vmem] * len(out_shape) if many else vmem,
        out_shape=out_shape,
        compiler_params=pltpu.CompilerParams(vmem_limit_bytes=VMEM_LIMIT),
        cost_estimate=cost(1 << 28, 1 << 21),
        name=name,
    )(*([] if pos is None else [pos]), *args, *deps)


def turn_kernel(pos_ref, q_ref, o_ref, out_ref, half_ref):
    q, o = q_ref[...].T, o_ref[...].T
    out_ref[0] = q
    out_ref[1] = o
    half_ref[...] = jnp.where(pos_ref[3] == 0, q, o)


def stack_kernel(own_ref, *refs):
    pieces, (far_ref, all_ref) = refs[:-2], refs[-2:]
    all_ref[0] = own_ref[...]
    for k, ref in enumerate(pieces):
        all_ref[k + 1] = ref[...]
        far_ref[k] = ref[...]


def choose(index, values):
    result = values[0]
    for k in range(1, len(values)):
        result = jnp.where(index == k, values[k], result)
    return result


def place_pieces(z, pieces, out_ref, which):
    n_sp, depth = len(pieces), pieces[0].shape[1]
    for place in range(n_sp):
        index = lax.rem(z - place + n_sp, n_sp)
        out_ref[which, :, place * depth : (place + 1) * depth] = choose(index, pieces)


def pack_kernel(n_sp, pos_ref, own_ref, here_ref, there_ref, part_ref, *refs):
    parts, (out_ref, kv_ref) = refs[:-2], refs[-2:]
    feats, depth = own_ref.shape[1:]
    rows = part_ref.shape[0]
    blocks, width = rows // n_sp, depth * n_sp
    z, y = pos_ref[0], pos_ref[3]
    for which in range(2):
        pieces = [own_ref[which]] + [
            jnp.where(y == which, here_ref[k], there_ref[k]) for k in range(n_sp - 1)
        ]
        place_pieces(z, pieces, out_ref, which)
        lanes = slice(which * feats, (which + 1) * feats)
        sums = []
        for j in range(n_sp):
            total = part_ref[j * blocks : (j + 1) * blocks, lanes]
            for k, part in enumerate(parts, 1):
                at = (j - k) % n_sp
                total = total + part[at * blocks : (at + 1) * blocks, lanes].astype(F32)
            sums.append(total)
        kv = jnp.concatenate(sums, axis=0).T.astype(BF)
        out_ref[which, :, width:] = kv
        kv_ref[which] = kv


def pack_far_kernel(pos_ref, here_ref, there_ref, kv_ref, out_ref):
    n_sp, feats, depth = here_ref.shape
    z, y = pos_ref[0], pos_ref[3]
    for which in range(2):
        pieces = [jnp.where(y == which, here_ref[k], there_ref[k]) for k in range(n_sp)]
        place_pieces(z, pieces, out_ref, which)
        out_ref[which, :, n_sp * depth :] = kv_ref[which]


def project_kernel(k_ref, v_ref, *refs):
    red, (cols_ref, part_ref, low_ref) = refs[:-3], refs[-3:]
    feats = k_ref.shape[1]
    rows = jnp.concatenate([ref[...] for ref in red], axis=0)
    cols_ref[...] = rows
    for which, ref in ((0, k_ref), (1, v_ref)):
        lanes = slice(which * feats, (which + 1) * feats)
        part = mm(rows, ref[...])
        part_ref[:, lanes] = part
        low_ref[:, lanes] = part.astype(BF)


def grad_add_kernel(n_sp, pos_ref, grad_ref, grad_far_ref, dkv_ref, dkv_far_ref, *refs):
    g_refs, d_refs = refs[:n_sp], refs[n_sp:]
    z = pos_ref[0]
    blocks = d_refs[0].shape[0]
    for k in range(n_sp):
        at = lax.rem(z + k, n_sp)
        total = grad_ref[at].astype(F32) + grad_far_ref[at].astype(F32)
        g_refs[k][...] = total.astype(g_refs[k].dtype)
        rows = pl.ds(((n_sp - k) % n_sp) * blocks, blocks)
        total = dkv_ref[rows, :] + dkv_far_ref[rows, :].astype(F32)
        d_refs[k][...] = total.astype(d_refs[k].dtype)


def back_kernel(n_sp, pos_ref, *refs):
    rows, weights = refs[:n_sp], refs[n_sp : 2 * n_sp]
    low_ref, mine_ref, other_ref, d_red = refs[-4:]
    blocks = rows[0].shape[0]
    depth, feats = weights[0].shape[1:]
    z, c = pos_ref[0], pos_ref[1]
    total = rows[0][...]
    for part in rows[1:]:
        total = total + part[...].astype(F32)
    low = total.astype(BF)
    low_ref[...] = low
    terms = [mm(low[:, :feats], w[0], NT) + mm(low[:, feats:], w[1], NT) for w in weights]
    for place in range(n_sp):
        index = lax.rem(z - place + n_sp, n_sp)
        d_red[:, place * depth : (place + 1) * depth] = choose(index, terms)
    half = blocks // 2
    mine_ref[...] = d_red[pl.ds(pl.multiple_of(c * half, half), half), :].astype(BF)
    other_ref[...] = d_red[pl.ds(pl.multiple_of((1 - c) * half, half), half), :].astype(BF)


def pair_kernel(k_ref, v_ref, out_ref):
    out_ref[0] = k_ref[...]
    out_ref[1] = v_ref[...]


def kv_grad_kernel(grad_factor, red_ref, *refs):
    rows, (key_ref, value_ref) = refs[:-2], refs[-2:]
    feats = key_ref.shape[1]
    d_kv = jnp.concatenate([ref[...] for ref in rows], axis=0)
    both = mm(red_ref[...].T, d_kv) * grad_factor
    key_ref[...] = both[:, :feats]
    value_ref[...] = both[:, feats:]


def grad_sum_kernel(*refs):
    query_ref, out_ref = refs[-2:]
    for which, ref in ((0, query_ref), (1, out_ref)):
        total = refs[0][which].astype(F32)
        for part in refs[1:-2]:
            total = total + part[which].astype(F32)
        ref[...] = total.T


def on_device(
    tokens,
    norm_gain,
    reduce_gain,
    query_weight,
    key_weight,
    value_weight,
    out_weight,
    out_cotangent,
):
    n_sp, n_hd = lax.axis_size("sp"), lax.axis_size("hd")
    n_x = n_hd // 2
    z, h, y = lax.axis_index("sp"), lax.axis_index("hd"), lax.axis_index("scene")
    c = h % 2
    depth, feats = query_weight.shape
    width = tokens.shape[1]
    own = tokens.shape[0] // 2
    grad_factor = float(2 * own * n_sp) ** (-0.5)
    pos = jnp.stack([z, c, h, y]).astype(jnp.int32)
    others = range(1, n_sp)

    def low(*shape):
        return jax.ShapeDtypeStruct(shape, BF)

    def wide(*shape):
        return jax.ShapeDtypeStruct(shape, F32)

    def to_sp(value, k):
        return lax.ppermute(value, "sp", [(i, (i + k) % n_sp) for i in range(n_sp)])

    def to_hd(value, k):
        return lax.ppermute(value, "hd", [(i, (i + k) % n_hd) for i in range(n_hd)])

    def swap(value):
        return lax.ppermute(value, "hd", [(i, i ^ 1) for i in range(n_hd)])

    def cross(value):
        return lax.ppermute(value, "scene", [(0, 1), (1, 0)])

    shard, half = small(
        turn_kernel,
        "turn",
        [low(2, feats, depth), low(feats, depth)],
        query_weight,
        out_weight,
        pos=pos,
    )
    here = [to_sp(half, k) for k in others]
    normed, cot, reduced, r_unit, r_inverse = norm_and_pool(
        pos, tokens, out_cotangent, norm_gain, reduce_gain, (half,)
    )
    blocks = reduced.shape[0]
    far3, all4 = small(
        stack_kernel,
        "stack",
        [low(n_sp - 1, feats, depth), low(n_sp, feats, depth)],
        half,
        *here,
        deps=(reduced,),
    )
    there3 = cross(far3)
    x_pieces = [to_hd(all4, 2 * k) for k in range(1, n_x)]

    red_cut = jnp.stack([reduced[:, i * depth : (i + 1) * depth] for i in range(n_sp)])
    cuts = [lax.dynamic_index_in_dim(red_cut, (z + k) % n_sp, 0, keepdims=False) for k in range(n_sp)]
    both = (blocks * n_sp, 2 * feats)
    reduced_cols, kv_part, kv_low = small(
        project_kernel,
        "project",
        [low(blocks * n_sp, depth), wide(*both), low(*both)],
        key_weight,
        value_weight,
        cuts[0],
        *[to_sp(cuts[k], k) for k in others],
        deps=(far3,),
    )
    packed, kv_own = small(
        functools.partial(pack_kernel, n_sp),
        "pack",
        [low(2, feats, width + blocks * n_sp), low(2, feats, blocks * n_sp)],
        shard,
        far3,
        there3,
        kv_part,
        *[to_sp(kv_low, k) for k in others],
        pos=pos,
    )

    kv_weight = small(
        pair_kernel,
        "pair",
        low(2, depth, feats),
        key_weight,
        value_weight,
        deps=(kv_low,),
    )
    kv_weights = [kv_weight] + [to_sp(kv_weight, k) for k in others]
    third = (n_sp + 1) // 3

    attn0, dq0, grad0, dkv0 = attend(n_sp, normed, cot, packed, (), grad_factor, F32)
    packed_sib = swap(packed)
    kv_far = [to_hd(kv_own, 2 * k) for k in range(1, n_x)]
    attn1, dq1, grad1, dkv1 = attend(
        n_sp,
        normed,
        cot,
        packed_sib,
        (attn0, *x_pieces, *kv_far, *kv_weights[1 : 1 + third]),
        grad_factor,
        BF,
    )
    attns, dqs, ws = [attn0, attn1], [dq0, dq1], [packed, packed_sib]
    grad1, dkv1 = swap(grad1), swap(dkv1)

    later = (attn1, *kv_weights[1 + third : 1 + 2 * third])
    for piece, kv in zip(x_pieces, kv_far):
        packed_far = small(
            pack_far_kernel, "pack_far", low(*packed.shape), piece, cross(piece), kv, pos=pos, deps=later
        )
        ws += [packed_far, swap(packed_far)]

    attn, dq = attend(n_sp, normed, cot, ws[2], ())
    attns.append(attn)
    dqs.append(dq)
    grads = small(
        functools.partial(grad_add_kernel, n_sp),
        "grad_add",
        [wide(2, feats, depth)]
        + [low(2, feats, depth)] * (n_sp - 1)
        + [wide(blocks, 2 * feats)]
        + [low(blocks, 2 * feats)] * (n_sp - 1),
        grad0,
        grad1,
        dkv0,
        dkv1,
        pos=pos,
        deps=(attn,),
    )
    grads, d_rows = grads[:n_sp], grads[n_sp:]
    grads = [grads[0]] + [to_sp(grads[k], k) for k in others]
    later = (d_rows[0], *kv_weights[1 + 2 * third :])
    for w in ws[3:]:
        attn, dq = attend(n_sp, normed, cot, w, later)
        attns.append(attn)
        dqs.append(dq)

    dkv_rows, d_mine, d_other = pl.pallas_call(
        after(functools.partial(back_kernel, n_sp), 1 + 2 * n_sp, 1),
        in_specs=[pl.BlockSpec(memory_space=pltpu.SMEM)]
        + [pl.BlockSpec(memory_space=pltpu.VMEM)] * (2 * n_sp)
        + [ANY],
        out_specs=[pl.BlockSpec(memory_space=pltpu.VMEM)] * 3,
        out_shape=[low(blocks, 2 * feats), low(blocks // 2, width), low(blocks // 2, width)],
        scratch_shapes=[pltpu.VMEM((blocks, width), F32)],
        compiler_params=pltpu.CompilerParams(vmem_limit_bytes=VMEM_LIMIT),
        cost_estimate=cost(1 << 28, 1 << 21),
        name="back",
    )(
        pos,
        d_rows[0],
        *[to_sp(d_rows[k], k) for k in others],
        *kv_weights,
        attns[-1],
    )
    parts = [d_mine] + [to_hd(d_other if k % 2 else d_mine, k) for k in range(1, n_hd)]
    dkv_all = [dkv_rows] + [to_sp(dkv_rows, k) for k in others]

    branch, other, d_heads = model_rows(
        pos, width, attns, dqs, ws, n_hd, (d_mine, *grads[1 : 1 + third])
    )
    place = (1 - c) * own
    branch = lax.dynamic_update_slice_in_dim(branch, swap(other), place, 0)
    input_grad, other = input_rows(
        pos,
        norm_gain,
        reduce_gain,
        tokens,
        r_unit,
        r_inverse,
        d_heads,
        parts,
        n_hd,
        tuple(grads[1 + third : 1 + 2 * third]),
    )
    input_grad = lax.dynamic_update_slice_in_dim(input_grad, swap(other), place, 0)
    query_grad, out_grad = small(
        grad_sum_kernel, "grad_sum", [wide(depth, feats)] * 2, *grads, deps=(other,)
    )
    key_grad, value_grad = small(
        functools.partial(kv_grad_kernel, grad_factor),
        "kv_grad",
        [wide(depth, feats)] * 2,
        reduced_cols,
        *dkv_all,
        deps=(other,),
    )
    return (branch, input_grad, query_grad, key_grad, value_grad, out_grad)


def solution(mesh):
    rows, whole, both = P(("scene", "sp"), None), P(), P("sp", "hd")
    out = P(("scene", "sp"), "hd")
    return jax.shard_map(
        on_device,
        mesh=mesh,
        in_specs=(rows, whole, whole, both, both, both, both, rows),
        out_specs=(out,) * 6,
        check_vma=False,
    )
```

```python
import functools
import jax
import jax.numpy as jnp
from jax import lax
from jax.experimental import pallas as pl
from jax.experimental.pallas import tpu as pltpu
from jax.sharding import PartitionSpec as P

HEAD_DIM = 64
POOL = 8
GRID_W = 128
EPS = 1e-06
BF = jnp.bfloat16
F32 = jnp.float32
VMEM_LIMIT = 24 * 1024 * 1024
NORM_LIMIT = 57 * 1024 * 1024

NN = (((1,), (0,)), ((), ()))
TN = (((0,), (0,)), ((), ()))
NT = (((1,), (1,)), ((), ()))


def mm(left, right, dims=NN):
    return lax.dot_general(left, right, dims, preferred_element_type=F32)


def cost(flops, moved):
    return pl.CostEstimate(flops=int(flops), bytes_accessed=int(moved), transcendentals=0)


ANY = pl.BlockSpec(memory_space=pl.ANY)


def after(kernel, inputs, deps):
    return lambda *refs: kernel(*refs[:inputs], *refs[inputs + deps :])


def params(axes=1, limit=VMEM_LIMIT):
    return pltpu.CompilerParams(
        dimension_semantics=("arbitrary",) * axes, vmem_limit_bytes=limit
    )


def norm_kernel(pos_ref, gain_ref, rgain_ref, tok_ref, cot_ref, normed_ref, cot_out_ref, red_ref,
                runit_ref, rinv_ref, pooled):
    step, col = pl.program_id(0), pl.program_id(1)
    half = pl.num_programs(0) // 2
    row = lax.rem(step + (1 - pos_ref[1]) * half, 2 * half)
    cols, width = tok_ref.shape[1], tok_ref.shape[2]
    gain = gain_ref[...].astype(F32).reshape(1, width)
    chunk = 2 * POOL
    sums = []
    for part in range(cols // chunk):
        acc = jnp.zeros((chunk, width), F32)
        for r in range(POOL):
            v = tok_ref[r, part * chunk : (part + 1) * chunk, :].astype(F32)
            d = v - jnp.mean(v, axis=-1, keepdims=True)
            inv = lax.rsqrt(jnp.mean(d * d, axis=-1, keepdims=True) + EPS)
            n = (d * inv * gain).astype(BF)
            normed_ref[r, part * chunk : (part + 1) * chunk, :] = n
            acc = acc + n.astype(F32)
        sums.append(jnp.sum(acc.reshape(2, POOL, width), axis=1))
    span = cols // POOL
    base = pl.multiple_of((row * pl.num_programs(1) + col) * span, span)
    pooled[pl.ds(base, span), :] = jnp.concatenate(sums, axis=0)

    @pl.when(step >= half)
    def _():
        cot_out_ref[...] = cot_ref[...]

    @pl.when((step == pl.num_programs(0) - 1) & (col == pl.num_programs(1) - 1))
    def _():
        v = pooled[...] / (POOL * POOL)
        d = v - jnp.mean(v, axis=-1, keepdims=True)
        inv = lax.rsqrt(jnp.mean(d * d, axis=-1, keepdims=True) + EPS)
        unit = d * inv
        runit_ref[...] = unit
        rinv_ref[...] = jnp.broadcast_to(inv, rinv_ref.shape)
        red_ref[...] = (unit * rgain_ref[...].astype(F32).reshape(1, width)).astype(BF)


def norm_and_pool(pos, tokens, cotangent, norm_gain, reduce_gain, deps):
    count, width = tokens.shape
    grid_rows = count // GRID_W
    blocks = count // (POOL * POOL)
    cols = 64
    rows = grid_rows // POOL
    half = rows // 2
    block = (POOL, cols, width)

    def own(i):
        return jnp.maximum(i - half, 0)

    def own_col(i, j):
        return jnp.where(i >= half, j, 0)

    tok = pl.BlockSpec(block, lambda i, j, p: (lax.rem(i + (1 - p[1]) * half, rows), j, 0))
    cot = pl.BlockSpec(block, lambda i, j, p: (p[1] * half + own(i), own_col(i, j), 0))
    out = pl.BlockSpec(block, lambda i, j, p: (own(i), own_col(i, j), 0))
    whole = lambda shape: pl.BlockSpec(shape, lambda i, j, p: (0,) * len(shape))
    normed, cot_own, reduced, unit, inverse = pl.pallas_call(
        after(norm_kernel, 5, len(deps)),
        grid_spec=pltpu.PrefetchScalarGridSpec(
            num_scalar_prefetch=1,
            grid=(rows, GRID_W // cols),
            in_specs=[whole((width,)), whole((width,)), tok, cot]
            + [ANY] * len(deps),
            out_specs=[
                out,
                out,
                whole((blocks, width)),
                whole((blocks, width)),
                whole((blocks, 128)),
            ],
            scratch_shapes=[pltpu.VMEM((blocks, width), F32)],
        ),
        out_shape=[
            jax.ShapeDtypeStruct((grid_rows // 2, GRID_W, width), BF),
            jax.ShapeDtypeStruct((grid_rows // 2, GRID_W, width), BF),
            jax.ShapeDtypeStruct((blocks, width), BF),
            jax.ShapeDtypeStruct((blocks, width), F32),
            jax.ShapeDtypeStruct((blocks, 128), F32),
        ],
        compiler_params=params(2, NORM_LIMIT),
        cost_estimate=cost(40 * count * width, 10 * count * width),
        name="norm_pool",
    )(
        pos,
        norm_gain,
        reduce_gain,
        tokens.reshape(grid_rows, GRID_W, width),
        cotangent.reshape(grid_rows, GRID_W, width),
        *deps,
    )
    return (
        normed.reshape(count // 2, width),
        cot_own.reshape(count // 2, width),
        reduced,
        unit,
        inverse,
    )


def spread_heads(w_ref, width, kbd, vbd, kbd_t, vbd_t):
    feats, blocks = w_ref.shape[1], w_ref.shape[2] - width
    row = lax.broadcasted_iota(jnp.int32, (feats, blocks), 0)
    k = w_ref[0, :, width:].astype(F32) * HEAD_DIM ** (-0.5)
    v = w_ref[1, :, width:].astype(F32)
    for head in range(feats // HEAD_DIM):
        mask = (row >= head * HEAD_DIM) & (row < (head + 1) * HEAD_DIM)
        lanes = slice(head * blocks, (head + 1) * blocks)
        kbd_t[:, lanes] = jnp.where(mask, k, 0.0).astype(BF)
        vbd_t[:, lanes] = jnp.where(mask, v, 0.0).astype(BF)
    kbd[...] = kbd_t[...].T
    vbd[...] = vbd_t[...].T


def attend_tile(x, y, w_ref, kbd, vbd, kbd_t, vbd_t):
    feats = w_ref.shape[1]
    heads = feats // HEAD_DIM
    blocks = kbd.shape[0] // heads
    q_t = mm(w_ref[0, :, : x.shape[1]], x, NT).astype(BF)
    da_t = mm(w_ref[1, :, : y.shape[1]], y, NT).astype(BF)
    scores = mm(kbd[...], q_t)
    d_chances = mm(vbd[...], da_t)
    low, d_low = [], []
    for head in range(heads):
        rows = slice(head * blocks, (head + 1) * blocks)
        s = scores[rows]
        e = jnp.exp(s - jnp.max(s, axis=0, keepdims=True))
        p = e * (1.0 / jnp.sum(e, axis=0, keepdims=True))
        dp = d_chances[rows]
        delta = jnp.sum(p * dp, axis=0, keepdims=True)
        low.append(p.astype(BF))
        d_low.append((p * (dp - delta)).astype(BF))
    low = jnp.concatenate(low, axis=0)
    d_low = jnp.concatenate(d_low, axis=0)
    attn_t = mm(vbd_t[...], low).astype(BF)
    dq_t = mm(kbd_t[...], d_low).astype(BF)
    return q_t, da_t, low, d_low, attn_t, dq_t


def head_mask(shape, head):
    lane = lax.broadcasted_iota(jnp.int32, shape, 1)
    return (lane >= head * HEAD_DIM) & (lane < (head + 1) * HEAD_DIM)


def head_scratch(heads, blocks, feats):
    return [
        pltpu.VMEM((heads * blocks, feats), BF),
        pltpu.VMEM((heads * blocks, feats), BF),
        pltpu.VMEM((feats, heads * blocks), BF),
        pltpu.VMEM((feats, heads * blocks), BF),
    ]


def attend_kernel(n_sp, grad_factor, x_ref, y_ref, w_ref, attn_ref, dq_ref, *rest):
    step = pl.program_id(0)
    feats, width = w_ref.shape[1], x_ref.shape[1]
    blocks = w_ref.shape[2] - width
    depth = width // n_sp
    heads_at = rest[-4:] if len(rest) == 4 else rest[2:6]
    if len(rest) > 4:
        grad_ref, dkv_ref = rest[:2]
        dk_acc, dv_acc, g_acc = rest[6:]

    @pl.when(step == 0)
    def _():
        spread_heads(w_ref, width, *heads_at)
        if len(rest) > 4:
            dk_acc[...] = jnp.zeros_like(dk_acc)
            dv_acc[...] = jnp.zeros_like(dv_acc)
            g_acc[...] = jnp.zeros_like(g_acc)

    x, y = x_ref[...], y_ref[...]
    q_t, da_t, low, d_low, attn_t, dq_t = attend_tile(x, y, w_ref, *heads_at)
    attn_ref[...] = attn_t
    dq_ref[...] = dq_t
    if len(rest) == 4:
        return
    dk_acc[...] += mm(d_low, q_t, NT)
    dv_acc[...] += mm(low, da_t, NT)
    g_acc[0] += mm(dq_t, x)
    g_acc[1] += mm(attn_t, y)

    @pl.when(step == pl.num_programs(0) - 1)
    def _():
        dk = jnp.zeros((blocks, feats), F32)
        dv = jnp.zeros((blocks, feats), F32)
        for head in range(feats // HEAD_DIM):
            mask = head_mask((blocks, feats), head)
            rows = slice(head * blocks, (head + 1) * blocks)
            dk = dk + jnp.where(mask, dk_acc[rows, :], 0.0)
            dv = dv + jnp.where(mask, dv_acc[rows, :], 0.0)
        dkv_ref[:, :feats] = (dk * HEAD_DIM ** (-0.5)).astype(dkv_ref.dtype)
        dkv_ref[:, feats:] = dv.astype(dkv_ref.dtype)
        for place in range(n_sp):
            cols = slice(place * depth, (place + 1) * depth)
            grad_ref[place] = (g_acc[:, :, cols] * grad_factor).astype(BF)


def fixed(shape):
    return pl.BlockSpec(shape, lambda i: (0,) * len(shape))


def attend(n_sp, normed, cotangent, weights, deps, grad_factor=None, dkv_type=BF):
    feats = weights.shape[1]
    own, width = normed.shape
    blocks = weights.shape[2] - width
    heads = feats // HEAD_DIM
    tile = 256
    rows = pl.BlockSpec((tile, width), lambda i: (i, 0))
    t_spec = pl.BlockSpec((feats, tile), lambda i: (0, i))
    out_specs = [t_spec, t_spec]
    out_shape = [jax.ShapeDtypeStruct((feats, own), BF)] * 2
    scratch = head_scratch(heads, blocks, feats)
    flops = 4 * own * width * feats + 8 * own * heads * blocks * feats
    if grad_factor is not None:
        grad_shape = (n_sp, 2, feats, width // n_sp)
        out_specs += [fixed(grad_shape), fixed((blocks, 2 * feats))]
        out_shape += [
            jax.ShapeDtypeStruct(grad_shape, BF),
            jax.ShapeDtypeStruct((blocks, 2 * feats), dkv_type),
        ]
        scratch += [
            pltpu.VMEM((heads * blocks, feats), F32),
            pltpu.VMEM((heads * blocks, feats), F32),
            pltpu.VMEM((2, feats, width), F32),
        ]
        flops = flops + 4 * own * width * feats + 4 * own * heads * blocks * feats
    return pl.pallas_call(
        after(functools.partial(attend_kernel, n_sp, grad_factor), 3, len(deps)),
        grid=(own // tile,),
        in_specs=[rows, rows, fixed(weights.shape)] + [ANY] * len(deps),
        out_specs=out_specs,
        out_shape=out_shape,
        scratch_shapes=scratch,
        compiler_params=params(),
        cost_estimate=cost(2 * flops, 4 * own * width + 8 * width * feats),
        name="attend" if grad_factor is None else "attend_grads",
    )(normed, cotangent, weights, *deps)


def rows_kernel(count, pos_ref, *refs):
    attn_refs, refs = refs[:count], refs[count:]
    dq_refs, refs = refs[:count], refs[count:]
    w_refs, (own_ref, sib_ref, heads_ref) = refs[:count], refs[count:]
    h = pos_ref[2]
    sib = h + 1 - 2 * lax.rem(h, 2)
    cols = own_ref.shape[1]
    rows = [ref[...].T for ref in attn_refs]
    for ref, owner in ((own_ref, h), (sib_ref, sib)):
        lanes = pl.ds(pl.multiple_of(owner * cols, 128), cols)
        total = None
        for row, w_ref in zip(rows, w_refs):
            term = mm(row, w_ref[1, :, lanes]).astype(BF).astype(F32)
            total = term if total is None else total + term
        ref[...] = total.astype(BF)
    total = None
    for dq_ref, w_ref in zip(dq_refs, w_refs):
        term = mm(dq_ref[...].T, w_ref[0, :, : heads_ref.shape[1]]).astype(BF).astype(F32)
        total = term if total is None else total + term
    heads_ref[...] = total


def model_rows(pos, width, attns, dqs, weights, n_hd, deps):
    count = len(attns)
    feats = weights[0].shape[1]
    own = attns[0].shape[1]
    cols = width // n_hd
    tile = 256
    steps = own // tile
    whole = lambda shape: pl.BlockSpec(shape, lambda i, p: (0,) * len(shape))
    t_spec = pl.BlockSpec((feats, tile), lambda i, p: (0, i))
    return pl.pallas_call(
        after(functools.partial(rows_kernel, count), 3 * count + 1, len(deps)),
        grid_spec=pltpu.PrefetchScalarGridSpec(
            num_scalar_prefetch=1,
            grid=(steps,),
            in_specs=[t_spec] * (2 * count) + [whole(w.shape) for w in weights]
            + [ANY] * len(deps),
            out_specs=[
                pl.BlockSpec((tile, cols), lambda i, p: (p[1] * steps + i, 0)),
                pl.BlockSpec((tile, cols), lambda i, p: (i, 0)),
                pl.BlockSpec((tile, width), lambda i, p: (i, 0)),
            ],
        ),
        out_shape=[
            jax.ShapeDtypeStruct((2 * own, cols), BF),
            jax.ShapeDtypeStruct((own, cols), BF),
            jax.ShapeDtypeStruct((own, width), F32),
        ],
        compiler_params=params(),
        cost_estimate=cost(4 * own * width * (width + 2 * cols), 12 * own * width),
        name="model_rows",
    )(pos, *attns, *dqs, *weights, *deps)


def input_kernel(count, pos_ref, gain_ref, rgain_ref, tok_ref, runit_ref, rinv_ref, heads_ref, *refs):
    d_refs, (own_ref, sib_ref, spread, u_ref) = refs[:count], refs[count:]
    width = tok_ref.shape[1]
    h = pos_ref[2]
    sib = h + 1 - 2 * lax.rem(h, 2)
    cols = own_ref.shape[1]

    @pl.when(pl.program_id(0) == 0)
    def _():
        groups = runit_ref.shape[0]
        total = d_refs[0][...].astype(F32)
        for ref in d_refs[1:]:
            total = total + ref[...].astype(F32)
        e = total * rgain_ref[...].astype(F32).reshape(1, width)
        unit = runit_ref[...]
        first = jnp.mean(e, axis=-1, keepdims=True)
        second = jnp.mean(e * unit, axis=-1, keepdims=True)
        d_pooled = rinv_ref[:, 0:1] * (e - first - unit * second) / (POOL * POOL)
        spread[...] = jnp.broadcast_to(d_pooled[:, None, :], (groups, POOL, width)).reshape(
            groups * POOL, width
        )

    gain = gain_ref[...].astype(F32).reshape(1, width)
    chunk = 2 * POOL
    for part in range(tok_ref.shape[0] // chunk):
        at = slice(part * chunk, (part + 1) * chunk)
        low = (part * chunk) % GRID_W
        v = tok_ref[at, :].astype(F32)
        d = v - jnp.mean(v, axis=-1, keepdims=True)
        inv = lax.rsqrt(jnp.mean(d * d, axis=-1, keepdims=True) + EPS)
        unit = d * inv
        e = (heads_ref[at, :] + spread[low : low + chunk, :]) * gain
        first = jnp.mean(e, axis=-1, keepdims=True)
        second = jnp.mean(e * unit, axis=-1, keepdims=True)
        u_ref[at, :] = inv * (e - first - unit * second)
    for ref, owner in ((own_ref, h), (sib_ref, sib)):
        ref[...] = u_ref[:, pl.ds(pl.multiple_of(owner * cols, 128), cols)].astype(BF)


def input_rows(pos, norm_gain, reduce_gain, tokens, unit, inverse, d_heads, parts, n_hd, deps):
    own, width = d_heads.shape
    cols = width // n_hd
    groups = parts[0].shape[0]
    tile = 256
    steps = own // tile
    whole = lambda shape: pl.BlockSpec(shape, lambda i, p: (0,) * len(shape))
    half = lambda shape: pl.BlockSpec(shape, lambda i, p: (p[1], 0))
    return pl.pallas_call(
        after(functools.partial(input_kernel, len(parts)), 7 + len(parts), len(deps)),
        grid_spec=pltpu.PrefetchScalarGridSpec(
            num_scalar_prefetch=1,
            grid=(steps,),
            in_specs=[
                whole((width,)),
                whole((width,)),
                pl.BlockSpec((tile, width), lambda i, p: (p[1] * steps + i, 0)),
                half((groups, width)),
                half((groups, 128)),
                pl.BlockSpec((tile, width), lambda i, p: (i, 0)),
            ]
            + [whole(part.shape) for part in parts]
            + [ANY] * len(deps),
            out_specs=[
                pl.BlockSpec((tile, cols), lambda i, p: (p[1] * steps + i, 0)),
                pl.BlockSpec((tile, cols), lambda i, p: (i, 0)),
            ],
            scratch_shapes=[
                pltpu.VMEM((groups * POOL, width), F32),
                pltpu.VMEM((tile, width), F32),
            ],
        ),
        out_shape=[
            jax.ShapeDtypeStruct((2 * own, cols), BF),
            jax.ShapeDtypeStruct((own, cols), BF),
        ],
        compiler_params=params(),
        cost_estimate=cost(40 * own * width, 16 * own * width),
        name="input_rows",
    )(
        pos,
        norm_gain,
        reduce_gain,
        tokens,
        unit,
        inverse,
        d_heads,
        *parts,
        *deps,
    )


def small(kernel, name, out_shape, *args, pos=None, deps=()):
    smem = [] if pos is None else [pl.BlockSpec(memory_space=pltpu.SMEM)]
    vmem = pl.BlockSpec(memory_space=pltpu.VMEM)
    many = isinstance(out_shape, list)
    return pl.pallas_call(
        after(kernel, len(smem) + len(args), len(deps)),
        in_specs=smem + [vmem] * len(args) + [ANY] * len(deps),
        out_specs=[vmem] * len(out_shape) if many else vmem,
        out_shape=out_shape,
        compiler_params=pltpu.CompilerParams(vmem_limit_bytes=VMEM_LIMIT),
        cost_estimate=cost(1 << 28, 1 << 21),
        name=name,
    )(*([] if pos is None else [pos]), *args, *deps)


def turn_kernel(pos_ref, q_ref, o_ref, out_ref, half_ref):
    q, o = q_ref[...].T, o_ref[...].T
    out_ref[0] = q
    out_ref[1] = o
    half_ref[...] = jnp.where(pos_ref[3] == 0, q, o)


def stack_kernel(own_ref, *refs):
    pieces, (far_ref, all_ref) = refs[:-2], refs[-2:]
    all_ref[0] = own_ref[...]
    for k, ref in enumerate(pieces):
        all_ref[k + 1] = ref[...]
        far_ref[k] = ref[...]


def choose(index, values):
    result = values[0]
    for k in range(1, len(values)):
        result = jnp.where(index == k, values[k], result)
    return result


def place_pieces(z, pieces, out_ref, which):
    n_sp, depth = len(pieces), pieces[0].shape[1]
    for place in range(n_sp):
        index = lax.rem(z - place + n_sp, n_sp)
        out_ref[which, :, place * depth : (place + 1) * depth] = choose(index, pieces)


def pack_kernel(n_sp, pos_ref, own_ref, here_ref, there_ref, part_ref, *refs):
    parts, (out_ref, kv_ref) = refs[:-2], refs[-2:]
    feats, depth = own_ref.shape[1:]
    rows = part_ref.shape[0]
    blocks, width = rows // n_sp, depth * n_sp
    z, y = pos_ref[0], pos_ref[3]
    for which in range(2):
        pieces = [own_ref[which]] + [
            jnp.where(y == which, here_ref[k], there_ref[k]) for k in range(n_sp - 1)
        ]
        place_pieces(z, pieces, out_ref, which)
        lanes = slice(which * feats, (which + 1) * feats)
        sums = []
        for j in range(n_sp):
            total = part_ref[j * blocks : (j + 1) * blocks, lanes]
            for k, part in enumerate(parts, 1):
                at = (j - k) % n_sp
                total = total + part[at * blocks : (at + 1) * blocks, lanes].astype(F32)
            sums.append(total)
        kv = jnp.concatenate(sums, axis=0).T.astype(BF)
        out_ref[which, :, width:] = kv
        kv_ref[which] = kv


def pack_far_kernel(pos_ref, here_ref, there_ref, kv_ref, out_ref):
    n_sp, feats, depth = here_ref.shape
    z, y = pos_ref[0], pos_ref[3]
    for which in range(2):
        pieces = [jnp.where(y == which, here_ref[k], there_ref[k]) for k in range(n_sp)]
        place_pieces(z, pieces, out_ref, which)
        out_ref[which, :, n_sp * depth :] = kv_ref[which]


def project_kernel(k_ref, v_ref, *refs):
    red, (cols_ref, part_ref, low_ref) = refs[:-3], refs[-3:]
    feats = k_ref.shape[1]
    rows = jnp.concatenate([ref[...] for ref in red], axis=0)
    cols_ref[...] = rows
    for which, ref in ((0, k_ref), (1, v_ref)):
        lanes = slice(which * feats, (which + 1) * feats)
        part = mm(rows, ref[...])
        part_ref[:, lanes] = part
        low_ref[:, lanes] = part.astype(BF)


def grad_add_kernel(n_sp, pos_ref, grad_ref, grad_far_ref, dkv_ref, dkv_far_ref, *refs):
    g_refs, d_refs = refs[:n_sp], refs[n_sp:]
    z = pos_ref[0]
    blocks = d_refs[0].shape[0]
    for k in range(n_sp):
        at = lax.rem(z + k, n_sp)
        total = grad_ref[at].astype(F32) + grad_far_ref[at].astype(F32)
        g_refs[k][...] = total.astype(g_refs[k].dtype)
        rows = pl.ds(((n_sp - k) % n_sp) * blocks, blocks)
        total = dkv_ref[rows, :] + dkv_far_ref[rows, :].astype(F32)
        d_refs[k][...] = total.astype(d_refs[k].dtype)


def back_kernel(n_sp, pos_ref, *refs):
    rows, weights = refs[:n_sp], refs[n_sp : 2 * n_sp]
    low_ref, mine_ref, other_ref, d_red = refs[-4:]
    blocks = rows[0].shape[0]
    depth, feats = weights[0].shape[1:]
    z, c = pos_ref[0], pos_ref[1]
    total = rows[0][...]
    for part in rows[1:]:
        total = total + part[...].astype(F32)
    low = total.astype(BF)
    low_ref[...] = low
    terms = [mm(low[:, :feats], w[0], NT) + mm(low[:, feats:], w[1], NT) for w in weights]
    for place in range(n_sp):
        index = lax.rem(z - place + n_sp, n_sp)
        d_red[:, place * depth : (place + 1) * depth] = choose(index, terms)
    half = blocks // 2
    mine_ref[...] = d_red[pl.ds(pl.multiple_of(c * half, half), half), :].astype(BF)
    other_ref[...] = d_red[pl.ds(pl.multiple_of((1 - c) * half, half), half), :].astype(BF)


def pair_kernel(k_ref, v_ref, out_ref):
    out_ref[0] = k_ref[...]
    out_ref[1] = v_ref[...]


def kv_grad_kernel(grad_factor, red_ref, *refs):
    rows, (key_ref, value_ref) = refs[:-2], refs[-2:]
    feats = key_ref.shape[1]
    d_kv = jnp.concatenate([ref[...] for ref in rows], axis=0)
    both = mm(red_ref[...].T, d_kv) * grad_factor
    key_ref[...] = both[:, :feats]
    value_ref[...] = both[:, feats:]


def grad_sum_kernel(*refs):
    query_ref, out_ref = refs[-2:]
    for which, ref in ((0, query_ref), (1, out_ref)):
        total = refs[0][which].astype(F32)
        for part in refs[1:-2]:
            total = total + part[which].astype(F32)
        ref[...] = total.T


def on_device(
    tokens,
    norm_gain,
    reduce_gain,
    query_weight,
    key_weight,
    value_weight,
    out_weight,
    out_cotangent,
):
    n_sp, n_hd = lax.axis_size("sp"), lax.axis_size("hd")
    n_x = n_hd // 2
    z, h, y = lax.axis_index("sp"), lax.axis_index("hd"), lax.axis_index("scene")
    c = h % 2
    depth, feats = query_weight.shape
    width = tokens.shape[1]
    own = tokens.shape[0] // 2
    grad_factor = float(2 * own * n_sp) ** (-0.5)
    pos = jnp.stack([z, c, h, y]).astype(jnp.int32)
    others = range(1, n_sp)

    def low(*shape):
        return jax.ShapeDtypeStruct(shape, BF)

    def wide(*shape):
        return jax.ShapeDtypeStruct(shape, F32)

    def to_sp(value, k):
        return lax.ppermute(value, "sp", [(i, (i + k) % n_sp) for i in range(n_sp)])

    def to_hd(value, k):
        return lax.ppermute(value, "hd", [(i, (i + k) % n_hd) for i in range(n_hd)])

    def swap(value):
        return lax.ppermute(value, "hd", [(i, i ^ 1) for i in range(n_hd)])

    def cross(value):
        return lax.ppermute(value, "scene", [(0, 1), (1, 0)])

    block = pl.BlockSpec((depth, feats), lambda i, p: (0, 0))
    shard, half = pl.pallas_call(
        turn_kernel,
        grid_spec=pltpu.PrefetchScalarGridSpec(
            num_scalar_prefetch=1,
            grid=(1,),
            in_specs=[block, block],
            out_specs=[
                pl.BlockSpec((2, feats, depth), lambda i, p: (0, 0, 0)),
                pl.BlockSpec((feats, depth), lambda i, p: (0, 0)),
            ],
        ),
        out_shape=[low(2, feats, depth), low(feats, depth)],
        compiler_params=params(1, NORM_LIMIT),
        name="turn",
    )(pos, query_weight, out_weight)
    here = [to_sp(half, k) for k in others]
    normed, cot, reduced, r_unit, r_inverse = norm_and_pool(
        pos, tokens, out_cotangent, norm_gain, reduce_gain, (half,)
    )
    blocks = reduced.shape[0]
    far3, all4 = small(
        stack_kernel,
        "stack",
        [low(n_sp - 1, feats, depth), low(n_sp, feats, depth)],
        half,
        *here,
        deps=(reduced,),
    )
    there3 = cross(far3)
    x_pieces = [to_hd(all4, 2 * k) for k in range(1, n_x)]

    red_cut = jnp.stack([reduced[:, i * depth : (i + 1) * depth] for i in range(n_sp)])
    cuts = [lax.dynamic_index_in_dim(red_cut, (z + k) % n_sp, 0, keepdims=False) for k in range(n_sp)]
    both = (blocks * n_sp, 2 * feats)
    reduced_cols, kv_part, kv_low = small(
        project_kernel,
        "project",
        [low(blocks * n_sp, depth), wide(*both), low(*both)],
        key_weight,
        value_weight,
        cuts[0],
        *[to_sp(cuts[k], k) for k in others],
        deps=(far3,),
    )
    packed, kv_own = small(
        functools.partial(pack_kernel, n_sp),
        "pack",
        [low(2, feats, width + blocks * n_sp), low(2, feats, blocks * n_sp)],
        shard,
        far3,
        there3,
        kv_part,
        *[to_sp(kv_low, k) for k in others],
        pos=pos,
        deps=tuple(x_pieces),
    )

    kv_weight = small(
        pair_kernel,
        "pair",
        low(2, depth, feats),
        key_weight,
        value_weight,
        deps=(packed,),
    )
    kv_weights = [kv_weight] + [to_sp(kv_weight, k) for k in others]
    third = (n_sp + 1) // 3

    attn0, dq0, grad0, dkv0 = attend(n_sp, normed, cot, packed, (kv_weight,), grad_factor, F32)
    packed_sib = swap(packed)
    kv_far = [to_hd(kv_own, 2 * k) for k in range(1, n_x)]
    attn1, dq1, grad1, dkv1 = attend(
        n_sp,
        normed,
        cot,
        packed_sib,
        (attn0, *kv_weights[1 : 1 + third]),
        grad_factor,
        BF,
    )
    attns, dqs, ws = [attn0, attn1], [dq0, dq1], [packed, packed_sib]
    grad1, dkv1 = swap(grad1), swap(dkv1)

    later = (attn1, *kv_weights[1 + third : 1 + 2 * third])
    for piece, kv in zip(x_pieces, kv_far):
        packed_far = small(
            pack_far_kernel, "pack_far", low(*packed.shape), piece, cross(piece), kv, pos=pos, deps=later
        )
        ws += [packed_far, swap(packed_far)]

    attn, dq = attend(n_sp, normed, cot, ws[2], ())
    attns.append(attn)
    dqs.append(dq)
    grads = small(
        functools.partial(grad_add_kernel, n_sp),
        "grad_add",
        [wide(2, feats, depth)]
        + [low(2, feats, depth)] * (n_sp - 1)
        + [wide(blocks, 2 * feats)]
        + [low(blocks, 2 * feats)] * (n_sp - 1),
        grad0,
        grad1,
        dkv0,
        dkv1,
        pos=pos,
        deps=(attn,),
    )
    grads, d_rows = grads[:n_sp], grads[n_sp:]
    grads = [grads[0]] + [to_sp(grads[k], k) for k in others]
    ranked = sorted(others, key=lambda k: -min(k, n_sp - k))
    first = [grads[k] for k in ranked[: 2 * third]]
    last = [grads[k] for k in ranked[2 * third :]]
    later = (d_rows[0], *kv_weights[1 + 2 * third :])
    for w in ws[3:]:
        attn, dq = attend(n_sp, normed, cot, w, later)
        attns.append(attn)
        dqs.append(dq)

    dkv_rows, d_mine, d_other = pl.pallas_call(
        after(functools.partial(back_kernel, n_sp), 1 + 2 * n_sp, 1),
        in_specs=[pl.BlockSpec(memory_space=pltpu.SMEM)]
        + [pl.BlockSpec(memory_space=pltpu.VMEM)] * (2 * n_sp)
        + [ANY],
        out_specs=[pl.BlockSpec(memory_space=pltpu.VMEM)] * 3,
        out_shape=[low(blocks, 2 * feats), low(blocks // 2, width), low(blocks // 2, width)],
        scratch_shapes=[pltpu.VMEM((blocks, width), F32)],
        compiler_params=pltpu.CompilerParams(vmem_limit_bytes=VMEM_LIMIT),
        cost_estimate=cost(1 << 28, 1 << 21),
        name="back",
    )(
        pos,
        d_rows[0],
        *[to_sp(d_rows[k], k) for k in others],
        *kv_weights,
        attns[-1],
    )
    parts = [d_mine] + [to_hd(d_other if k % 2 else d_mine, k) for k in range(1, n_hd)]
    dkv_all = [dkv_rows] + [to_sp(dkv_rows, k) for k in others]

    branch, other, d_heads = model_rows(
        pos, width, attns, dqs, ws, n_hd, (d_mine, *first)
    )
    key_grad, value_grad = small(
        functools.partial(kv_grad_kernel, grad_factor),
        "kv_grad",
        [wide(depth, feats)] * 2,
        reduced_cols,
        *dkv_all,
        deps=(d_heads,),
    )
    place = (1 - c) * own
    branch = lax.dynamic_update_slice_in_dim(branch, swap(other), place, 0)
    input_grad, other = input_rows(
        pos,
        norm_gain,
        reduce_gain,
        tokens,
        r_unit,
        r_inverse,
        d_heads,
        parts,
        n_hd,
        (key_grad, *last),
    )
    input_grad = lax.dynamic_update_slice_in_dim(input_grad, swap(other), place, 0)
    query_grad, out_grad = small(
        grad_sum_kernel, "grad_sum", [wide(depth, feats)] * 2, *grads, deps=(other,)
    )
    return (branch, input_grad, query_grad, key_grad, value_grad, out_grad)


def solution(mesh):
    rows, whole, both = P(("scene", "sp"), None), P(), P("sp", "hd")
    out = P(("scene", "sp"), "hd")
    return jax.shard_map(
        on_device,
        mesh=mesh,
        in_specs=(rows, whole, whole, both, both, both, both, rows),
        out_specs=(out,) * 6,
        check_vma=False,
    )
```

```python
import functools
import jax
import jax.numpy as jnp
from jax import lax
from jax.experimental import pallas as pl
from jax.experimental.pallas import tpu as pltpu
from jax.sharding import PartitionSpec as P

HEAD_DIM = 64
POOL = 8
GRID_W = 128
EPS = 1e-06
BF = jnp.bfloat16
F32 = jnp.float32
VMEM_LIMIT = 24 * 1024 * 1024
NORM_LIMIT = 57 * 1024 * 1024

NN = (((1,), (0,)), ((), ()))
TN = (((0,), (0,)), ((), ()))
NT = (((1,), (1,)), ((), ()))


def mm(left, right, dims=NN):
    return lax.dot_general(left, right, dims, preferred_element_type=F32)


def cost(flops, moved):
    return pl.CostEstimate(flops=int(flops), bytes_accessed=int(moved), transcendentals=0)


ANY = pl.BlockSpec(memory_space=pl.ANY)


def after(kernel, inputs, deps):
    return lambda *refs: kernel(*refs[:inputs], *refs[inputs + deps :])


def params(axes=1, limit=VMEM_LIMIT):
    return pltpu.CompilerParams(
        dimension_semantics=("arbitrary",) * axes, vmem_limit_bytes=limit
    )


def norm_kernel(pos_ref, gain_ref, rgain_ref, tok_ref, cot_ref, normed_ref, cot_out_ref, red_ref,
                runit_ref, rinv_ref, pooled):
    step, col = pl.program_id(0), pl.program_id(1)
    half = pl.num_programs(0) // 2
    row = lax.rem(step + (1 - pos_ref[1]) * half, 2 * half)
    cols, width = tok_ref.shape[1], tok_ref.shape[2]
    gain = gain_ref[...].astype(F32).reshape(1, 1, width)
    chunk = 2 * POOL
    sums = []
    for part in range(cols // chunk):
        at = slice(part * chunk, (part + 1) * chunk)
        v = tok_ref[:, at, :].astype(F32)
        d = v - jnp.mean(v, axis=-1, keepdims=True)
        inv = lax.rsqrt(jnp.mean(d * d, axis=-1, keepdims=True) + EPS)
        n = (d * inv * gain).astype(BF)
        normed_ref[:, at, :] = n
        acc = jnp.sum(n.astype(F32), axis=0)
        sums.append(jnp.sum(acc.reshape(2, POOL, width), axis=1))
    span = cols // POOL
    base = pl.multiple_of((row * pl.num_programs(1) + col) * span, span)
    pooled[pl.ds(base, span), :] = jnp.concatenate(sums, axis=0)

    @pl.when(step >= half)
    def _():
        cot_out_ref[...] = cot_ref[...]

    @pl.when((step == pl.num_programs(0) - 1) & (col == pl.num_programs(1) - 1))
    def _():
        v = pooled[...] / (POOL * POOL)
        d = v - jnp.mean(v, axis=-1, keepdims=True)
        inv = lax.rsqrt(jnp.mean(d * d, axis=-1, keepdims=True) + EPS)
        unit = d * inv
        runit_ref[...] = unit
        rinv_ref[...] = jnp.broadcast_to(inv, rinv_ref.shape)
        red_ref[...] = (unit * rgain_ref[...].astype(F32).reshape(1, width)).astype(BF)


def norm_and_pool(pos, tokens, cotangent, norm_gain, reduce_gain, deps):
    count, width = tokens.shape
    grid_rows = count // GRID_W
    blocks = count // (POOL * POOL)
    cols = 64
    rows = grid_rows // POOL
    half = rows // 2
    block = (POOL, cols, width)

    def own(i):
        return jnp.maximum(i - half, 0)

    def own_col(i, j):
        return jnp.where(i >= half, j, 0)

    tok = pl.BlockSpec(block, lambda i, j, p: (lax.rem(i + (1 - p[1]) * half, rows), j, 0))
    cot = pl.BlockSpec(block, lambda i, j, p: (p[1] * half + own(i), own_col(i, j), 0))
    out = pl.BlockSpec(block, lambda i, j, p: (own(i), own_col(i, j), 0))
    whole = lambda shape: pl.BlockSpec(shape, lambda i, j, p: (0,) * len(shape))
    normed, cot_own, reduced, unit, inverse = pl.pallas_call(
        after(norm_kernel, 5, len(deps)),
        grid_spec=pltpu.PrefetchScalarGridSpec(
            num_scalar_prefetch=1,
            grid=(rows, GRID_W // cols),
            in_specs=[whole((width,)), whole((width,)), tok, cot]
            + [ANY] * len(deps),
            out_specs=[
                out,
                out,
                whole((blocks, width)),
                whole((blocks, width)),
                whole((blocks, 128)),
            ],
            scratch_shapes=[pltpu.VMEM((blocks, width), F32)],
        ),
        out_shape=[
            jax.ShapeDtypeStruct((grid_rows // 2, GRID_W, width), BF),
            jax.ShapeDtypeStruct((grid_rows // 2, GRID_W, width), BF),
            jax.ShapeDtypeStruct((blocks, width), BF),
            jax.ShapeDtypeStruct((blocks, width), F32),
            jax.ShapeDtypeStruct((blocks, 128), F32),
        ],
        compiler_params=params(2, NORM_LIMIT),
        cost_estimate=cost(40 * count * width, 10 * count * width),
        name="norm_pool",
    )(
        pos,
        norm_gain,
        reduce_gain,
        tokens.reshape(grid_rows, GRID_W, width),
        cotangent.reshape(grid_rows, GRID_W, width),
        *deps,
    )
    return (
        normed.reshape(count // 2, width),
        cot_own.reshape(count // 2, width),
        reduced,
        unit,
        inverse,
    )


def spread_heads(w_ref, width, kbd, vbd, kbd_t, vbd_t):
    feats, blocks = w_ref.shape[1], w_ref.shape[2] - width
    row = lax.broadcasted_iota(jnp.int32, (feats, blocks), 0)
    k = w_ref[0, :, width:].astype(F32) * HEAD_DIM ** (-0.5)
    v = w_ref[1, :, width:].astype(F32)
    for head in range(feats // HEAD_DIM):
        mask = (row >= head * HEAD_DIM) & (row < (head + 1) * HEAD_DIM)
        lanes = slice(head * blocks, (head + 1) * blocks)
        kbd_t[:, lanes] = jnp.where(mask, k, 0.0).astype(BF)
        vbd_t[:, lanes] = jnp.where(mask, v, 0.0).astype(BF)
    kbd[...] = kbd_t[...].T
    vbd[...] = vbd_t[...].T


def attend_tile(x, y, w_ref, kbd, vbd, kbd_t, vbd_t):
    feats = w_ref.shape[1]
    heads = feats // HEAD_DIM
    blocks = kbd.shape[0] // heads
    q_t = mm(w_ref[0, :, : x.shape[1]], x, NT).astype(BF)
    da_t = mm(w_ref[1, :, : y.shape[1]], y, NT).astype(BF)
    scores = mm(kbd[...], q_t)
    d_chances = mm(vbd[...], da_t)
    low, d_low = [], []
    for head in range(heads):
        rows = slice(head * blocks, (head + 1) * blocks)
        s = scores[rows]
        e = jnp.exp(s - jnp.max(s, axis=0, keepdims=True))
        p = e * (1.0 / jnp.sum(e, axis=0, keepdims=True))
        dp = d_chances[rows]
        delta = jnp.sum(p * dp, axis=0, keepdims=True)
        low.append(p.astype(BF))
        d_low.append((p * (dp - delta)).astype(BF))
    low = jnp.concatenate(low, axis=0)
    d_low = jnp.concatenate(d_low, axis=0)
    attn_t = mm(vbd_t[...], low).astype(BF)
    dq_t = mm(kbd_t[...], d_low).astype(BF)
    return q_t, da_t, low, d_low, attn_t, dq_t


def head_mask(shape, head):
    lane = lax.broadcasted_iota(jnp.int32, shape, 1)
    return (lane >= head * HEAD_DIM) & (lane < (head + 1) * HEAD_DIM)


def head_scratch(heads, blocks, feats):
    return [
        pltpu.VMEM((heads * blocks, feats), BF),
        pltpu.VMEM((heads * blocks, feats), BF),
        pltpu.VMEM((feats, heads * blocks), BF),
        pltpu.VMEM((feats, heads * blocks), BF),
    ]


def attend_kernel(n_sp, grad_factor, x_ref, y_ref, w_ref, attn_ref, dq_ref, *rest):
    step = pl.program_id(0)
    feats, width = w_ref.shape[1], x_ref.shape[1]
    blocks = w_ref.shape[2] - width
    depth = width // n_sp
    heads_at = rest[-4:] if len(rest) == 4 else rest[2:6]
    if len(rest) > 4:
        grad_ref, dkv_ref = rest[:2]
        dk_acc, dv_acc, g_acc = rest[6:]

    @pl.when(step == 0)
    def _():
        spread_heads(w_ref, width, *heads_at)
        if len(rest) > 4:
            dk_acc[...] = jnp.zeros_like(dk_acc)
            dv_acc[...] = jnp.zeros_like(dv_acc)
            g_acc[...] = jnp.zeros_like(g_acc)

    x, y = x_ref[...], y_ref[...]
    q_t, da_t, low, d_low, attn_t, dq_t = attend_tile(x, y, w_ref, *heads_at)
    attn_ref[...] = attn_t
    dq_ref[...] = dq_t
    if len(rest) == 4:
        return
    dk_acc[...] += mm(d_low, q_t, NT)
    dv_acc[...] += mm(low, da_t, NT)
    g_acc[0] += mm(dq_t, x)
    g_acc[1] += mm(attn_t, y)

    @pl.when(step == pl.num_programs(0) - 1)
    def _():
        dk = jnp.zeros((blocks, feats), F32)
        dv = jnp.zeros((blocks, feats), F32)
        for head in range(feats // HEAD_DIM):
            mask = head_mask((blocks, feats), head)
            rows = slice(head * blocks, (head + 1) * blocks)
            dk = dk + jnp.where(mask, dk_acc[rows, :], 0.0)
            dv = dv + jnp.where(mask, dv_acc[rows, :], 0.0)
        dkv_ref[:, :feats] = (dk * HEAD_DIM ** (-0.5)).astype(dkv_ref.dtype)
        dkv_ref[:, feats:] = dv.astype(dkv_ref.dtype)
        for place in range(n_sp):
            cols = slice(place * depth, (place + 1) * depth)
            grad_ref[place] = (g_acc[:, :, cols] * grad_factor).astype(BF)


def fixed(shape):
    return pl.BlockSpec(shape, lambda i: (0,) * len(shape))


def attend(n_sp, normed, cotangent, weights, deps, grad_factor=None, dkv_type=BF):
    feats = weights.shape[1]
    own, width = normed.shape
    blocks = weights.shape[2] - width
    heads = feats // HEAD_DIM
    tile = 256
    rows = pl.BlockSpec((tile, width), lambda i: (i, 0))
    t_spec = pl.BlockSpec((feats, tile), lambda i: (0, i))
    out_specs = [t_spec, t_spec]
    out_shape = [jax.ShapeDtypeStruct((feats, own), BF)] * 2
    scratch = head_scratch(heads, blocks, feats)
    flops = 4 * own * width * feats + 8 * own * heads * blocks * feats
    if grad_factor is not None:
        grad_shape = (n_sp, 2, feats, width // n_sp)
        out_specs += [fixed(grad_shape), fixed((blocks, 2 * feats))]
        out_shape += [
            jax.ShapeDtypeStruct(grad_shape, BF),
            jax.ShapeDtypeStruct((blocks, 2 * feats), dkv_type),
        ]
        scratch += [
            pltpu.VMEM((heads * blocks, feats), F32),
            pltpu.VMEM((heads * blocks, feats), F32),
            pltpu.VMEM((2, feats, width), F32),
        ]
        flops = flops + 4 * own * width * feats + 4 * own * heads * blocks * feats
    return pl.pallas_call(
        after(functools.partial(attend_kernel, n_sp, grad_factor), 3, len(deps)),
        grid=(own // tile,),
        in_specs=[rows, rows, fixed(weights.shape)] + [ANY] * len(deps),
        out_specs=out_specs,
        out_shape=out_shape,
        scratch_shapes=scratch,
        compiler_params=params(),
        cost_estimate=cost(2 * flops, 4 * own * width + 8 * width * feats),
        name="attend" if grad_factor is None else "attend_grads",
    )(normed, cotangent, weights, *deps)


def rows_kernel(count, pos_ref, *refs):
    attn_refs, refs = refs[:count], refs[count:]
    dq_refs, refs = refs[:count], refs[count:]
    w_refs, (own_ref, sib_ref, heads_ref) = refs[:count], refs[count:]
    h = pos_ref[2]
    sib = h + 1 - 2 * lax.rem(h, 2)
    cols = own_ref.shape[1]
    rows = [ref[...].T for ref in attn_refs]
    for ref, owner in ((own_ref, h), (sib_ref, sib)):
        lanes = pl.ds(pl.multiple_of(owner * cols, 128), cols)
        total = None
        for row, w_ref in zip(rows, w_refs):
            term = mm(row, w_ref[1, :, lanes]).astype(BF).astype(F32)
            total = term if total is None else total + term
        ref[...] = total.astype(BF)
    total = None
    for dq_ref, w_ref in zip(dq_refs, w_refs):
        term = mm(dq_ref[...].T, w_ref[0, :, : heads_ref.shape[1]]).astype(BF).astype(F32)
        total = term if total is None else total + term
    heads_ref[...] = total


def model_rows(pos, width, attns, dqs, weights, n_hd, deps):
    count = len(attns)
    feats = weights[0].shape[1]
    own = attns[0].shape[1]
    cols = width // n_hd
    tile = 256
    steps = own // tile
    whole = lambda shape: pl.BlockSpec(shape, lambda i, p: (0,) * len(shape))
    t_spec = pl.BlockSpec((feats, tile), lambda i, p: (0, i))
    return pl.pallas_call(
        after(functools.partial(rows_kernel, count), 3 * count + 1, len(deps)),
        grid_spec=pltpu.PrefetchScalarGridSpec(
            num_scalar_prefetch=1,
            grid=(steps,),
            in_specs=[t_spec] * (2 * count) + [whole(w.shape) for w in weights]
            + [ANY] * len(deps),
            out_specs=[
                pl.BlockSpec((tile, cols), lambda i, p: (p[1] * steps + i, 0)),
                pl.BlockSpec((tile, cols), lambda i, p: (i, 0)),
                pl.BlockSpec((tile, width), lambda i, p: (i, 0)),
            ],
        ),
        out_shape=[
            jax.ShapeDtypeStruct((2 * own, cols), BF),
            jax.ShapeDtypeStruct((own, cols), BF),
            jax.ShapeDtypeStruct((own, width), F32),
        ],
        compiler_params=params(),
        cost_estimate=cost(4 * own * width * (width + 2 * cols), 12 * own * width),
        name="model_rows",
    )(pos, *attns, *dqs, *weights, *deps)


def input_kernel(count, pos_ref, gain_ref, rgain_ref, tok_ref, runit_ref, rinv_ref, heads_ref, *refs):
    d_refs, (own_ref, sib_ref, spread, u_ref) = refs[:count], refs[count:]
    width = tok_ref.shape[1]
    h = pos_ref[2]
    sib = h + 1 - 2 * lax.rem(h, 2)
    cols = own_ref.shape[1]

    @pl.when(pl.program_id(0) == 0)
    def _():
        groups = runit_ref.shape[0]
        total = d_refs[0][...].astype(F32)
        for ref in d_refs[1:]:
            total = total + ref[...].astype(F32)
        e = total * rgain_ref[...].astype(F32).reshape(1, width)
        unit = runit_ref[...]
        first = jnp.mean(e, axis=-1, keepdims=True)
        second = jnp.mean(e * unit, axis=-1, keepdims=True)
        d_pooled = rinv_ref[:, 0:1] * (e - first - unit * second) / (POOL * POOL)
        spread[...] = jnp.broadcast_to(d_pooled[:, None, :], (groups, POOL, width)).reshape(
            groups * POOL, width
        )

    gain = gain_ref[...].astype(F32).reshape(1, width)
    for part in range(tok_ref.shape[0] // GRID_W):
        at = slice(part * GRID_W, (part + 1) * GRID_W)
        v = tok_ref[at, :].astype(F32)
        d = v - jnp.mean(v, axis=-1, keepdims=True)
        inv = lax.rsqrt(jnp.mean(d * d, axis=-1, keepdims=True) + EPS)
        unit = d * inv
        e = (heads_ref[at, :] + spread[...]) * gain
        first = jnp.mean(e, axis=-1, keepdims=True)
        second = jnp.mean(e * unit, axis=-1, keepdims=True)
        u_ref[at, :] = inv * (e - first - unit * second)
    for ref, owner in ((own_ref, h), (sib_ref, sib)):
        ref[...] = u_ref[:, pl.ds(pl.multiple_of(owner * cols, 128), cols)].astype(BF)


def input_rows(pos, norm_gain, reduce_gain, tokens, unit, inverse, d_heads, parts, n_hd, deps):
    own, width = d_heads.shape
    cols = width // n_hd
    groups = parts[0].shape[0]
    tile = 256
    steps = own // tile
    whole = lambda shape: pl.BlockSpec(shape, lambda i, p: (0,) * len(shape))
    half = lambda shape: pl.BlockSpec(shape, lambda i, p: (p[1], 0))
    return pl.pallas_call(
        after(functools.partial(input_kernel, len(parts)), 7 + len(parts), len(deps)),
        grid_spec=pltpu.PrefetchScalarGridSpec(
            num_scalar_prefetch=1,
            grid=(steps,),
            in_specs=[
                whole((width,)),
                whole((width,)),
                pl.BlockSpec((tile, width), lambda i, p: (p[1] * steps + i, 0)),
                half((groups, width)),
                half((groups, 128)),
                pl.BlockSpec((tile, width), lambda i, p: (i, 0)),
            ]
            + [whole(part.shape) for part in parts]
            + [ANY] * len(deps),
            out_specs=[
                pl.BlockSpec((tile, cols), lambda i, p: (p[1] * steps + i, 0)),
                pl.BlockSpec((tile, cols), lambda i, p: (i, 0)),
            ],
            scratch_shapes=[
                pltpu.VMEM((groups * POOL, width), F32),
                pltpu.VMEM((tile, width), F32),
            ],
        ),
        out_shape=[
            jax.ShapeDtypeStruct((2 * own, cols), BF),
            jax.ShapeDtypeStruct((own, cols), BF),
        ],
        compiler_params=params(),
        cost_estimate=cost(40 * own * width, 16 * own * width),
        name="input_rows",
    )(
        pos,
        norm_gain,
        reduce_gain,
        tokens,
        unit,
        inverse,
        d_heads,
        *parts,
        *deps,
    )


def small(kernel, name, out_shape, *args, pos=None, deps=()):
    smem = [] if pos is None else [pl.BlockSpec(memory_space=pltpu.SMEM)]
    vmem = pl.BlockSpec(memory_space=pltpu.VMEM)
    many = isinstance(out_shape, list)
    return pl.pallas_call(
        after(kernel, len(smem) + len(args), len(deps)),
        in_specs=smem + [vmem] * len(args) + [ANY] * len(deps),
        out_specs=[vmem] * len(out_shape) if many else vmem,
        out_shape=out_shape,
        compiler_params=pltpu.CompilerParams(vmem_limit_bytes=VMEM_LIMIT),
        cost_estimate=cost(1 << 28, 1 << 21),
        name=name,
    )(*([] if pos is None else [pos]), *args, *deps)


def turn_kernel(pos_ref, q_ref, o_ref, out_ref, half_ref):
    q, o = q_ref[...].T, o_ref[...].T
    out_ref[0] = q
    out_ref[1] = o
    half_ref[...] = jnp.where(pos_ref[3] == 0, q, o)


def stack_kernel(*refs):
    for k, ref in enumerate(refs[:-1]):
        refs[-1][k] = ref[...]


def choose(index, values):
    result = values[0]
    for k in range(1, len(values)):
        result = jnp.where(index == k, values[k], result)
    return result


def place_pieces(z, pieces, out_ref, which):
    n_sp, depth = len(pieces), pieces[0].shape[1]
    for place in range(n_sp):
        index = lax.rem(z - place + n_sp, n_sp)
        out_ref[which, :, place * depth : (place + 1) * depth] = choose(index, pieces)


def pack_kernel(n_sp, pos_ref, own_ref, here_ref, there_ref, part_ref, *refs):
    parts, (out_ref, kv_ref) = refs[:-2], refs[-2:]
    feats, depth = own_ref.shape[1:]
    rows = part_ref.shape[0]
    blocks, width = rows // n_sp, depth * n_sp
    z, y = pos_ref[0], pos_ref[3]
    for which in range(2):
        pieces = [own_ref[which]] + [
            jnp.where(y == which, here_ref[k], there_ref[k]) for k in range(n_sp - 1)
        ]
        place_pieces(z, pieces, out_ref, which)
        lanes = slice(which * feats, (which + 1) * feats)
        sums = []
        for j in range(n_sp):
            total = part_ref[j * blocks : (j + 1) * blocks, lanes]
            for k, part in enumerate(parts, 1):
                at = (j - k) % n_sp
                total = total + part[at * blocks : (at + 1) * blocks, lanes].astype(F32)
            sums.append(total)
        kv = jnp.concatenate(sums, axis=0).T.astype(BF)
        out_ref[which, :, width:] = kv
        kv_ref[which] = kv


def pack_far_kernel(pos_ref, here_ref, there_ref, kv_ref, out_ref):
    n_sp, feats, depth = here_ref.shape
    z, y = pos_ref[0], pos_ref[3]
    for which in range(2):
        pieces = [jnp.where(y == which, here_ref[k], there_ref[k]) for k in range(n_sp)]
        place_pieces(z, pieces, out_ref, which)
        out_ref[which, :, n_sp * depth :] = kv_ref[which]


def project_kernel(k_ref, v_ref, own_ref, far_ref, *refs):
    red, (cols_ref, part_ref, low_ref, all_ref) = refs[:-4], refs[-4:]
    all_ref[0] = own_ref[...]
    all_ref[1:] = far_ref[...]
    feats = k_ref.shape[1]
    rows = jnp.concatenate([ref[...] for ref in red], axis=0)
    cols_ref[...] = rows
    for which, ref in ((0, k_ref), (1, v_ref)):
        lanes = slice(which * feats, (which + 1) * feats)
        part = mm(rows, ref[...])
        part_ref[:, lanes] = part
        low_ref[:, lanes] = part.astype(BF)


def grad_add_kernel(n_sp, pos_ref, grad_ref, grad_far_ref, dkv_ref, dkv_far_ref, *refs):
    g_refs, (d_ref, d_low_ref) = refs[:n_sp], refs[n_sp:]
    z = pos_ref[0]
    for k in range(n_sp):
        at = lax.rem(z + k, n_sp)
        total = grad_ref[at].astype(F32) + grad_far_ref[at].astype(F32)
        g_refs[k][...] = total.astype(g_refs[k].dtype)
    total = dkv_ref[...] + dkv_far_ref[...].astype(F32)
    d_ref[...] = total
    d_low_ref[...] = total.astype(BF)


def back_kernel(n_sp, pos_ref, own_ref, *refs):
    parts, weights = refs[: n_sp - 1], refs[n_sp - 1 : 2 * n_sp - 1]
    low_ref, mine_ref, other_ref, d_red = refs[-4:]
    blocks = own_ref.shape[0] // n_sp
    depth, feats = weights[0].shape[1:]
    z, c = pos_ref[0], pos_ref[1]
    for j in range(n_sp):
        total = own_ref[j * blocks : (j + 1) * blocks, :]
        for k, part in enumerate(parts, 1):
            at = (j - k) % n_sp
            total = total + part[at * blocks : (at + 1) * blocks, :].astype(F32)
        low_ref[j * blocks : (j + 1) * blocks, :] = total.astype(BF)
    low = low_ref[:blocks, :]
    terms = [mm(low[:, :feats], w[0], NT) + mm(low[:, feats:], w[1], NT) for w in weights]
    for place in range(n_sp):
        index = lax.rem(z - place + n_sp, n_sp)
        d_red[:, place * depth : (place + 1) * depth] = choose(index, terms)
    half = blocks // 2
    mine_ref[...] = d_red[pl.ds(pl.multiple_of(c * half, half), half), :].astype(BF)
    other_ref[...] = d_red[pl.ds(pl.multiple_of((1 - c) * half, half), half), :].astype(BF)


def pair_kernel(k_ref, v_ref, out_ref):
    out_ref[0] = k_ref[...]
    out_ref[1] = v_ref[...]


def kv_grad_kernel(grad_factor, red_ref, d_ref, key_ref, value_ref):
    feats = key_ref.shape[1]
    both = mm(red_ref[...].T, d_ref[...]) * grad_factor
    key_ref[...] = both[:, :feats]
    value_ref[...] = both[:, feats:]


def grad_sum_kernel(*refs):
    query_ref, out_ref = refs[-2:]
    for which, ref in ((0, query_ref), (1, out_ref)):
        total = refs[0][which].astype(F32)
        for part in refs[1:-2]:
            total = total + part[which].astype(F32)
        ref[...] = total.T


def on_device(
    tokens,
    norm_gain,
    reduce_gain,
    query_weight,
    key_weight,
    value_weight,
    out_weight,
    out_cotangent,
):
    n_sp, n_hd = lax.axis_size("sp"), lax.axis_size("hd")
    n_x = n_hd // 2
    z, h, y = lax.axis_index("sp"), lax.axis_index("hd"), lax.axis_index("scene")
    c = h % 2
    depth, feats = query_weight.shape
    width = tokens.shape[1]
    own = tokens.shape[0] // 2
    grad_factor = float(2 * own * n_sp) ** (-0.5)
    pos = jnp.stack([z, c, h, y]).astype(jnp.int32)
    others = range(1, n_sp)

    def low(*shape):
        return jax.ShapeDtypeStruct(shape, BF)

    def wide(*shape):
        return jax.ShapeDtypeStruct(shape, F32)

    def to_sp(value, k):
        return lax.ppermute(value, "sp", [(i, (i + k) % n_sp) for i in range(n_sp)])

    def to_hd(value, k):
        return lax.ppermute(value, "hd", [(i, (i + k) % n_hd) for i in range(n_hd)])

    def swap(value):
        return lax.ppermute(value, "hd", [(i, i ^ 1) for i in range(n_hd)])

    def cross(value):
        return lax.ppermute(value, "scene", [(0, 1), (1, 0)])

    block = pl.BlockSpec((depth, feats), lambda i, p: (0, 0))
    shard, half = pl.pallas_call(
        turn_kernel,
        grid_spec=pltpu.PrefetchScalarGridSpec(
            num_scalar_prefetch=1,
            grid=(1,),
            in_specs=[block, block],
            out_specs=[
                pl.BlockSpec((2, feats, depth), lambda i, p: (0, 0, 0)),
                pl.BlockSpec((feats, depth), lambda i, p: (0, 0)),
            ],
        ),
        out_shape=[low(2, feats, depth), low(feats, depth)],
        compiler_params=params(1, NORM_LIMIT),
        name="turn",
    )(pos, query_weight, out_weight)
    here = [to_sp(half, k) for k in others]
    normed, cot, reduced, r_unit, r_inverse = norm_and_pool(
        pos, tokens, out_cotangent, norm_gain, reduce_gain, (half,)
    )
    blocks = reduced.shape[0]
    far3 = small(stack_kernel, "stack", low(n_sp - 1, feats, depth), *here, deps=(reduced,))
    there3 = cross(far3)

    red_cut = jnp.stack([reduced[:, i * depth : (i + 1) * depth] for i in range(n_sp)])
    cuts = [lax.dynamic_index_in_dim(red_cut, (z + k) % n_sp, 0, keepdims=False) for k in range(n_sp)]
    both = (blocks * n_sp, 2 * feats)
    reduced_cols, kv_part, kv_low, all4 = small(
        project_kernel,
        "project",
        [low(blocks * n_sp, depth), wide(*both), low(*both), low(n_sp, feats, depth)],
        key_weight,
        value_weight,
        half,
        far3,
        cuts[0],
        *[to_sp(cuts[k], k) for k in others],
    )
    x_pieces = [to_hd(all4, 2 * k) for k in range(1, n_x)]
    packed, kv_own = small(
        functools.partial(pack_kernel, n_sp),
        "pack",
        [low(2, feats, width + blocks * n_sp), low(2, feats, blocks * n_sp)],
        shard,
        far3,
        there3,
        kv_part,
        *[to_sp(kv_low, k) for k in others],
        pos=pos,
        deps=tuple(x_pieces),
    )

    kv_weight = small(
        pair_kernel,
        "pair",
        low(2, depth, feats),
        key_weight,
        value_weight,
        deps=(packed,),
    )
    kv_weights = [kv_weight] + [to_sp(kv_weight, k) for k in others]
    third = (n_sp + 1) // 3

    attn0, dq0, grad0, dkv0 = attend(n_sp, normed, cot, packed, (kv_weight,), grad_factor, F32)
    packed_sib = swap(packed)
    kv_far = [to_hd(kv_own, 2 * k) for k in range(1, n_x)]
    attn1, dq1, grad1, dkv1 = attend(
        n_sp,
        normed,
        cot,
        packed_sib,
        (attn0,),
        grad_factor,
        BF,
    )
    attns, dqs, ws = [attn0, attn1], [dq0, dq1], [packed, packed_sib]
    grad1, dkv1 = swap(grad1), swap(dkv1)

    later = (attn1, *kv_weights[1 : 1 + 2 * third])
    for piece, kv in zip(x_pieces, kv_far):
        packed_far = small(
            pack_far_kernel, "pack_far", low(*packed.shape), piece, cross(piece), kv, pos=pos, deps=later
        )
        ws += [packed_far, swap(packed_far)]

    attn, dq = attend(n_sp, normed, cot, ws[2], ())
    attns.append(attn)
    dqs.append(dq)
    grads = small(
        functools.partial(grad_add_kernel, n_sp),
        "grad_add",
        [wide(2, feats, depth)]
        + [low(2, feats, depth)] * (n_sp - 1)
        + [wide(*both), low(*both)],
        grad0,
        grad1,
        dkv0,
        dkv1,
        pos=pos,
        deps=(attn, *kv_weights[1 + 2 * third :]),
    )
    grads, (d_own, d_low) = grads[:n_sp], grads[n_sp:]
    grads = [grads[0]] + [to_sp(grads[k], k) for k in others]
    ranked = sorted(others, key=lambda k: -min(k, n_sp - k))
    first = [grads[k] for k in ranked[: 2 * third]]
    last = [grads[k] for k in ranked[2 * third :]]
    later = (d_low,)
    for w in ws[3:]:
        attn, dq = attend(n_sp, normed, cot, w, later)
        attns.append(attn)
        dqs.append(dq)

    dkv_all, d_mine, d_other = pl.pallas_call(
        after(functools.partial(back_kernel, n_sp), 1 + 2 * n_sp, 1),
        in_specs=[pl.BlockSpec(memory_space=pltpu.SMEM)]
        + [pl.BlockSpec(memory_space=pltpu.VMEM)] * (2 * n_sp)
        + [ANY],
        out_specs=[pl.BlockSpec(memory_space=pltpu.VMEM)] * 3,
        out_shape=[low(*both), low(blocks // 2, width), low(blocks // 2, width)],
        scratch_shapes=[pltpu.VMEM((blocks, width), F32)],
        compiler_params=pltpu.CompilerParams(vmem_limit_bytes=VMEM_LIMIT),
        cost_estimate=cost(1 << 28, 1 << 21),
        name="back",
    )(
        pos,
        d_own,
        *[to_sp(d_low, k) for k in others],
        *kv_weights,
        attns[-1],
    )
    parts = [d_mine] + [to_hd(d_other if k % 2 else d_mine, k) for k in range(1, n_hd)]

    branch, other, d_heads = model_rows(
        pos, width, attns, dqs, ws, n_hd, (d_mine, *first)
    )
    key_grad, value_grad = small(
        functools.partial(kv_grad_kernel, grad_factor),
        "kv_grad",
        [wide(depth, feats)] * 2,
        reduced_cols,
        dkv_all,
        deps=(d_heads,),
    )
    place = (1 - c) * own
    branch = lax.dynamic_update_slice_in_dim(branch, swap(other), place, 0)
    input_grad, other = input_rows(
        pos,
        norm_gain,
        reduce_gain,
        tokens,
        r_unit,
        r_inverse,
        d_heads,
        parts,
        n_hd,
        (key_grad, *last),
    )
    input_grad = lax.dynamic_update_slice_in_dim(input_grad, swap(other), place, 0)
    query_grad, out_grad = small(
        grad_sum_kernel, "grad_sum", [wide(depth, feats)] * 2, *grads, deps=(other,)
    )
    return (branch, input_grad, query_grad, key_grad, value_grad, out_grad)


def solution(mesh):
    rows, whole, both = P(("scene", "sp"), None), P(), P("sp", "hd")
    out = P(("scene", "sp"), "hd")
    return jax.shard_map(
        on_device,
        mesh=mesh,
        in_specs=(rows, whole, whole, both, both, both, both, rows),
        out_specs=(out,) * 6,
        check_vma=False,
    )
```

```python
import functools
import jax
import jax.numpy as jnp
from jax import lax
from jax.experimental import pallas as pl
from jax.experimental.pallas import tpu as pltpu
from jax.sharding import PartitionSpec as P

HEAD_DIM = 64
POOL = 8
GRID_W = 128
EPS = 1e-06
BF = jnp.bfloat16
F32 = jnp.float32
VMEM_LIMIT = 24 * 1024 * 1024
NORM_LIMIT = 50 * 1024 * 1024
TURN_LIMIT = 58 * 1024 * 1024

NN = (((1,), (0,)), ((), ()))
TN = (((0,), (0,)), ((), ()))
NT = (((1,), (1,)), ((), ()))


def mm(left, right, dims=NN):
    return lax.dot_general(left, right, dims, preferred_element_type=F32)


def cost(flops, moved):
    return pl.CostEstimate(flops=int(flops), bytes_accessed=int(moved), transcendentals=0)


ANY = pl.BlockSpec(memory_space=pl.ANY)


def after(kernel, inputs, deps):
    return lambda *refs: kernel(*refs[:inputs], *refs[inputs + deps :])


def params(axes=1, limit=VMEM_LIMIT):
    return pltpu.CompilerParams(
        dimension_semantics=("arbitrary",) * axes, vmem_limit_bytes=limit
    )


def row_mean(values):
    width = values.shape[1]
    ones = jnp.ones((width, 128), BF)
    high = values.astype(BF)
    total = mm(high, ones) + mm((values - high.astype(F32)).astype(BF), ones)
    return jnp.concatenate([total * (1.0 / width)] * (width // 128), axis=1)


def unit_and_inverse(low):
    width = low.shape[1]
    mean = mm(low, jnp.ones((width, 128), BF)) * (1.0 / width)
    d = low.astype(F32) - jnp.concatenate([mean] * (width // 128), axis=1)
    inv = lax.rsqrt(row_mean(d * d) + EPS)
    return d * inv, inv


def norm_kernel(pos_ref, gain_ref, rgain_ref, tok_ref, cot_ref, normed_ref, cot_out_ref, red_ref,
                runit_ref, rinv_ref, pooled):
    step, col = pl.program_id(0), pl.program_id(1)
    half = pl.num_programs(0) // 2
    row = lax.rem(step + (1 - pos_ref[1]) * half, 2 * half)
    cols, width = tok_ref.shape[1], tok_ref.shape[2]
    gain = gain_ref[...].astype(F32).reshape(1, width)
    chunk = 2 * POOL
    sums = []
    for part in range(cols // chunk):
        at = slice(part * chunk, (part + 1) * chunk)
        unit, _ = unit_and_inverse(tok_ref[:, at, :].reshape(POOL * chunk, width))
        n = (unit * gain).astype(BF).reshape(POOL, chunk, width)
        normed_ref[:, at, :] = n
        acc = jnp.sum(n.astype(F32), axis=0)
        sums.append(jnp.sum(acc.reshape(2, POOL, width), axis=1))
    span = cols // POOL
    base = pl.multiple_of((row * pl.num_programs(1) + col) * span, span)
    pooled[pl.ds(base, span), :] = jnp.concatenate(sums, axis=0)

    @pl.when(step >= half)
    def _():
        cot_out_ref[...] = cot_ref[...]

    @pl.when((step == pl.num_programs(0) - 1) & (col == pl.num_programs(1) - 1))
    def _():
        v = pooled[...] / (POOL * POOL)
        d = v - jnp.mean(v, axis=-1, keepdims=True)
        inv = lax.rsqrt(jnp.mean(d * d, axis=-1, keepdims=True) + EPS)
        unit = d * inv
        runit_ref[...] = unit
        rinv_ref[...] = jnp.broadcast_to(inv, rinv_ref.shape)
        red_ref[...] = (unit * rgain_ref[...].astype(F32).reshape(1, width)).astype(BF)


def norm_and_pool(pos, tokens, cotangent, norm_gain, reduce_gain, deps):
    count, width = tokens.shape
    grid_rows = count // GRID_W
    blocks = count // (POOL * POOL)
    cols = 64
    rows = grid_rows // POOL
    half = rows // 2
    block = (POOL, cols, width)

    def own(i):
        return jnp.maximum(i - half, 0)

    def own_col(i, j):
        return jnp.where(i >= half, j, 0)

    tok = pl.BlockSpec(block, lambda i, j, p: (lax.rem(i + (1 - p[1]) * half, rows), j, 0))
    cot = pl.BlockSpec(block, lambda i, j, p: (p[1] * half + own(i), own_col(i, j), 0))
    out = pl.BlockSpec(block, lambda i, j, p: (own(i), own_col(i, j), 0))
    whole = lambda shape: pl.BlockSpec(shape, lambda i, j, p: (0,) * len(shape))
    normed, cot_own, reduced, unit, inverse = pl.pallas_call(
        after(norm_kernel, 5, len(deps)),
        grid_spec=pltpu.PrefetchScalarGridSpec(
            num_scalar_prefetch=1,
            grid=(rows, GRID_W // cols),
            in_specs=[whole((width,)), whole((width,)), tok, cot]
            + [ANY] * len(deps),
            out_specs=[
                out,
                out,
                whole((blocks, width)),
                whole((blocks, width)),
                whole((blocks, 128)),
            ],
            scratch_shapes=[pltpu.VMEM((blocks, width), F32)],
        ),
        out_shape=[
            jax.ShapeDtypeStruct((grid_rows // 2, GRID_W, width), BF),
            jax.ShapeDtypeStruct((grid_rows // 2, GRID_W, width), BF),
            jax.ShapeDtypeStruct((blocks, width), BF),
            jax.ShapeDtypeStruct((blocks, width), F32),
            jax.ShapeDtypeStruct((blocks, 128), F32),
        ],
        compiler_params=params(2, NORM_LIMIT),
        cost_estimate=cost(40 * count * width, 10 * count * width),
        name="norm_pool",
    )(
        pos,
        norm_gain,
        reduce_gain,
        tokens.reshape(grid_rows, GRID_W, width),
        cotangent.reshape(grid_rows, GRID_W, width),
        *deps,
    )
    return (
        normed.reshape(count // 2, width),
        cot_own.reshape(count // 2, width),
        reduced,
        unit,
        inverse,
    )


def spread_heads(w_ref, width, kbd, vbd, kbd_t, vbd_t):
    feats, blocks = w_ref.shape[1], w_ref.shape[2] - width
    row = lax.broadcasted_iota(jnp.int32, (feats, blocks), 0)
    k = w_ref[0, :, width:].astype(F32) * HEAD_DIM ** (-0.5)
    v = w_ref[1, :, width:].astype(F32)
    for head in range(feats // HEAD_DIM):
        mask = (row >= head * HEAD_DIM) & (row < (head + 1) * HEAD_DIM)
        lanes = slice(head * blocks, (head + 1) * blocks)
        kbd_t[:, lanes] = jnp.where(mask, k, 0.0).astype(BF)
        vbd_t[:, lanes] = jnp.where(mask, v, 0.0).astype(BF)
    kbd[...] = kbd_t[...].T
    vbd[...] = vbd_t[...].T


def attend_tile(x, y, w_ref, kbd, vbd, kbd_t, vbd_t):
    feats = w_ref.shape[1]
    heads = feats // HEAD_DIM
    blocks = kbd.shape[0] // heads
    q_t = mm(w_ref[0, :, : x.shape[1]], x, NT).astype(BF)
    da_t = mm(w_ref[1, :, : y.shape[1]], y, NT).astype(BF)
    scores = mm(kbd[...], q_t)
    d_chances = mm(vbd[...], da_t)
    low, d_low = [], []
    for head in range(heads):
        rows = slice(head * blocks, (head + 1) * blocks)
        s = scores[rows]
        e = jnp.exp(s - jnp.max(s, axis=0, keepdims=True))
        p = e * (1.0 / jnp.sum(e, axis=0, keepdims=True))
        dp = d_chances[rows]
        delta = jnp.sum(p * dp, axis=0, keepdims=True)
        low.append(p.astype(BF))
        d_low.append((p * (dp - delta)).astype(BF))
    low = jnp.concatenate(low, axis=0)
    d_low = jnp.concatenate(d_low, axis=0)
    attn_t = mm(vbd_t[...], low).astype(BF)
    dq_t = mm(kbd_t[...], d_low).astype(BF)
    return q_t, da_t, low, d_low, attn_t, dq_t


def head_mask(shape, head):
    lane = lax.broadcasted_iota(jnp.int32, shape, 1)
    return (lane >= head * HEAD_DIM) & (lane < (head + 1) * HEAD_DIM)


def head_scratch(heads, blocks, feats):
    return [
        pltpu.VMEM((heads * blocks, feats), BF),
        pltpu.VMEM((heads * blocks, feats), BF),
        pltpu.VMEM((feats, heads * blocks), BF),
        pltpu.VMEM((feats, heads * blocks), BF),
    ]


def attend_kernel(n_sp, grad_factor, x_ref, y_ref, w_ref, attn_ref, dq_ref, *rest):
    step = pl.program_id(0)
    feats, width = w_ref.shape[1], x_ref.shape[1]
    blocks = w_ref.shape[2] - width
    depth = width // n_sp
    heads_at = rest[-4:] if len(rest) == 4 else rest[2:6]
    if len(rest) > 4:
        grad_ref, dkv_ref = rest[:2]
        dk_acc, dv_acc, g_acc = rest[6:]

    @pl.when(step == 0)
    def _():
        spread_heads(w_ref, width, *heads_at)
        if len(rest) > 4:
            dk_acc[...] = jnp.zeros_like(dk_acc)
            dv_acc[...] = jnp.zeros_like(dv_acc)
            g_acc[...] = jnp.zeros_like(g_acc)

    x, y = x_ref[...], y_ref[...]
    q_t, da_t, low, d_low, attn_t, dq_t = attend_tile(x, y, w_ref, *heads_at)
    attn_ref[...] = attn_t
    dq_ref[...] = dq_t
    if len(rest) == 4:
        return
    dk_acc[...] += mm(d_low, q_t, NT)
    dv_acc[...] += mm(low, da_t, NT)
    g_acc[0] += mm(dq_t, x)
    g_acc[1] += mm(attn_t, y)

    @pl.when(step == pl.num_programs(0) - 1)
    def _():
        dk = jnp.zeros((blocks, feats), F32)
        dv = jnp.zeros((blocks, feats), F32)
        for head in range(feats // HEAD_DIM):
            mask = head_mask((blocks, feats), head)
            rows = slice(head * blocks, (head + 1) * blocks)
            dk = dk + jnp.where(mask, dk_acc[rows, :], 0.0)
            dv = dv + jnp.where(mask, dv_acc[rows, :], 0.0)
        dkv_ref[:, :feats] = (dk * HEAD_DIM ** (-0.5)).astype(dkv_ref.dtype)
        dkv_ref[:, feats:] = dv.astype(dkv_ref.dtype)
        for place in range(n_sp):
            cols = slice(place * depth, (place + 1) * depth)
            grad_ref[place] = (g_acc[:, :, cols] * grad_factor).astype(BF)


def fixed(shape):
    return pl.BlockSpec(shape, lambda i: (0,) * len(shape))


def attend(n_sp, normed, cotangent, weights, deps, grad_factor=None, dkv_type=BF):
    feats = weights.shape[1]
    own, width = normed.shape
    blocks = weights.shape[2] - width
    heads = feats // HEAD_DIM
    tile = 256
    rows = pl.BlockSpec((tile, width), lambda i: (i, 0))
    t_spec = pl.BlockSpec((feats, tile), lambda i: (0, i))
    out_specs = [t_spec, t_spec]
    out_shape = [jax.ShapeDtypeStruct((feats, own), BF)] * 2
    scratch = head_scratch(heads, blocks, feats)
    flops = 4 * own * width * feats + 8 * own * heads * blocks * feats
    if grad_factor is not None:
        grad_shape = (n_sp, 2, feats, width // n_sp)
        out_specs += [fixed(grad_shape), fixed((blocks, 2 * feats))]
        out_shape += [
            jax.ShapeDtypeStruct(grad_shape, BF),
            jax.ShapeDtypeStruct((blocks, 2 * feats), dkv_type),
        ]
        scratch += [
            pltpu.VMEM((heads * blocks, feats), F32),
            pltpu.VMEM((heads * blocks, feats), F32),
            pltpu.VMEM((2, feats, width), F32),
        ]
        flops = flops + 4 * own * width * feats + 4 * own * heads * blocks * feats
    return pl.pallas_call(
        after(functools.partial(attend_kernel, n_sp, grad_factor), 3, len(deps)),
        grid=(own // tile,),
        in_specs=[rows, rows, fixed(weights.shape)] + [ANY] * len(deps),
        out_specs=out_specs,
        out_shape=out_shape,
        scratch_shapes=scratch,
        compiler_params=params(),
        cost_estimate=cost(2 * flops, 4 * own * width + 8 * width * feats),
        name="attend" if grad_factor is None else "attend_grads",
    )(normed, cotangent, weights, *deps)


def rows_kernel(count, pos_ref, *refs):
    attn_refs, refs = refs[:count], refs[count:]
    dq_refs, refs = refs[:count], refs[count:]
    w_refs, (own_ref, sib_ref, heads_ref) = refs[:count], refs[count:]
    h = pos_ref[2]
    sib = h + 1 - 2 * lax.rem(h, 2)
    cols = own_ref.shape[1]
    rows = [ref[...].T for ref in attn_refs]
    for ref, owner in ((own_ref, h), (sib_ref, sib)):
        lanes = pl.ds(pl.multiple_of(owner * cols, 128), cols)
        total = None
        for row, w_ref in zip(rows, w_refs):
            term = mm(row, w_ref[1, :, lanes]).astype(BF).astype(F32)
            total = term if total is None else total + term
        ref[...] = total.astype(BF)
    total = None
    for dq_ref, w_ref in zip(dq_refs, w_refs):
        term = mm(dq_ref[...].T, w_ref[0, :, : heads_ref.shape[1]]).astype(BF).astype(F32)
        total = term if total is None else total + term
    heads_ref[...] = total


def model_rows(pos, width, attns, dqs, weights, n_hd, deps):
    count = len(attns)
    feats = weights[0].shape[1]
    own = attns[0].shape[1]
    cols = width // n_hd
    tile = 256
    steps = own // tile
    whole = lambda shape: pl.BlockSpec(shape, lambda i, p: (0,) * len(shape))
    t_spec = pl.BlockSpec((feats, tile), lambda i, p: (0, i))
    return pl.pallas_call(
        after(functools.partial(rows_kernel, count), 3 * count + 1, len(deps)),
        grid_spec=pltpu.PrefetchScalarGridSpec(
            num_scalar_prefetch=1,
            grid=(steps,),
            in_specs=[t_spec] * (2 * count) + [whole(w.shape) for w in weights]
            + [ANY] * len(deps),
            out_specs=[
                pl.BlockSpec((tile, cols), lambda i, p: (p[1] * steps + i, 0)),
                pl.BlockSpec((tile, cols), lambda i, p: (i, 0)),
                pl.BlockSpec((tile, width), lambda i, p: (i, 0)),
            ],
        ),
        out_shape=[
            jax.ShapeDtypeStruct((2 * own, cols), BF),
            jax.ShapeDtypeStruct((own, cols), BF),
            jax.ShapeDtypeStruct((own, width), F32),
        ],
        compiler_params=params(),
        cost_estimate=cost(4 * own * width * (width + 2 * cols), 12 * own * width),
        name="model_rows",
    )(pos, *attns, *dqs, *weights, *deps)


def input_kernel(count, pos_ref, gain_ref, rgain_ref, tok_ref, runit_ref, rinv_ref, heads_ref, *refs):
    d_refs, (own_ref, sib_ref, spread, u_ref) = refs[:count], refs[count:]
    width = tok_ref.shape[1]
    h = pos_ref[2]
    sib = h + 1 - 2 * lax.rem(h, 2)
    cols = own_ref.shape[1]

    @pl.when(pl.program_id(0) == 0)
    def _():
        groups = runit_ref.shape[0]
        total = d_refs[0][...].astype(F32)
        for ref in d_refs[1:]:
            total = total + ref[...].astype(F32)
        e = total * rgain_ref[...].astype(F32).reshape(1, width)
        unit = runit_ref[...]
        first = jnp.mean(e, axis=-1, keepdims=True)
        second = jnp.mean(e * unit, axis=-1, keepdims=True)
        d_pooled = rinv_ref[:, 0:1] * (e - first - unit * second) / (POOL * POOL)
        spread[...] = jnp.broadcast_to(d_pooled[:, None, :], (groups, POOL, width)).reshape(
            groups * POOL, width
        )

    gain = gain_ref[...].astype(F32).reshape(1, width)
    for part in range(tok_ref.shape[0] // GRID_W):
        at = slice(part * GRID_W, (part + 1) * GRID_W)
        unit, inv = unit_and_inverse(tok_ref[at, :])
        e = (heads_ref[at, :] + spread[...]) * gain
        first = row_mean(e)
        second = row_mean(e * unit)
        u_ref[at, :] = inv * (e - first - unit * second)
    for ref, owner in ((own_ref, h), (sib_ref, sib)):
        ref[...] = u_ref[:, pl.ds(pl.multiple_of(owner * cols, 128), cols)].astype(BF)


def input_rows(pos, norm_gain, reduce_gain, tokens, unit, inverse, d_heads, parts, n_hd, deps):
    own, width = d_heads.shape
    cols = width // n_hd
    groups = parts[0].shape[0]
    tile = 256
    steps = own // tile
    whole = lambda shape: pl.BlockSpec(shape, lambda i, p: (0,) * len(shape))
    half = lambda shape: pl.BlockSpec(shape, lambda i, p: (p[1], 0))
    return pl.pallas_call(
        after(functools.partial(input_kernel, len(parts)), 7 + len(parts), len(deps)),
        grid_spec=pltpu.PrefetchScalarGridSpec(
            num_scalar_prefetch=1,
            grid=(steps,),
            in_specs=[
                whole((width,)),
                whole((width,)),
                pl.BlockSpec((tile, width), lambda i, p: (p[1] * steps + i, 0)),
                half((groups, width)),
                half((groups, 128)),
                pl.BlockSpec((tile, width), lambda i, p: (i, 0)),
            ]
            + [whole(part.shape) for part in parts]
            + [ANY] * len(deps),
            out_specs=[
                pl.BlockSpec((tile, cols), lambda i, p: (p[1] * steps + i, 0)),
                pl.BlockSpec((tile, cols), lambda i, p: (i, 0)),
            ],
            scratch_shapes=[
                pltpu.VMEM((groups * POOL, width), F32),
                pltpu.VMEM((tile, width), F32),
            ],
        ),
        out_shape=[
            jax.ShapeDtypeStruct((2 * own, cols), BF),
            jax.ShapeDtypeStruct((own, cols), BF),
        ],
        compiler_params=params(),
        cost_estimate=cost(40 * own * width, 16 * own * width),
        name="input_rows",
    )(
        pos,
        norm_gain,
        reduce_gain,
        tokens,
        unit,
        inverse,
        d_heads,
        *parts,
        *deps,
    )


def small(kernel, name, out_shape, *args, pos=None, deps=()):
    smem = [] if pos is None else [pl.BlockSpec(memory_space=pltpu.SMEM)]
    vmem = pl.BlockSpec(memory_space=pltpu.VMEM)
    many = isinstance(out_shape, list)
    return pl.pallas_call(
        after(kernel, len(smem) + len(args), len(deps)),
        in_specs=smem + [vmem] * len(args) + [ANY] * len(deps),
        out_specs=[vmem] * len(out_shape) if many else vmem,
        out_shape=out_shape,
        compiler_params=pltpu.CompilerParams(vmem_limit_bytes=VMEM_LIMIT),
        cost_estimate=cost(1 << 28, 1 << 21),
        name=name,
    )(*([] if pos is None else [pos]), *args, *deps)


def turn_kernel(q_ref, o_ref, out_ref, half_ref):
    q, o = q_ref[...].T, o_ref[...].T
    out_ref[0] = q
    out_ref[1] = o
    half_ref[...] = jnp.where(lax.axis_index("scene") == 0, q, o)


def stack_kernel(n_sp, pos_ref, red_ref, *refs):
    pieces, far_ref, cut_refs = refs[: n_sp - 1], refs[n_sp - 1], refs[n_sp:]
    depth = far_ref.shape[2]
    z = pos_ref[0]
    for k, ref in enumerate(pieces):
        far_ref[k] = ref[...]
    parts = [red_ref[:, i * depth : (i + 1) * depth] for i in range(n_sp)]
    for k, ref in enumerate(cut_refs):
        ref[...] = choose(lax.rem(z + k, n_sp), parts)


def choose(index, values):
    result = values[0]
    for k in range(1, len(values)):
        result = jnp.where(index == k, values[k], result)
    return result


def place_pieces(z, pieces, out_ref, which):
    n_sp, depth = len(pieces), pieces[0].shape[1]
    for place in range(n_sp):
        index = lax.rem(z - place + n_sp, n_sp)
        out_ref[which, :, place * depth : (place + 1) * depth] = choose(index, pieces)


def pack_kernel(n_sp, pos_ref, own_ref, here_ref, there_ref, part_ref, *refs):
    parts, (out_ref, kv_ref) = refs[:-2], refs[-2:]
    feats, depth = own_ref.shape[1:]
    rows = part_ref.shape[0]
    blocks, width = rows // n_sp, depth * n_sp
    z, y = pos_ref[0], pos_ref[3]
    for which in range(2):
        pieces = [own_ref[which]] + [
            jnp.where(y == which, here_ref[k], there_ref[k]) for k in range(n_sp - 1)
        ]
        place_pieces(z, pieces, out_ref, which)
        lanes = slice(which * feats, (which + 1) * feats)
        sums = []
        for j in range(n_sp):
            total = part_ref[j * blocks : (j + 1) * blocks, lanes]
            for k, part in enumerate(parts, 1):
                at = (j - k) % n_sp
                total = total + part[at * blocks : (at + 1) * blocks, lanes].astype(F32)
            sums.append(total)
        kv = jnp.concatenate(sums, axis=0).T.astype(BF)
        out_ref[which, :, width:] = kv
        kv_ref[which] = kv


def pack_far_kernel(pos_ref, here_ref, there_ref, kv_ref, out_ref):
    n_sp, feats, depth = here_ref.shape
    z, y = pos_ref[0], pos_ref[3]
    for which in range(2):
        pieces = [jnp.where(y == which, here_ref[k], there_ref[k]) for k in range(n_sp)]
        place_pieces(z, pieces, out_ref, which)
        out_ref[which, :, n_sp * depth :] = kv_ref[which]


def project_kernel(k_ref, v_ref, own_ref, far_ref, *refs):
    red, (cols_ref, part_ref, low_ref, all_ref) = refs[:-4], refs[-4:]
    all_ref[0] = own_ref[...]
    all_ref[1:] = far_ref[...]
    feats = k_ref.shape[1]
    rows = jnp.concatenate([ref[...] for ref in red], axis=0)
    cols_ref[...] = rows
    for which, ref in ((0, k_ref), (1, v_ref)):
        lanes = slice(which * feats, (which + 1) * feats)
        part = mm(rows, ref[...])
        part_ref[:, lanes] = part
        low_ref[:, lanes] = part.astype(BF)


def grad_add_kernel(n_sp, pos_ref, grad_ref, grad_far_ref, dkv_ref, dkv_far_ref, *refs):
    g_refs, d_refs = refs[:n_sp], refs[n_sp:]
    z = pos_ref[0]
    blocks = d_refs[0].shape[0]
    for k in range(n_sp):
        at = lax.rem(z + k, n_sp)
        total = grad_ref[at].astype(F32) + grad_far_ref[at].astype(F32)
        g_refs[k][...] = total.astype(g_refs[k].dtype)
        rows = pl.ds(((n_sp - k) % n_sp) * blocks, blocks)
        total = dkv_ref[rows, :] + dkv_far_ref[rows, :].astype(F32)
        d_refs[k][...] = total.astype(d_refs[k].dtype)


def back_kernel(n_sp, pos_ref, *refs):
    rows, weights = refs[:n_sp], refs[n_sp : 2 * n_sp]
    low_ref, mine_ref, other_ref, d_red = refs[-4:]
    blocks = rows[0].shape[0]
    depth, feats = weights[0].shape[1:]
    z, c = pos_ref[0], pos_ref[1]
    total = rows[0][...]
    for part in rows[1:]:
        total = total + part[...].astype(F32)
    low = total.astype(BF)
    low_ref[...] = low
    terms = [mm(low[:, :feats], w[0], NT) + mm(low[:, feats:], w[1], NT) for w in weights]
    for place in range(n_sp):
        index = lax.rem(z - place + n_sp, n_sp)
        d_red[:, place * depth : (place + 1) * depth] = choose(index, terms)
    half = blocks // 2
    mine_ref[...] = d_red[pl.ds(pl.multiple_of(c * half, half), half), :].astype(BF)
    other_ref[...] = d_red[pl.ds(pl.multiple_of((1 - c) * half, half), half), :].astype(BF)


def pair_kernel(k_ref, v_ref, out_ref):
    out_ref[0] = k_ref[...]
    out_ref[1] = v_ref[...]


def copy_kernel(in_ref, out_ref):
    out_ref[...] = in_ref[...]


def kv_grad_kernel(grad_factor, red_ref, *refs):
    rows, (key_ref, value_ref) = refs[:-2], refs[-2:]
    feats = key_ref.shape[1]
    d_kv = jnp.concatenate([ref[...] for ref in rows], axis=0)
    both = mm(red_ref[...].T, d_kv) * grad_factor
    key_ref[...] = both[:, :feats]
    value_ref[...] = both[:, feats:]


def grad_sum_kernel(*refs):
    query_ref, out_ref = refs[-2:]
    for which, ref in ((0, query_ref), (1, out_ref)):
        total = refs[0][which].astype(F32)
        for part in refs[1:-2]:
            total = total + part[which].astype(F32)
        ref[...] = total.T


def on_device(
    tokens,
    norm_gain,
    reduce_gain,
    query_weight,
    key_weight,
    value_weight,
    out_weight,
    out_cotangent,
):
    n_sp, n_hd = lax.axis_size("sp"), lax.axis_size("hd")
    n_x = n_hd // 2
    z, h, y = lax.axis_index("sp"), lax.axis_index("hd"), lax.axis_index("scene")
    c = h % 2
    depth, feats = query_weight.shape
    width = tokens.shape[1]
    own = tokens.shape[0] // 2
    grad_factor = float(2 * own * n_sp) ** (-0.5)
    pos = jnp.stack([z, c, h, y]).astype(jnp.int32)
    others = range(1, n_sp)

    def low(*shape):
        return jax.ShapeDtypeStruct(shape, BF)

    def wide(*shape):
        return jax.ShapeDtypeStruct(shape, F32)

    def to_sp(value, k):
        return lax.ppermute(value, "sp", [(i, (i + k) % n_sp) for i in range(n_sp)])

    def to_hd(value, k):
        return lax.ppermute(value, "hd", [(i, (i + k) % n_hd) for i in range(n_hd)])

    def swap(value):
        return lax.ppermute(value, "hd", [(i, i ^ 1) for i in range(n_hd)])

    def cross(value):
        return lax.ppermute(value, "scene", [(0, 1), (1, 0)])

    block = pl.BlockSpec((depth, feats), lambda i: (0, 0))
    shard, half = pl.pallas_call(
        turn_kernel,
        grid=(1,),
        in_specs=[block, block],
        out_specs=[fixed((2, feats, depth)), fixed((feats, depth))],
        out_shape=[low(2, feats, depth), low(feats, depth)],
        compiler_params=params(1, TURN_LIMIT),
        name="turn",
    )(query_weight, out_weight)
    here = [to_sp(half, k) for k in others]
    normed, cot, reduced, r_unit, r_inverse = norm_and_pool(
        pos, tokens, out_cotangent, norm_gain, reduce_gain, (half,)
    )
    blocks = reduced.shape[0]
    far3, *cuts = small(
        functools.partial(stack_kernel, n_sp),
        "stack",
        [low(n_sp - 1, feats, depth)] + [low(blocks, depth)] * n_sp,
        reduced,
        *here,
        pos=pos,
    )
    there3 = cross(far3)

    both = (blocks * n_sp, 2 * feats)
    reduced_cols, kv_part, kv_low, all4 = small(
        project_kernel,
        "project",
        [low(blocks * n_sp, depth), wide(*both), low(*both), low(n_sp, feats, depth)],
        key_weight,
        value_weight,
        half,
        far3,
        cuts[0],
        *[to_sp(cuts[k], k) for k in others],
    )
    x_pieces = [to_hd(all4, 2 * k) for k in range(1, n_x)]
    packed, kv_own = small(
        functools.partial(pack_kernel, n_sp),
        "pack",
        [low(2, feats, width + blocks * n_sp), low(2, feats, blocks * n_sp)],
        shard,
        far3,
        there3,
        kv_part,
        *[to_sp(kv_low, k) for k in others],
        pos=pos,
        deps=tuple(x_pieces),
    )

    kv_weight = small(
        pair_kernel,
        "pair",
        low(2, depth, feats),
        key_weight,
        value_weight,
        deps=(packed,),
    )
    kv_weights = [kv_weight] + [to_sp(kv_weight, k) for k in others]
    third = (n_sp + 1) // 3

    attn0, dq0, grad0, dkv0 = attend(n_sp, normed, cot, packed, (kv_weight,), grad_factor, F32)
    packed_sib = swap(packed)
    kv_far = [to_hd(kv_own, 2 * k) for k in range(1, n_x)]
    attn1, dq1, grad1, dkv1 = attend(
        n_sp,
        normed,
        cot,
        packed_sib,
        (attn0,),
        grad_factor,
        BF,
    )
    attns, dqs, ws = [attn0, attn1], [dq0, dq1], [packed, packed_sib]
    grad1, dkv1 = swap(grad1), swap(dkv1)

    later = (attn1,)
    for piece, kv in zip(x_pieces, kv_far):
        packed_far = small(
            pack_far_kernel, "pack_far", low(*packed.shape), piece, cross(piece), kv, pos=pos, deps=later
        )
        ws += [packed_far, swap(packed_far)]

    attn, dq = attend(n_sp, normed, cot, ws[2], ())
    attns.append(attn)
    dqs.append(dq)
    grads = small(
        functools.partial(grad_add_kernel, n_sp),
        "grad_add",
        [wide(2, feats, depth)]
        + [low(2, feats, depth)] * (n_sp - 1)
        + [wide(blocks, 2 * feats)]
        + [low(blocks, 2 * feats)] * (n_sp - 1),
        grad0,
        grad1,
        dkv0,
        dkv1,
        pos=pos,
        deps=(attn, *kv_weights[1 : 1 + 2 * third]),
    )
    grads, d_rows = grads[:n_sp], grads[n_sp:]
    grads = [grads[0]] + [to_sp(grads[k], k) for k in others]
    ranked = sorted(others, key=lambda k: -min(k, n_sp - k))
    first, second, last = (
        tuple(grads[k] for k in ranked[i * third : (i + 1) * third if i < 2 else n_sp])
        for i in range(3)
    )
    later = (d_rows[0],)
    for w in ws[3:]:
        attn, dq = attend(n_sp, normed, cot, w, later)
        attns.append(attn)
        dqs.append(dq)

    dkv_rows, d_mine, d_other = pl.pallas_call(
        after(functools.partial(back_kernel, n_sp), 1 + 2 * n_sp, 1),
        in_specs=[pl.BlockSpec(memory_space=pltpu.SMEM)]
        + [pl.BlockSpec(memory_space=pltpu.VMEM)] * (2 * n_sp)
        + [ANY],
        out_specs=[pl.BlockSpec(memory_space=pltpu.VMEM)] * 3,
        out_shape=[low(blocks, 2 * feats), low(blocks // 2, width), low(blocks // 2, width)],
        scratch_shapes=[pltpu.VMEM((blocks, width), F32)],
        compiler_params=pltpu.CompilerParams(vmem_limit_bytes=VMEM_LIMIT),
        cost_estimate=cost(1 << 28, 1 << 21),
        name="back",
    )(
        pos,
        d_rows[0],
        *[to_sp(d_rows[k], k) for k in others],
        *kv_weights,
        attns[-1],
    )
    parts = [d_mine] + [to_hd(d_other if k % 2 else d_mine, k) for k in range(1, n_hd)]

    branch, other, d_heads = model_rows(pos, width, attns, dqs, ws, n_hd, (d_mine, *first))
    place = (1 - c) * own
    branch = lax.dynamic_update_slice_in_dim(branch, swap(other), place, 0)
    input_grad, other = input_rows(
        pos,
        norm_gain,
        reduce_gain,
        tokens,
        r_unit,
        r_inverse,
        d_heads,
        parts,
        n_hd,
        second + last,
    )
    input_grad = lax.dynamic_update_slice_in_dim(input_grad, swap(other), place, 0)
    query_grad, out_grad = small(
        grad_sum_kernel, "grad_sum", [wide(depth, feats)] * 2, *grads, deps=(other,)
    )
    dkv_rows = small(copy_kernel, "copy_rows", low(blocks, 2 * feats), dkv_rows, deps=(other,))
    dkv_all = [dkv_rows] + [to_sp(dkv_rows, k) for k in others]
    key_grad, value_grad = small(
        functools.partial(kv_grad_kernel, grad_factor),
        "kv_grad",
        [wide(depth, feats)] * 2,
        reduced_cols,
        *dkv_all,
    )
    return (branch, input_grad, query_grad, key_grad, value_grad, out_grad)


def solution(mesh):
    rows, whole, both = P(("scene", "sp"), None), P(), P("sp", "hd")
    out = P(("scene", "sp"), "hd")
    return jax.shard_map(
        on_device,
        mesh=mesh,
        in_specs=(rows, whole, whole, both, both, both, both, rows),
        out_specs=(out,) * 6,
        check_vma=False,
    )
```

```python
import functools
import jax
import jax.numpy as jnp
from jax import lax
from jax.experimental import pallas as pl
from jax.experimental.pallas import tpu as pltpu
from jax.sharding import PartitionSpec as P

HEAD_DIM = 64
POOL = 8
GRID_W = 128
EPS = 1e-06
BF = jnp.bfloat16
F32 = jnp.float32
VMEM_LIMIT = 24 * 1024 * 1024
NORM_LIMIT = 50 * 1024 * 1024
TURN_LIMIT = 58 * 1024 * 1024
ATTEND_LIMIT = 48 * 1024 * 1024

NN = (((1,), (0,)), ((), ()))
TN = (((0,), (0,)), ((), ()))
NT = (((1,), (1,)), ((), ()))


def mm(left, right, dims=NN):
    return lax.dot_general(left, right, dims, preferred_element_type=F32)


def cost(flops, moved):
    return pl.CostEstimate(flops=int(flops), bytes_accessed=int(moved), transcendentals=0)


ANY = pl.BlockSpec(memory_space=pl.ANY)


def after(kernel, inputs, deps):
    return lambda *refs: kernel(*refs[:inputs], *refs[inputs + deps :])


def params(axes=1, limit=VMEM_LIMIT):
    return pltpu.CompilerParams(
        dimension_semantics=("arbitrary",) * axes, vmem_limit_bytes=limit
    )


def norm_kernel(gain_ref, rgain_ref, tok_ref, normed_ref, red_ref, runit_ref, rinv_ref, pooled):
    row, col = pl.program_id(0), pl.program_id(1)
    cols, width = tok_ref.shape[1], tok_ref.shape[2]
    gain = gain_ref[...].astype(F32).reshape(1, 1, width)
    chunk = 2 * POOL
    sums = []
    for part in range(cols // chunk):
        at = slice(part * chunk, (part + 1) * chunk)
        v = tok_ref[:, at, :].astype(F32)
        d = v - jnp.mean(v, axis=-1, keepdims=True)
        inv = lax.rsqrt(jnp.mean(d * d, axis=-1, keepdims=True) + EPS)
        n = (d * inv * gain).astype(BF)
        normed_ref[:, at, :] = n
        acc = jnp.sum(n.astype(F32), axis=0)
        sums.append(jnp.sum(acc.reshape(2, POOL, width), axis=1))
    span = cols // POOL
    base = pl.multiple_of((row * pl.num_programs(1) + col) * span, span)
    pooled[pl.ds(base, span), :] = jnp.concatenate(sums, axis=0)

    @pl.when((row == pl.num_programs(0) - 1) & (col == pl.num_programs(1) - 1))
    def _():
        v = pooled[...] / (POOL * POOL)
        d = v - jnp.mean(v, axis=-1, keepdims=True)
        inv = lax.rsqrt(jnp.mean(d * d, axis=-1, keepdims=True) + EPS)
        unit = d * inv
        runit_ref[...] = unit
        rinv_ref[...] = jnp.broadcast_to(inv, rinv_ref.shape)
        red_ref[...] = (unit * rgain_ref[...].astype(F32).reshape(1, width)).astype(BF)


def norm_and_pool(tokens, norm_gain, reduce_gain, deps):
    count, width = tokens.shape
    grid_rows = count // GRID_W
    blocks = count // (POOL * POOL)
    cols = 64
    tok = pl.BlockSpec((POOL, cols, width), lambda i, j: (i, j, 0))
    whole = lambda shape: pl.BlockSpec(shape, lambda i, j: (0,) * len(shape))
    normed, reduced, unit, inverse = pl.pallas_call(
        after(norm_kernel, 3, len(deps)),
        grid=(grid_rows // POOL, GRID_W // cols),
        in_specs=[whole((width,)), whole((width,)), tok] + [ANY] * len(deps),
        out_specs=[tok, whole((blocks, width)), whole((blocks, width)), whole((blocks, 128))],
        out_shape=[
            jax.ShapeDtypeStruct((grid_rows, GRID_W, width), BF),
            jax.ShapeDtypeStruct((blocks, width), BF),
            jax.ShapeDtypeStruct((blocks, width), F32),
            jax.ShapeDtypeStruct((blocks, 128), F32),
        ],
        scratch_shapes=[pltpu.VMEM((blocks, width), F32)],
        compiler_params=params(2, NORM_LIMIT),
        cost_estimate=cost(40 * count * width, 10 * count * width),
        name="norm_pool",
    )(norm_gain, reduce_gain, tokens.reshape(grid_rows, GRID_W, width), *deps)
    return normed.reshape(count, width), reduced, unit, inverse


def spread_heads(w_ref, width, kbd, vbd, kbd_t, vbd_t):
    feats, blocks = w_ref.shape[1], w_ref.shape[2] - width
    row = lax.broadcasted_iota(jnp.int32, (feats, blocks), 0)
    k = w_ref[0, :, width:].astype(F32) * HEAD_DIM ** (-0.5)
    v = w_ref[1, :, width:].astype(F32)
    for head in range(feats // HEAD_DIM):
        mask = (row >= head * HEAD_DIM) & (row < (head + 1) * HEAD_DIM)
        lanes = slice(head * blocks, (head + 1) * blocks)
        kbd_t[:, lanes] = jnp.where(mask, k, 0.0).astype(BF)
        vbd_t[:, lanes] = jnp.where(mask, v, 0.0).astype(BF)
    kbd[...] = kbd_t[...].T
    vbd[...] = vbd_t[...].T


def attend_tile(x, y, w_ref, kbd, vbd, kbd_t, vbd_t):
    feats = w_ref.shape[1]
    heads = feats // HEAD_DIM
    blocks = kbd.shape[0] // heads
    q_t = mm(w_ref[0, :, : x.shape[1]], x, NT).astype(BF)
    da_t = mm(w_ref[1, :, : y.shape[1]], y, NT).astype(BF)
    scores = mm(kbd[...], q_t)
    d_chances = mm(vbd[...], da_t)
    low, d_low = [], []
    for head in range(heads):
        rows = slice(head * blocks, (head + 1) * blocks)
        s = scores[rows]
        e = jnp.exp(s - jnp.max(s, axis=0, keepdims=True))
        p = e * (1.0 / jnp.sum(e, axis=0, keepdims=True))
        dp = d_chances[rows]
        delta = jnp.sum(p * dp, axis=0, keepdims=True)
        low.append(p.astype(BF))
        d_low.append((p * (dp - delta)).astype(BF))
    low = jnp.concatenate(low, axis=0)
    d_low = jnp.concatenate(d_low, axis=0)
    attn_t = mm(vbd_t[...], low).astype(BF)
    dq_t = mm(kbd_t[...], d_low).astype(BF)
    return q_t, da_t, low, d_low, attn_t, dq_t


def head_mask(shape, head):
    lane = lax.broadcasted_iota(jnp.int32, shape, 1)
    return (lane >= head * HEAD_DIM) & (lane < (head + 1) * HEAD_DIM)


def head_scratch(heads, blocks, feats):
    return [
        pltpu.VMEM((heads * blocks, feats), BF),
        pltpu.VMEM((heads * blocks, feats), BF),
        pltpu.VMEM((feats, heads * blocks), BF),
        pltpu.VMEM((feats, heads * blocks), BF),
    ]


def attend_kernel(n_sp, grad_factor, pos_ref, x_ref, y_ref, w_ref, sib_ref, own_ref, *rest):
    step = pl.program_id(0)
    half = pl.num_programs(0) // 2
    feats, width = w_ref.shape[1], x_ref.shape[1]
    blocks = w_ref.shape[2] - width
    depth = width // n_sp
    g_refs, d_refs = rest[:n_sp], rest[n_sp : 2 * n_sp]
    heads_at = rest[2 * n_sp : 2 * n_sp + 4]
    dk_acc, dv_acc, g_acc = rest[2 * n_sp + 4 :]

    @pl.when(step == 0)
    def _():
        spread_heads(w_ref, width, *heads_at)
        dk_acc[...] = jnp.zeros_like(dk_acc)
        dv_acc[...] = jnp.zeros_like(dv_acc)
        g_acc[...] = jnp.zeros_like(g_acc)

    x, y = x_ref[...], y_ref[...]
    q_t, da_t, low, d_low, attn_t, dq_t = attend_tile(x, y, w_ref, *heads_at)

    @pl.when(step < half)
    def _():
        sib_ref[0] = attn_t
        sib_ref[1] = dq_t

    @pl.when(step >= half)
    def _():
        own_ref[0] = attn_t
        own_ref[1] = dq_t

    dk_acc[...] += mm(d_low, q_t, NT)
    dv_acc[...] += mm(low, da_t, NT)
    g_acc[0] += mm(dq_t, x)
    g_acc[1] += mm(attn_t, y)

    @pl.when(step == pl.num_programs(0) - 1)
    def _():
        z = pos_ref[0]
        dk = jnp.zeros((blocks, feats), F32)
        dv = jnp.zeros((blocks, feats), F32)
        for head in range(feats // HEAD_DIM):
            mask = head_mask((blocks, feats), head)
            rows = slice(head * blocks, (head + 1) * blocks)
            dk = dk + jnp.where(mask, dk_acc[rows, :], 0.0)
            dv = dv + jnp.where(mask, dv_acc[rows, :], 0.0)
        dk = dk * HEAD_DIM ** (-0.5)
        part = blocks // n_sp
        for k in range(n_sp):
            at = ((n_sp - k) % n_sp) * part
            d_refs[k][:, :feats] = dk[at : at + part].astype(d_refs[k].dtype)
            d_refs[k][:, feats:] = dv[at : at + part].astype(d_refs[k].dtype)
            for which in range(2):
                cuts = [g_acc[which, :, i * depth : (i + 1) * depth] for i in range(n_sp)]
                total = choose(lax.rem(z + k, n_sp), cuts) * grad_factor
                g_refs[k][which] = total.astype(g_refs[k].dtype)


def far_kernel(x_ref, y_ref, w_ref, out_ref, *heads_at):
    @pl.when(pl.program_id(0) == 0)
    def _():
        spread_heads(w_ref, x_ref.shape[1], *heads_at)

    out = attend_tile(x_ref[...], y_ref[...], w_ref, *heads_at)
    out_ref[0] = out[4]
    out_ref[1] = out[5]


def fixed(shape):
    return pl.BlockSpec(shape, lambda *i: (0,) * len(shape))


def attend(n_sp, pos, normed, cotangent, weights, grad_factor, deps):
    feats = weights.shape[1]
    count, width = normed.shape
    own = count // 2
    blocks = weights.shape[2] - width
    heads = feats // HEAD_DIM
    depth = width // n_sp
    tile = 256
    half = own // tile
    rows = pl.BlockSpec((tile, width), lambda i, p: (lax.rem(i + (1 - p[1]) * half, 2 * half), 0))
    sib = pl.BlockSpec((2, feats, tile), lambda i, p: (0, 0, jnp.minimum(i, half - 1)))
    mine = pl.BlockSpec((2, feats, tile), lambda i, p: (0, 0, jnp.maximum(i - half, 0)))
    g_shape, d_shape = (2, feats, depth), (blocks // n_sp, 2 * feats)
    out = pl.pallas_call(
        after(functools.partial(attend_kernel, n_sp, grad_factor), 4, len(deps)),
        grid_spec=pltpu.PrefetchScalarGridSpec(
            num_scalar_prefetch=1,
            grid=(2 * half,),
            in_specs=[rows, rows, fixed(weights.shape)] + [ANY] * len(deps),
            out_specs=[sib, mine] + [fixed(g_shape)] * n_sp + [fixed(d_shape)] * n_sp,
            scratch_shapes=head_scratch(heads, blocks, feats)
            + [
                pltpu.VMEM((heads * blocks, feats), F32),
                pltpu.VMEM((heads * blocks, feats), F32),
                pltpu.VMEM((2, feats, width), F32),
            ],
        ),
        out_shape=[
            jax.ShapeDtypeStruct((2, feats, own), BF),
            jax.ShapeDtypeStruct((2, feats, own), BF),
        ]
        + [jax.ShapeDtypeStruct(g_shape, F32 if k == 0 else BF) for k in range(n_sp)]
        + [jax.ShapeDtypeStruct(d_shape, F32 if k == 0 else BF) for k in range(n_sp)],
        compiler_params=params(1, ATTEND_LIMIT),
        cost_estimate=cost(
            16 * count * width * feats + 24 * count * heads * blocks * feats, 8 * count * width
        ),
        name="attend_grads",
    )(pos, normed, cotangent, weights, *deps)
    return out[0], out[1], out[2 : 2 + n_sp], out[2 + n_sp :]


def attend_far(pos, sibling, normed, cotangent, weights, deps):
    feats = weights.shape[1]
    count, width = normed.shape
    own = count // 2
    blocks = weights.shape[2] - width
    heads = feats // HEAD_DIM
    tile = 256
    half = own // tile
    if sibling:
        rows = pl.BlockSpec((tile, width), lambda i, p: (i + (1 - p[1]) * half, 0))
    else:
        rows = pl.BlockSpec((tile, width), lambda i, p: (i + p[1] * half, 0))
    return pl.pallas_call(
        after(lambda pos_ref, *refs: far_kernel(*refs), 4, len(deps)),
        grid_spec=pltpu.PrefetchScalarGridSpec(
            num_scalar_prefetch=1,
            grid=(half,),
            in_specs=[rows, rows, fixed(weights.shape)] + [ANY] * len(deps),
            out_specs=pl.BlockSpec((2, feats, tile), lambda i, p: (0, 0, i)),
            scratch_shapes=head_scratch(heads, blocks, feats),
        ),
        out_shape=jax.ShapeDtypeStruct((2, feats, own), BF),
        compiler_params=params(),
        cost_estimate=cost(
            8 * own * width * feats + 16 * own * heads * blocks * feats, 8 * own * width
        ),
        name="attend_far",
    )(pos, normed, cotangent, weights, *deps)


def rows_kernel(count, pos_ref, *refs):
    in_refs, refs = refs[:count], refs[count:]
    w_refs, (own_ref, sib_ref, heads_ref) = refs[:count], refs[count:]
    h = pos_ref[2]
    sib = h + 1 - 2 * lax.rem(h, 2)
    cols = own_ref.shape[1]
    rows = [ref[0].T for ref in in_refs]
    for ref, owner in ((own_ref, h), (sib_ref, sib)):
        lanes = pl.ds(pl.multiple_of(owner * cols, 128), cols)
        total = None
        for row, w_ref in zip(rows, w_refs):
            term = mm(row, w_ref[1, :, lanes]).astype(BF).astype(F32)
            total = term if total is None else total + term
        ref[...] = total.astype(BF)
    total = None
    for in_ref, w_ref in zip(in_refs, w_refs):
        term = mm(in_ref[1].T, w_ref[0, :, : heads_ref.shape[1]]).astype(BF).astype(F32)
        total = term if total is None else total + term
    heads_ref[...] = total


def model_rows(pos, width, pieces, weights, n_hd, deps):
    count = len(pieces)
    feats = pieces[0].shape[-2]
    own = pieces[0].shape[-1]
    cols = width // n_hd
    tile = 256
    steps = own // tile
    whole = lambda shape: pl.BlockSpec(shape, lambda i, p: (0,) * len(shape))
    t_spec = pl.BlockSpec((2, feats, tile), lambda i, p: (0, 0, i))
    return pl.pallas_call(
        after(functools.partial(rows_kernel, count), 2 * count + 1, len(deps)),
        grid_spec=pltpu.PrefetchScalarGridSpec(
            num_scalar_prefetch=1,
            grid=(steps,),
            in_specs=[t_spec] * count
            + [whole(w.shape) for w in weights]
            + [ANY] * len(deps),
            out_specs=[
                pl.BlockSpec((tile, cols), lambda i, p: (p[1] * steps + i, 0)),
                pl.BlockSpec((tile, cols), lambda i, p: (i, 0)),
                pl.BlockSpec((tile, width), lambda i, p: (i, 0)),
            ],
        ),
        out_shape=[
            jax.ShapeDtypeStruct((2 * own, cols), BF),
            jax.ShapeDtypeStruct((own, cols), BF),
            jax.ShapeDtypeStruct((own, width), F32),
        ],
        compiler_params=params(),
        cost_estimate=cost(4 * own * width * (width + 2 * cols), 12 * own * width),
        name="model_rows",
    )(pos, *pieces, *weights, *deps)


def input_kernel(count, pos_ref, gain_ref, rgain_ref, tok_ref, runit_ref, rinv_ref, heads_ref, *refs):
    d_refs, (own_ref, sib_ref, spread, u_ref) = refs[:count], refs[count:]
    width = tok_ref.shape[1]
    h = pos_ref[2]
    sib = h + 1 - 2 * lax.rem(h, 2)
    cols = own_ref.shape[1]

    @pl.when(pl.program_id(0) == 0)
    def _():
        groups = runit_ref.shape[0]
        total = d_refs[0][...].astype(F32)
        for ref in d_refs[1:]:
            total = total + ref[...].astype(F32)
        e = total * rgain_ref[...].astype(F32).reshape(1, width)
        unit = runit_ref[...]
        first = jnp.mean(e, axis=-1, keepdims=True)
        second = jnp.mean(e * unit, axis=-1, keepdims=True)
        d_pooled = rinv_ref[:, 0:1] * (e - first - unit * second) / (POOL * POOL)
        spread[...] = jnp.broadcast_to(d_pooled[:, None, :], (groups, POOL, width)).reshape(
            groups * POOL, width
        )

    gain = gain_ref[...].astype(F32).reshape(1, width)
    for part in range(tok_ref.shape[0] // GRID_W):
        at = slice(part * GRID_W, (part + 1) * GRID_W)
        v = tok_ref[at, :].astype(F32)
        d = v - jnp.mean(v, axis=-1, keepdims=True)
        inv = lax.rsqrt(jnp.mean(d * d, axis=-1, keepdims=True) + EPS)
        unit = d * inv
        e = (heads_ref[at, :] + spread[...]) * gain
        first = jnp.mean(e, axis=-1, keepdims=True)
        second = jnp.mean(e * unit, axis=-1, keepdims=True)
        u_ref[at, :] = inv * (e - first - unit * second)
    for ref, owner in ((own_ref, h), (sib_ref, sib)):
        ref[...] = u_ref[:, pl.ds(pl.multiple_of(owner * cols, 128), cols)].astype(BF)


def input_rows(pos, norm_gain, reduce_gain, tokens, unit, inverse, d_heads, parts, n_hd, deps):
    own, width = d_heads.shape
    cols = width // n_hd
    groups = parts[0].shape[0]
    tile = 256
    steps = own // tile
    whole = lambda shape: pl.BlockSpec(shape, lambda i, p: (0,) * len(shape))
    half = lambda shape: pl.BlockSpec(shape, lambda i, p: (p[1], 0))
    return pl.pallas_call(
        after(functools.partial(input_kernel, len(parts)), 7 + len(parts), len(deps)),
        grid_spec=pltpu.PrefetchScalarGridSpec(
            num_scalar_prefetch=1,
            grid=(steps,),
            in_specs=[
                whole((width,)),
                whole((width,)),
                pl.BlockSpec((tile, width), lambda i, p: (p[1] * steps + i, 0)),
                half((groups, width)),
                half((groups, 128)),
                pl.BlockSpec((tile, width), lambda i, p: (i, 0)),
            ]
            + [whole(part.shape) for part in parts]
            + [ANY] * len(deps),
            out_specs=[
                pl.BlockSpec((tile, cols), lambda i, p: (p[1] * steps + i, 0)),
                pl.BlockSpec((tile, cols), lambda i, p: (i, 0)),
            ],
            scratch_shapes=[
                pltpu.VMEM((groups * POOL, width), F32),
                pltpu.VMEM((tile, width), F32),
            ],
        ),
        out_shape=[
            jax.ShapeDtypeStruct((2 * own, cols), BF),
            jax.ShapeDtypeStruct((own, cols), BF),
        ],
        compiler_params=params(),
        cost_estimate=cost(40 * own * width, 16 * own * width),
        name="input_rows",
    )(
        pos,
        norm_gain,
        reduce_gain,
        tokens,
        unit,
        inverse,
        d_heads,
        *parts,
        *deps,
    )


def small(kernel, name, out_shape, *args, pos=None, deps=()):
    smem = [] if pos is None else [pl.BlockSpec(memory_space=pltpu.SMEM)]
    vmem = pl.BlockSpec(memory_space=pltpu.VMEM)
    many = isinstance(out_shape, list)
    return pl.pallas_call(
        after(kernel, len(smem) + len(args), len(deps)),
        in_specs=smem + [vmem] * len(args) + [ANY] * len(deps),
        out_specs=[vmem] * len(out_shape) if many else vmem,
        out_shape=out_shape,
        compiler_params=pltpu.CompilerParams(vmem_limit_bytes=VMEM_LIMIT),
        cost_estimate=cost(1 << 28, 1 << 21),
        name=name,
    )(*([] if pos is None else [pos]), *args, *deps)


def turn_kernel(q_ref, o_ref, out_ref, half_ref):
    q, o = q_ref[...].T, o_ref[...].T
    out_ref[0] = q
    out_ref[1] = o
    half_ref[...] = jnp.where(lax.axis_index("scene") == 0, q, o)


def stack_kernel(n_sp, pos_ref, red_ref, *refs):
    pieces, far_ref, cut_refs = refs[: n_sp - 1], refs[n_sp - 1], refs[n_sp:]
    depth = far_ref.shape[2]
    z = pos_ref[0]
    for k, ref in enumerate(pieces):
        far_ref[k] = ref[...]
    parts = [red_ref[:, i * depth : (i + 1) * depth] for i in range(n_sp)]
    for k, ref in enumerate(cut_refs):
        ref[...] = choose(lax.rem(z + k, n_sp), parts)


def choose(index, values):
    result = values[0]
    for k in range(1, len(values)):
        result = jnp.where(index == k, values[k], result)
    return result


def place_pieces(z, pieces, out_ref, which):
    n_sp, depth = len(pieces), pieces[0].shape[1]
    for place in range(n_sp):
        index = lax.rem(z - place + n_sp, n_sp)
        out_ref[which, :, place * depth : (place + 1) * depth] = choose(index, pieces)


def pack_kernel(n_sp, pos_ref, own_ref, here_ref, there_ref, part_ref, *refs):
    parts, (out_ref, kv_ref) = refs[:-2], refs[-2:]
    feats, depth = own_ref.shape[1:]
    rows = part_ref.shape[0]
    blocks, width = rows // n_sp, depth * n_sp
    z, y = pos_ref[0], pos_ref[3]
    for which in range(2):
        pieces = [own_ref[which]] + [
            jnp.where(y == which, here_ref[k], there_ref[k]) for k in range(n_sp - 1)
        ]
        place_pieces(z, pieces, out_ref, which)
        lanes = slice(which * feats, (which + 1) * feats)
        sums = []
        for j in range(n_sp):
            total = part_ref[j * blocks : (j + 1) * blocks, lanes]
            for k, part in enumerate(parts, 1):
                at = (j - k) % n_sp
                total = total + part[at * blocks : (at + 1) * blocks, lanes].astype(F32)
            sums.append(total)
        kv = jnp.concatenate(sums, axis=0).T.astype(BF)
        out_ref[which, :, width:] = kv
        kv_ref[which] = kv


def pack_far_kernel(pos_ref, here_ref, there_ref, kv_ref, out_ref):
    n_sp, feats, depth = here_ref.shape
    z, y = pos_ref[0], pos_ref[3]
    for which in range(2):
        pieces = [jnp.where(y == which, here_ref[k], there_ref[k]) for k in range(n_sp)]
        place_pieces(z, pieces, out_ref, which)
        out_ref[which, :, n_sp * depth :] = kv_ref[which]


def project_kernel(k_ref, v_ref, own_ref, far_ref, *refs):
    red, (cols_ref, part_ref, low_ref, all_ref) = refs[:-4], refs[-4:]
    all_ref[0] = own_ref[...]
    all_ref[1:] = far_ref[...]
    feats = k_ref.shape[1]
    rows = jnp.concatenate([ref[...] for ref in red], axis=0)
    cols_ref[...] = rows
    for which, ref in ((0, k_ref), (1, v_ref)):
        lanes = slice(which * feats, (which + 1) * feats)
        part = mm(rows, ref[...])
        part_ref[:, lanes] = part
        low_ref[:, lanes] = part.astype(BF)


def back_kernel(n_sp, pos_ref, key_ref, value_ref, here_ref, there_ref, *rows):
    rows, (low_ref, out_ref) = rows[:n_sp], rows[n_sp:]
    blocks = rows[0].shape[0]
    depth, feats = key_ref.shape
    z, y = pos_ref[0], pos_ref[3]
    total = rows[0][...]
    for part in rows[1:]:
        total = total + part[...].astype(F32)
    low = total.astype(BF)
    low_ref[...] = low
    terms = [mm(low[:, :feats], key_ref[...], NT) + mm(low[:, feats:], value_ref[...], NT)]
    for k in range(n_sp - 1):
        here, there = here_ref[k], there_ref[k]
        key, value = jnp.where(y == 0, here, there), jnp.where(y == 0, there, here)
        terms.append(mm(low[:, :feats], key, NT) + mm(low[:, feats:], value, NT))
    for place in range(n_sp):
        index = lax.rem(z - place + n_sp, n_sp)
        out_ref[:, place * depth : (place + 1) * depth] = choose(index, terms).astype(BF)


def half_kernel(k_ref, v_ref, out_ref):
    out_ref[...] = jnp.where(lax.axis_index("scene") == 0, k_ref[...], v_ref[...])


def gather_kernel(count, *refs):
    out_ref, passed = refs[2 * count], refs[2 * count + 1 :]
    for k in range(count):
        out_ref[k] = refs[k][...]
        passed[k][...] = refs[count + k][...]


def fold_kernel(pos_ref, low_ref, *refs):
    count = len(refs) - 6
    near_ref, d_ref, mine_ref, other_ref, both_ref, total = refs[count:]
    c = pos_ref[1]
    total[...] = low_ref[...].astype(F32)
    for ref in refs[:count]:
        total[...] += ref[...].astype(F32)
    half = mine_ref.shape[0]
    mine_ref[...] = total[pl.ds(pl.multiple_of(c * half, half), half), :]
    other_ref[...] = total[pl.ds(pl.multiple_of((1 - c) * half, half), half), :].astype(BF)
    blocks = near_ref.shape[0]
    both_ref[:blocks, :] = d_ref[...]
    both_ref[blocks:, :] = near_ref[...]


def kv_grad_kernel(n_sp, grad_factor, pos_ref, red_ref, d_ref, key_ref, value_ref):
    feats = key_ref.shape[1]
    blocks = d_ref.shape[0] // n_sp
    z = pos_ref[0]
    both = None
    for j in range(n_sp):
        index = lax.rem(z - lax.bitwise_xor(z, j) + n_sp, n_sp)
        red = red_ref[pl.ds(pl.multiple_of(index * blocks, blocks), blocks), :]
        term = mm(red.T, d_ref[j * blocks : (j + 1) * blocks, :])
        both = term if both is None else both + term
    key_ref[...] = both[:, :feats] * grad_factor
    value_ref[...] = both[:, feats:] * grad_factor


def grad_sum_kernel(*refs):
    query_ref, out_ref = refs[-2:]
    for which, ref in ((0, query_ref), (1, out_ref)):
        total = refs[0][which].astype(F32)
        for part in refs[1:-2]:
            total = total + part[which].astype(F32)
        ref[...] = total.T


def on_device(
    tokens,
    norm_gain,
    reduce_gain,
    query_weight,
    key_weight,
    value_weight,
    out_weight,
    out_cotangent,
):
    n_sp, n_hd = lax.axis_size("sp"), lax.axis_size("hd")
    n_x = n_hd // 2
    z, h, y = lax.axis_index("sp"), lax.axis_index("hd"), lax.axis_index("scene")
    c = h % 2
    depth, feats = query_weight.shape
    width = tokens.shape[1]
    own = tokens.shape[0] // 2
    grad_factor = float(2 * own * n_sp) ** (-0.5)
    pos = jnp.stack([z, c, h, y]).astype(jnp.int32)
    others = range(1, n_sp)

    def low(*shape):
        return jax.ShapeDtypeStruct(shape, BF)

    def wide(*shape):
        return jax.ShapeDtypeStruct(shape, F32)

    def to_sp(value, k):
        return lax.ppermute(value, "sp", [(i, (i + k) % n_sp) for i in range(n_sp)])

    def to_xor(value, bit):
        return lax.ppermute(value, "sp", [(i, i ^ bit) for i in range(n_sp)])

    def to_hd(value, k):
        return lax.ppermute(value, "hd", [(i, (i + k) % n_hd) for i in range(n_hd)])

    def swap(value):
        return lax.ppermute(value, "hd", [(i, i ^ 1) for i in range(n_hd)])

    def cross(value):
        return lax.ppermute(value, "scene", [(0, 1), (1, 0)])

    block = pl.BlockSpec((depth, feats), lambda i: (0, 0))
    shard, half = pl.pallas_call(
        turn_kernel,
        grid=(1,),
        in_specs=[block, block],
        out_specs=[fixed((2, feats, depth)), fixed((feats, depth))],
        out_shape=[low(2, feats, depth), low(feats, depth)],
        compiler_params=params(1, TURN_LIMIT),
        name="turn",
    )(query_weight, out_weight)
    here = [to_sp(half, k) for k in others]
    normed, reduced, r_unit, r_inverse = norm_and_pool(tokens, norm_gain, reduce_gain, (half,))
    blocks = reduced.shape[0]
    far3, *cuts = small(
        functools.partial(stack_kernel, n_sp),
        "stack",
        [low(n_sp - 1, feats, depth)] + [low(blocks, depth)] * n_sp,
        reduced,
        *here,
        pos=pos,
    )
    there3 = cross(far3)

    both = (blocks * n_sp, 2 * feats)
    reduced_cols, kv_part, kv_low, all4 = small(
        project_kernel,
        "project",
        [low(blocks * n_sp, depth), wide(*both), low(*both), low(n_sp, feats, depth)],
        key_weight,
        value_weight,
        half,
        far3,
        cuts[0],
        *[to_sp(cuts[k], k) for k in others],
    )
    x_pieces = [to_hd(all4, 2 * k) for k in range(1, n_x)]
    packed, kv_own = small(
        functools.partial(pack_kernel, n_sp),
        "pack",
        [low(2, feats, width + blocks * n_sp), low(2, feats, blocks * n_sp)],
        shard,
        far3,
        there3,
        kv_part,
        *[to_sp(kv_low, k) for k in others],
        pos=pos,
        deps=tuple(x_pieces),
    )

    kv_half = small(
        half_kernel, "half", low(depth, feats), key_weight, value_weight, deps=(packed,)
    )
    kv_here = [to_sp(kv_half, k) for k in others]
    kv_far = [to_hd(kv_own, 2 * k) for k in range(1, n_x)]

    for_sib, own_pair, grads, d_rows = attend(
        n_sp, pos, normed, out_cotangent, packed, grad_factor, (kv_half, *kv_far)
    )
    packed_sib = swap(packed)
    kv_here, *d_low = small(
        functools.partial(gather_kernel, n_sp - 1),
        "gather",
        [low(n_sp - 1, depth, feats)] + [low(blocks, 2 * feats)] * (n_sp - 1),
        *kv_here,
        *d_rows[1:],
        deps=(own_pair, packed_sib),
    )
    kv_there = cross(kv_here)
    d_rows = [d_rows[0]] + [to_sp(d_low[k - 1], k) for k in others]
    pairs, ws = [own_pair, swap(for_sib)], [packed, packed_sib]
    packed_far = [
        small(
            pack_far_kernel,
            "pack_far",
            low(*packed.shape),
            piece,
            cross(piece),
            kv,
            pos=pos,
            deps=(kv_here,),
        )
        for piece, kv in zip(x_pieces, kv_far)
    ]
    grads = [grads[0]] + [to_sp(grads[k], k) for k in others]
    far_sib = [attend_far(pos, True, normed, out_cotangent, w, ()) for w in packed_far]

    vmem = pl.BlockSpec(memory_space=pltpu.VMEM)
    smem = pl.BlockSpec(memory_space=pltpu.SMEM)
    grant = pltpu.CompilerParams(vmem_limit_bytes=VMEM_LIMIT)
    passed = len(far_sib)
    dkv_rows, d_red, *far_sib = pl.pallas_call(
        lambda *refs: back_kernel(n_sp, *refs[: 5 + n_sp], *refs[5 + n_sp + passed :][:2]),
        in_specs=[smem] + [vmem] * (4 + n_sp) + [ANY] * passed,
        out_specs=[vmem] * 2 + [ANY] * passed,
        out_shape=[low(blocks, 2 * feats), low(blocks, width)]
        + [low(*pair.shape) for pair in far_sib],
        input_output_aliases={5 + n_sp + k: 2 + k for k in range(passed)},
        compiler_params=grant,
        cost_estimate=cost(1 << 28, 1 << 21),
        name="back",
    )(pos, key_weight, value_weight, kv_here, kv_there, *d_rows, *far_sib)
    d_far = [to_hd(d_red, 2 * k) for k in range(1, n_x)]
    near = to_xor(dkv_rows, 1)
    ranked = sorted(others, key=lambda k: -min(k, n_sp - k))
    for w, pair in zip(packed_far, far_sib):
        mine = attend_far(pos, False, normed, out_cotangent, w, (d_red, pairs[1]))
        pairs += [mine, swap(pair)]
        ws += [w, swap(w)]
    d_mine, d_other, dkv_all = pl.pallas_call(
        lambda pos_ref, *refs: fold_kernel(pos_ref, *refs[: n_x + 2], *refs[n_x + 3 :]),
        in_specs=[smem] + [vmem] * (n_x + 2) + [ANY],
        out_specs=[vmem] * 3,
        out_shape=[
            wide(blocks // 2, width),
            low(blocks // 2, width),
            low(2 * blocks, 2 * feats),
        ],
        scratch_shapes=[pltpu.VMEM((blocks, width), F32)],
        compiler_params=grant,
        cost_estimate=cost(1 << 28, 1 << 21),
        name="fold",
    )(pos, d_red, *d_far, near, dkv_rows, pairs[-2])
    bit = 2
    while bit < n_sp:
        dkv_all = jnp.concatenate([dkv_all, to_xor(dkv_all, bit)])
        bit *= 2
    parts = [d_mine, swap(d_other)]
    branch, other, d_heads = model_rows(pos, width, pairs, ws, n_hd, (d_other, grads[ranked[0]]))
    place = (1 - c) * own
    branch = lax.dynamic_update_slice_in_dim(branch, swap(other), place, 0)
    input_grad, other = input_rows(
        pos,
        norm_gain,
        reduce_gain,
        tokens,
        r_unit,
        r_inverse,
        d_heads,
        parts,
        n_hd,
        (dkv_all, *(grads[k] for k in ranked[1:])),
    )
    input_grad = lax.dynamic_update_slice_in_dim(input_grad, swap(other), place, 0)
    query_grad, out_grad = small(
        grad_sum_kernel, "grad_sum", [wide(depth, feats)] * 2, *grads, deps=(other,)
    )
    key_grad, value_grad = small(
        functools.partial(kv_grad_kernel, n_sp, grad_factor),
        "kv_grad",
        [wide(depth, feats)] * 2,
        reduced_cols,
        dkv_all,
        pos=pos,
        deps=(other,),
    )
    return (branch, input_grad, query_grad, key_grad, value_grad, out_grad)


def solution(mesh):
    rows, whole, both = P(("scene", "sp"), None), P(), P("sp", "hd")
    out = P(("scene", "sp"), "hd")
    return jax.shard_map(
        on_device,
        mesh=mesh,
        in_specs=(rows, whole, whole, both, both, both, both, rows),
        out_specs=(out,) * 6,
        check_vma=False,
    )
```

```python
import functools
import jax
import jax.numpy as jnp
from jax import lax
from jax.experimental import pallas as pl
from jax.experimental.pallas import tpu as pltpu
from jax.sharding import PartitionSpec as P

HEAD_DIM = 64
POOL = 8
GRID_W = 128
EPS = 1e-06
BF = jnp.bfloat16
F32 = jnp.float32
VMEM_LIMIT = 24 * 1024 * 1024
NORM_LIMIT = 50 * 1024 * 1024
TURN_LIMIT = 58 * 1024 * 1024
ATTEND_LIMIT = 48 * 1024 * 1024

NN = (((1,), (0,)), ((), ()))
TN = (((0,), (0,)), ((), ()))
NT = (((1,), (1,)), ((), ()))


def mm(left, right, dims=NN):
    return lax.dot_general(left, right, dims, preferred_element_type=F32)


def cost(flops, moved):
    return pl.CostEstimate(flops=int(flops), bytes_accessed=int(moved), transcendentals=0)


ANY = pl.BlockSpec(memory_space=pl.ANY)


def after(kernel, inputs, deps):
    return lambda *refs: kernel(*refs[:inputs], *refs[inputs + deps :])


def params(axes=1, limit=VMEM_LIMIT):
    return pltpu.CompilerParams(
        dimension_semantics=("arbitrary",) * axes, vmem_limit_bytes=limit
    )


def norm_kernel(gain_ref, rgain_ref, tok_ref, normed_ref, red_ref, runit_ref, rinv_ref, pooled):
    row, col = pl.program_id(0), pl.program_id(1)
    cols, width = tok_ref.shape[1], tok_ref.shape[2]
    gain = gain_ref[...].astype(F32).reshape(1, 1, width)
    chunk = 2 * POOL
    sums = []
    for part in range(cols // chunk):
        at = slice(part * chunk, (part + 1) * chunk)
        v = tok_ref[:, at, :].astype(F32)
        d = v - jnp.mean(v, axis=-1, keepdims=True)
        inv = lax.rsqrt(jnp.mean(d * d, axis=-1, keepdims=True) + EPS)
        n = (d * inv * gain).astype(BF)
        normed_ref[:, at, :] = n
        acc = jnp.sum(n.astype(F32), axis=0)
        sums.append(jnp.sum(acc.reshape(2, POOL, width), axis=1))
    span = cols // POOL
    base = pl.multiple_of((row * pl.num_programs(1) + col) * span, span)
    pooled[pl.ds(base, span), :] = jnp.concatenate(sums, axis=0)

    @pl.when((row == pl.num_programs(0) - 1) & (col == pl.num_programs(1) - 1))
    def _():
        v = pooled[...] / (POOL * POOL)
        d = v - jnp.mean(v, axis=-1, keepdims=True)
        inv = lax.rsqrt(jnp.mean(d * d, axis=-1, keepdims=True) + EPS)
        unit = d * inv
        runit_ref[...] = unit
        rinv_ref[...] = jnp.broadcast_to(inv, rinv_ref.shape)
        red_ref[...] = (unit * rgain_ref[...].astype(F32).reshape(1, width)).astype(BF)


def norm_and_pool(tokens, norm_gain, reduce_gain, deps):
    count, width = tokens.shape
    grid_rows = count // GRID_W
    blocks = count // (POOL * POOL)
    cols = 64
    tok = pl.BlockSpec((POOL, cols, width), lambda i, j: (i, j, 0))
    whole = lambda shape: pl.BlockSpec(shape, lambda i, j: (0,) * len(shape))
    normed, reduced, unit, inverse = pl.pallas_call(
        after(norm_kernel, 3, len(deps)),
        grid=(grid_rows // POOL, GRID_W // cols),
        in_specs=[whole((width,)), whole((width,)), tok] + [ANY] * len(deps),
        out_specs=[tok, whole((blocks, width)), whole((blocks, width)), whole((blocks, 128))],
        out_shape=[
            jax.ShapeDtypeStruct((grid_rows, GRID_W, width), BF),
            jax.ShapeDtypeStruct((blocks, width), BF),
            jax.ShapeDtypeStruct((blocks, width), F32),
            jax.ShapeDtypeStruct((blocks, 128), F32),
        ],
        scratch_shapes=[pltpu.VMEM((blocks, width), F32)],
        compiler_params=params(2, NORM_LIMIT),
        cost_estimate=cost(40 * count * width, 10 * count * width),
        name="norm_pool",
    )(norm_gain, reduce_gain, tokens.reshape(grid_rows, GRID_W, width), *deps)
    return normed.reshape(count, width), reduced, unit, inverse


def spread_heads(w_ref, width, kbd, vbd, kbd_t, vbd_t):
    feats, blocks = w_ref.shape[1], w_ref.shape[2] - width
    row = lax.broadcasted_iota(jnp.int32, (feats, blocks), 0)
    k = w_ref[0, :, width:].astype(F32) * HEAD_DIM ** (-0.5)
    v = w_ref[1, :, width:].astype(F32)
    for head in range(feats // HEAD_DIM):
        mask = (row >= head * HEAD_DIM) & (row < (head + 1) * HEAD_DIM)
        lanes = slice(head * blocks, (head + 1) * blocks)
        kbd_t[:, lanes] = jnp.where(mask, k, 0.0).astype(BF)
        vbd_t[:, lanes] = jnp.where(mask, v, 0.0).astype(BF)
    kbd[...] = kbd_t[...].T
    vbd[...] = vbd_t[...].T


def attend_tile(x, y, w_ref, kbd, vbd, kbd_t, vbd_t):
    feats = w_ref.shape[1]
    heads = feats // HEAD_DIM
    blocks = kbd.shape[0] // heads
    q_t = mm(w_ref[0, :, : x.shape[1]], x, NT).astype(BF)
    da_t = mm(w_ref[1, :, : y.shape[1]], y, NT).astype(BF)
    scores = mm(kbd[...], q_t)
    d_chances = mm(vbd[...], da_t)
    low, d_low = [], []
    for head in range(heads):
        rows = slice(head * blocks, (head + 1) * blocks)
        s = scores[rows]
        e = jnp.exp(s - jnp.max(s, axis=0, keepdims=True))
        p = e * (1.0 / jnp.sum(e, axis=0, keepdims=True))
        dp = d_chances[rows]
        delta = jnp.sum(p * dp, axis=0, keepdims=True)
        low.append(p.astype(BF))
        d_low.append((p * (dp - delta)).astype(BF))
    low = jnp.concatenate(low, axis=0)
    d_low = jnp.concatenate(d_low, axis=0)
    attn_t = mm(vbd_t[...], low).astype(BF)
    dq_t = mm(kbd_t[...], d_low).astype(BF)
    return q_t, da_t, low, d_low, attn_t, dq_t


def head_mask(shape, head):
    lane = lax.broadcasted_iota(jnp.int32, shape, 1)
    return (lane >= head * HEAD_DIM) & (lane < (head + 1) * HEAD_DIM)


def head_scratch(heads, blocks, feats):
    return [
        pltpu.VMEM((heads * blocks, feats), BF),
        pltpu.VMEM((heads * blocks, feats), BF),
        pltpu.VMEM((feats, heads * blocks), BF),
        pltpu.VMEM((feats, heads * blocks), BF),
    ]


def attend_kernel(n_sp, grad_factor, pos_ref, x_ref, y_ref, w_ref, sib_ref, own_ref, *rest):
    step = pl.program_id(0)
    half = pl.num_programs(0) // 2
    feats, width = w_ref.shape[1], x_ref.shape[1]
    blocks = w_ref.shape[2] - width
    depth = width // n_sp
    g_refs, d_refs = rest[:n_sp], rest[n_sp : 2 * n_sp]
    heads_at = rest[2 * n_sp : 2 * n_sp + 4]
    dk_acc, dv_acc, g_acc = rest[2 * n_sp + 4 :]

    @pl.when(step == 0)
    def _():
        spread_heads(w_ref, width, *heads_at)
        dk_acc[...] = jnp.zeros_like(dk_acc)
        dv_acc[...] = jnp.zeros_like(dv_acc)
        g_acc[...] = jnp.zeros_like(g_acc)

    x, y = x_ref[...], y_ref[...]
    q_t, da_t, low, d_low, attn_t, dq_t = attend_tile(x, y, w_ref, *heads_at)

    dk_acc[...] += mm(d_low, q_t, NT)
    dv_acc[...] += mm(low, da_t, NT)
    g_acc[0] += mm(dq_t, x)
    g_acc[1] += mm(attn_t, y)

    @pl.when(step < half)
    def _():
        sib_ref[0] = attn_t
        sib_ref[1] = dq_t

    @pl.when(step >= half)
    def _():
        own_ref[0] = attn_t
        own_ref[1] = dq_t

    @pl.when(step == pl.num_programs(0) - 1)
    def _():
        z = pos_ref[0]
        dk = jnp.zeros((blocks, feats), F32)
        dv = jnp.zeros((blocks, feats), F32)
        for head in range(feats // HEAD_DIM):
            mask = head_mask((blocks, feats), head)
            rows = slice(head * blocks, (head + 1) * blocks)
            dk = dk + jnp.where(mask, dk_acc[rows, :], 0.0)
            dv = dv + jnp.where(mask, dv_acc[rows, :], 0.0)
        dk = dk * HEAD_DIM ** (-0.5)
        part = blocks // n_sp
        for k in range(n_sp):
            at = ((n_sp - k) % n_sp) * part
            d_refs[k][:, :feats] = dk[at : at + part].astype(d_refs[k].dtype)
            d_refs[k][:, feats:] = dv[at : at + part].astype(d_refs[k].dtype)
            for which in range(2):
                cuts = [g_acc[which, :, i * depth : (i + 1) * depth] for i in range(n_sp)]
                total = choose(lax.rem(z + k, n_sp), cuts) * grad_factor
                g_refs[k][which] = total.astype(g_refs[k].dtype)


def far_kernel(x_ref, y_ref, w_ref, out_ref, *heads_at):
    @pl.when(pl.program_id(0) == 0)
    def _():
        spread_heads(w_ref, x_ref.shape[1], *heads_at)

    out = attend_tile(x_ref[...], y_ref[...], w_ref, *heads_at)
    out_ref[0] = out[4]
    out_ref[1] = out[5]


def fixed(shape):
    return pl.BlockSpec(shape, lambda *i: (0,) * len(shape))


def attend(n_sp, pos, normed, cotangent, weights, grad_factor, deps):
    feats = weights.shape[1]
    count, width = normed.shape
    own = count // 2
    blocks = weights.shape[2] - width
    heads = feats // HEAD_DIM
    depth = width // n_sp
    tile = 256
    half = own // tile
    rows = pl.BlockSpec((tile, width), lambda i, p: (lax.rem(i + (1 - p[1]) * half, 2 * half), 0))
    sib = pl.BlockSpec((2, feats, tile), lambda i, p: (0, 0, jnp.minimum(i, half - 1)))
    mine = pl.BlockSpec((2, feats, tile), lambda i, p: (0, 0, jnp.maximum(i - half, 0)))
    g_shape, d_shape = (2, feats, depth), (blocks // n_sp, 2 * feats)
    out = pl.pallas_call(
        after(functools.partial(attend_kernel, n_sp, grad_factor), 4, len(deps)),
        grid_spec=pltpu.PrefetchScalarGridSpec(
            num_scalar_prefetch=1,
            grid=(2 * half,),
            in_specs=[rows, rows, fixed(weights.shape)] + [ANY] * len(deps),
            out_specs=[sib, mine] + [fixed(g_shape)] * n_sp + [fixed(d_shape)] * n_sp,
            scratch_shapes=head_scratch(heads, blocks, feats)
            + [
                pltpu.VMEM((heads * blocks, feats), F32),
                pltpu.VMEM((heads * blocks, feats), F32),
                pltpu.VMEM((2, feats, width), F32),
            ],
        ),
        out_shape=[
            jax.ShapeDtypeStruct((2, feats, own), BF),
            jax.ShapeDtypeStruct((2, feats, own), BF),
        ]
        + [jax.ShapeDtypeStruct(g_shape, F32 if k == 0 else BF) for k in range(n_sp)]
        + [jax.ShapeDtypeStruct(d_shape, F32 if k == 0 else BF) for k in range(n_sp)],
        compiler_params=params(1, ATTEND_LIMIT),
        cost_estimate=cost(
            16 * count * width * feats + 24 * count * heads * blocks * feats, 8 * count * width
        ),
        name="attend_grads",
    )(pos, normed, cotangent, weights, *deps)
    return out[0], out[1], out[2 : 2 + n_sp], out[2 + n_sp :]


def attend_far(pos, sibling, normed, cotangent, weights, deps):
    feats = weights.shape[1]
    count, width = normed.shape
    own = count // 2
    blocks = weights.shape[2] - width
    heads = feats // HEAD_DIM
    tile = 256
    half = own // tile
    if sibling:
        rows = pl.BlockSpec((tile, width), lambda i, p: (i + (1 - p[1]) * half, 0))
    else:
        rows = pl.BlockSpec((tile, width), lambda i, p: (i + p[1] * half, 0))
    return pl.pallas_call(
        after(lambda pos_ref, *refs: far_kernel(*refs), 4, len(deps)),
        grid_spec=pltpu.PrefetchScalarGridSpec(
            num_scalar_prefetch=1,
            grid=(half,),
            in_specs=[rows, rows, fixed(weights.shape)] + [ANY] * len(deps),
            out_specs=pl.BlockSpec((2, feats, tile), lambda i, p: (0, 0, i)),
            scratch_shapes=head_scratch(heads, blocks, feats),
        ),
        out_shape=jax.ShapeDtypeStruct((2, feats, own), BF),
        compiler_params=params(1, ATTEND_LIMIT),
        cost_estimate=cost(
            8 * own * width * feats + 16 * own * heads * blocks * feats, 8 * own * width
        ),
        name="attend_far",
    )(pos, normed, cotangent, weights, *deps)


def rows_kernel(count, pos_ref, *refs):
    in_refs, refs = refs[:count], refs[count:]
    w_refs, (own_ref, sib_ref, heads_ref) = refs[:count], refs[count:]
    h = pos_ref[2]
    sib = h + 1 - 2 * lax.rem(h, 2)
    cols = own_ref.shape[1]
    rows = [ref[0].T for ref in in_refs]
    for ref, owner in ((own_ref, h), (sib_ref, sib)):
        lanes = pl.ds(pl.multiple_of(owner * cols, 128), cols)
        total = None
        for row, w_ref in zip(rows, w_refs):
            term = mm(row, w_ref[1, :, lanes]).astype(BF).astype(F32)
            total = term if total is None else total + term
        ref[...] = total.astype(BF)
    total = None
    for in_ref, w_ref in zip(in_refs, w_refs):
        term = mm(in_ref[1].T, w_ref[0, :, : heads_ref.shape[1]]).astype(BF).astype(F32)
        total = term if total is None else total + term
    heads_ref[...] = total


def model_rows(pos, width, pieces, weights, n_hd, deps):
    count = len(pieces)
    feats = pieces[0].shape[-2]
    own = pieces[0].shape[-1]
    cols = width // n_hd
    tile = 256
    steps = own // tile
    whole = lambda shape: pl.BlockSpec(shape, lambda i, p: (0,) * len(shape))
    t_spec = pl.BlockSpec((2, feats, tile), lambda i, p: (0, 0, i))
    return pl.pallas_call(
        after(functools.partial(rows_kernel, count), 2 * count + 1, len(deps)),
        grid_spec=pltpu.PrefetchScalarGridSpec(
            num_scalar_prefetch=1,
            grid=(steps,),
            in_specs=[t_spec] * count
            + [whole(w.shape) for w in weights]
            + [ANY] * len(deps),
            out_specs=[
                pl.BlockSpec((tile, cols), lambda i, p: (p[1] * steps + i, 0)),
                pl.BlockSpec((tile, cols), lambda i, p: (i, 0)),
                pl.BlockSpec((tile, width), lambda i, p: (i, 0)),
            ],
        ),
        out_shape=[
            jax.ShapeDtypeStruct((2 * own, cols), BF),
            jax.ShapeDtypeStruct((own, cols), BF),
            jax.ShapeDtypeStruct((own, width), F32),
        ],
        compiler_params=params(),
        cost_estimate=cost(4 * own * width * (width + 2 * cols), 12 * own * width),
        name="model_rows",
    )(pos, *pieces, *weights, *deps)


def input_kernel(count, pos_ref, gain_ref, rgain_ref, tok_ref, runit_ref, rinv_ref, heads_ref, *refs):
    d_refs, (own_ref, sib_ref, spread, u_ref) = refs[:count], refs[count:]
    width = tok_ref.shape[1]
    h = pos_ref[2]
    sib = h + 1 - 2 * lax.rem(h, 2)
    cols = own_ref.shape[1]

    @pl.when(pl.program_id(0) == 0)
    def _():
        groups = runit_ref.shape[0]
        total = d_refs[0][...].astype(F32)
        for ref in d_refs[1:]:
            total = total + ref[...].astype(F32)
        e = total * rgain_ref[...].astype(F32).reshape(1, width)
        unit = runit_ref[...]
        first = jnp.mean(e, axis=-1, keepdims=True)
        second = jnp.mean(e * unit, axis=-1, keepdims=True)
        d_pooled = rinv_ref[:, 0:1] * (e - first - unit * second) / (POOL * POOL)
        spread[...] = jnp.broadcast_to(d_pooled[:, None, :], (groups, POOL, width)).reshape(
            groups * POOL, width
        )

    gain = gain_ref[...].astype(F32).reshape(1, width)
    for part in range(tok_ref.shape[0] // GRID_W):
        at = slice(part * GRID_W, (part + 1) * GRID_W)
        v = tok_ref[at, :].astype(F32)
        d = v - jnp.mean(v, axis=-1, keepdims=True)
        inv = lax.rsqrt(jnp.mean(d * d, axis=-1, keepdims=True) + EPS)
        unit = d * inv
        e = (heads_ref[at, :] + spread[...]) * gain
        first = jnp.mean(e, axis=-1, keepdims=True)
        second = jnp.mean(e * unit, axis=-1, keepdims=True)
        u_ref[at, :] = inv * (e - first - unit * second)
    for ref, owner in ((own_ref, h), (sib_ref, sib)):
        ref[...] = u_ref[:, pl.ds(pl.multiple_of(owner * cols, 128), cols)].astype(BF)


def input_rows(pos, norm_gain, reduce_gain, tokens, unit, inverse, d_heads, parts, n_hd, deps):
    own, width = d_heads.shape
    cols = width // n_hd
    groups = parts[0].shape[0]
    tile = 256
    steps = own // tile
    whole = lambda shape: pl.BlockSpec(shape, lambda i, p: (0,) * len(shape))
    half = lambda shape: pl.BlockSpec(shape, lambda i, p: (p[1], 0))
    return pl.pallas_call(
        after(functools.partial(input_kernel, len(parts)), 7 + len(parts), len(deps)),
        grid_spec=pltpu.PrefetchScalarGridSpec(
            num_scalar_prefetch=1,
            grid=(steps,),
            in_specs=[
                whole((width,)),
                whole((width,)),
                pl.BlockSpec((tile, width), lambda i, p: (p[1] * steps + i, 0)),
                half((groups, width)),
                half((groups, 128)),
                pl.BlockSpec((tile, width), lambda i, p: (i, 0)),
            ]
            + [whole(part.shape) for part in parts]
            + [ANY] * len(deps),
            out_specs=[
                pl.BlockSpec((tile, cols), lambda i, p: (p[1] * steps + i, 0)),
                pl.BlockSpec((tile, cols), lambda i, p: (i, 0)),
            ],
            scratch_shapes=[
                pltpu.VMEM((groups * POOL, width), F32),
                pltpu.VMEM((tile, width), F32),
            ],
        ),
        out_shape=[
            jax.ShapeDtypeStruct((2 * own, cols), BF),
            jax.ShapeDtypeStruct((own, cols), BF),
        ],
        compiler_params=params(),
        cost_estimate=cost(40 * own * width, 16 * own * width),
        name="input_rows",
    )(
        pos,
        norm_gain,
        reduce_gain,
        tokens,
        unit,
        inverse,
        d_heads,
        *parts,
        *deps,
    )


def small(kernel, name, out_shape, *args, pos=None, deps=()):
    smem = [] if pos is None else [pl.BlockSpec(memory_space=pltpu.SMEM)]
    vmem = pl.BlockSpec(memory_space=pltpu.VMEM)
    many = isinstance(out_shape, list)
    return pl.pallas_call(
        after(kernel, len(smem) + len(args), len(deps)),
        in_specs=smem + [vmem] * len(args) + [ANY] * len(deps),
        out_specs=[vmem] * len(out_shape) if many else vmem,
        out_shape=out_shape,
        compiler_params=pltpu.CompilerParams(vmem_limit_bytes=VMEM_LIMIT),
        cost_estimate=cost(1 << 28, 1 << 21),
        name=name,
    )(*([] if pos is None else [pos]), *args, *deps)


def turn_kernel(q_ref, o_ref, out_ref, half_ref, tag_ref):
    tag_ref[...] = jnp.zeros_like(tag_ref)
    q, o = q_ref[...].T, o_ref[...].T
    out_ref[0] = q
    out_ref[1] = o
    half_ref[...] = jnp.where(lax.axis_index("scene") == 0, q, o)


def stack_kernel(n_sp, pos_ref, red_ref, *refs):
    pieces, far_ref, cut_refs = refs[: n_sp - 1], refs[n_sp - 1], refs[n_sp:]
    depth = far_ref.shape[2]
    z = pos_ref[0]
    for k, ref in enumerate(pieces):
        far_ref[k] = ref[...]
    parts = [red_ref[:, i * depth : (i + 1) * depth] for i in range(n_sp)]
    for k, ref in enumerate(cut_refs):
        ref[...] = choose(lax.rem(z + k, n_sp), parts)


def choose(index, values):
    result = values[0]
    for k in range(1, len(values)):
        result = jnp.where(index == k, values[k], result)
    return result


def place_pieces(z, pieces, out_ref, which):
    n_sp, depth = len(pieces), pieces[0].shape[1]
    for place in range(n_sp):
        index = lax.rem(z - place + n_sp, n_sp)
        out_ref[which, :, place * depth : (place + 1) * depth] = choose(index, pieces)


def pack_kernel(n_sp, pos_ref, own_ref, here_ref, there_ref, part_ref, *refs):
    parts, (out_ref, kv_ref) = refs[:-2], refs[-2:]
    feats, depth = own_ref.shape[1:]
    rows = part_ref.shape[0]
    blocks, width = rows // n_sp, depth * n_sp
    z, y = pos_ref[0], pos_ref[3]
    for which in range(2):
        pieces = [own_ref[which]] + [
            jnp.where(y == which, here_ref[k], there_ref[k]) for k in range(n_sp - 1)
        ]
        place_pieces(z, pieces, out_ref, which)
        lanes = slice(which * feats, (which + 1) * feats)
        sums = []
        for j in range(n_sp):
            total = part_ref[j * blocks : (j + 1) * blocks, lanes]
            for k, part in enumerate(parts, 1):
                at = (j - k) % n_sp
                total = total + part[at * blocks : (at + 1) * blocks, lanes].astype(F32)
            sums.append(total)
        kv = jnp.concatenate(sums, axis=0).T.astype(BF)
        out_ref[which, :, width:] = kv
        kv_ref[which] = kv


def pack_far_kernel(pos_ref, here_ref, there_ref, kv_ref, out_ref):
    n_sp, feats, depth = here_ref.shape
    z, y = pos_ref[0], pos_ref[3]
    for which in range(2):
        pieces = [jnp.where(y == which, here_ref[k], there_ref[k]) for k in range(n_sp)]
        place_pieces(z, pieces, out_ref, which)
        out_ref[which, :, n_sp * depth :] = kv_ref[which]


def project_kernel(k_ref, v_ref, own_ref, far_ref, *refs):
    red, (cols_ref, part_ref, low_ref, all_ref) = refs[:-4], refs[-4:]
    all_ref[0] = own_ref[...]
    all_ref[1:] = far_ref[...]
    feats = k_ref.shape[1]
    rows = jnp.concatenate([ref[...] for ref in red], axis=0)
    cols_ref[...] = rows
    for which, ref in ((0, k_ref), (1, v_ref)):
        lanes = slice(which * feats, (which + 1) * feats)
        part = mm(rows, ref[...])
        part_ref[:, lanes] = part
        low_ref[:, lanes] = part.astype(BF)


def back_kernel(n_sp, pos_ref, key_ref, value_ref, here_ref, there_ref, *rows):
    rows, (low_ref, out_ref) = rows[:n_sp], rows[n_sp:]
    blocks = rows[0].shape[0]
    depth, feats = key_ref.shape
    z, y = pos_ref[0], pos_ref[3]
    total = rows[0][...]
    for part in rows[1:]:
        total = total + part[...].astype(F32)
    low = total.astype(BF)
    low_ref[...] = low
    terms = [mm(low[:, :feats], key_ref[...], NT) + mm(low[:, feats:], value_ref[...], NT)]
    for k in range(n_sp - 1):
        here, there = here_ref[k], there_ref[k]
        key, value = jnp.where(y == 0, here, there), jnp.where(y == 0, there, here)
        terms.append(mm(low[:, :feats], key, NT) + mm(low[:, feats:], value, NT))
    for place in range(n_sp):
        index = lax.rem(z - place + n_sp, n_sp)
        out_ref[:, place * depth : (place + 1) * depth] = choose(index, terms).astype(BF)


def half_kernel(k_ref, v_ref, out_ref):
    out_ref[...] = jnp.where(lax.axis_index("scene") == 0, k_ref[...], v_ref[...])


def gather_kernel(count, *refs):
    out_ref, passed = refs[2 * count], refs[2 * count + 1 :]
    for k in range(count):
        out_ref[k] = refs[k][...]
        passed[k][...] = refs[count + k][...]


def fold_kernel(pos_ref, low_ref, *refs):
    count = len(refs) - 6
    near_ref, d_ref, mine_ref, other_ref, both_ref, total = refs[count:]
    c = pos_ref[1]
    total[...] = low_ref[...].astype(F32)
    for ref in refs[:count]:
        total[...] += ref[...].astype(F32)
    half = mine_ref.shape[0]
    mine_ref[...] = total[pl.ds(pl.multiple_of(c * half, half), half), :]
    other_ref[...] = total[pl.ds(pl.multiple_of((1 - c) * half, half), half), :].astype(BF)
    blocks = near_ref.shape[0]
    both_ref[:blocks, :] = d_ref[...]
    both_ref[blocks:, :] = near_ref[...]


def kv_grad_kernel(n_sp, grad_factor, pos_ref, red_ref, d_ref, key_ref, value_ref):
    feats = key_ref.shape[1]
    blocks = d_ref.shape[0] // n_sp
    z = pos_ref[0]
    both = None
    for j in range(n_sp):
        index = lax.rem(z - lax.bitwise_xor(z, j) + n_sp, n_sp)
        red = red_ref[pl.ds(pl.multiple_of(index * blocks, blocks), blocks), :]
        term = mm(red.T, d_ref[j * blocks : (j + 1) * blocks, :])
        both = term if both is None else both + term
    key_ref[...] = both[:, :feats] * grad_factor
    value_ref[...] = both[:, feats:] * grad_factor


def grad_sum_kernel(*refs):
    query_ref, out_ref = refs[-2:]
    for which, ref in ((0, query_ref), (1, out_ref)):
        total = refs[0][which].astype(F32)
        for part in refs[1:-2]:
            total = total + part[which].astype(F32)
        ref[...] = total.T


def on_device(
    tokens,
    norm_gain,
    reduce_gain,
    query_weight,
    key_weight,
    value_weight,
    out_weight,
    out_cotangent,
):
    n_sp, n_hd = lax.axis_size("sp"), lax.axis_size("hd")
    n_x = n_hd // 2
    z, h, y = lax.axis_index("sp"), lax.axis_index("hd"), lax.axis_index("scene")
    c = h % 2
    depth, feats = query_weight.shape
    width = tokens.shape[1]
    own = tokens.shape[0] // 2
    grad_factor = float(2 * own * n_sp) ** (-0.5)
    pos = jnp.stack([z, c, h, y]).astype(jnp.int32)
    others = range(1, n_sp)

    def low(*shape):
        return jax.ShapeDtypeStruct(shape, BF)

    def wide(*shape):
        return jax.ShapeDtypeStruct(shape, F32)

    def to_sp(value, k):
        return lax.ppermute(value, "sp", [(i, (i + k) % n_sp) for i in range(n_sp)])

    def to_xor(value, bit):
        return lax.ppermute(value, "sp", [(i, i ^ bit) for i in range(n_sp)])

    def to_hd(value, k):
        return lax.ppermute(value, "hd", [(i, (i + k) % n_hd) for i in range(n_hd)])

    def swap(value):
        return lax.ppermute(value, "hd", [(i, i ^ 1) for i in range(n_hd)])

    def cross(value):
        return lax.ppermute(value, "scene", [(0, 1), (1, 0)])

    block = pl.BlockSpec((depth, feats), lambda i: (0, 0))
    shard, half, tag = pl.pallas_call(
        turn_kernel,
        grid=(1,),
        in_specs=[block, block],
        out_specs=[fixed((2, feats, depth)), fixed((feats, depth)), fixed((8, 128))],
        out_shape=[low(2, feats, depth), low(feats, depth), wide(8, 128)],
        compiler_params=params(1, TURN_LIMIT),
        name="turn",
    )(query_weight, out_weight)
    here = [to_sp(half, k) for k in others]
    normed, reduced, r_unit, r_inverse = norm_and_pool(tokens, norm_gain, reduce_gain, (tag,))
    blocks = reduced.shape[0]
    far3, *cuts = small(
        functools.partial(stack_kernel, n_sp),
        "stack",
        [low(n_sp - 1, feats, depth)] + [low(blocks, depth)] * n_sp,
        reduced,
        *here,
        pos=pos,
    )
    there3 = cross(far3)

    both = (blocks * n_sp, 2 * feats)
    reduced_cols, kv_part, kv_low, all4 = small(
        project_kernel,
        "project",
        [low(blocks * n_sp, depth), wide(*both), low(*both), low(n_sp, feats, depth)],
        key_weight,
        value_weight,
        half,
        far3,
        cuts[0],
        *[to_sp(cuts[k], k) for k in others],
    )
    x_pieces = [to_hd(all4, 2 * k) for k in range(1, n_x)]
    packed, kv_own = small(
        functools.partial(pack_kernel, n_sp),
        "pack",
        [low(2, feats, width + blocks * n_sp), low(2, feats, blocks * n_sp)],
        shard,
        far3,
        there3,
        kv_part,
        *[to_sp(kv_low, k) for k in others],
        pos=pos,
        deps=tuple(x_pieces),
    )

    kv_half = small(
        half_kernel, "half", low(depth, feats), key_weight, value_weight, deps=(packed,)
    )
    kv_here = [to_sp(kv_half, k) for k in others]
    kv_far = [to_hd(kv_own, 2 * k) for k in range(1, n_x)]

    for_sib, own_pair, grads, d_rows = attend(
        n_sp, pos, normed, out_cotangent, packed, grad_factor, (kv_half, *kv_far)
    )
    packed_sib = swap(packed)
    kv_here, *d_low = small(
        functools.partial(gather_kernel, n_sp - 1),
        "gather",
        [low(n_sp - 1, depth, feats)] + [low(blocks, 2 * feats)] * (n_sp - 1),
        *kv_here,
        *d_rows[1:],
        deps=(own_pair, packed_sib),
    )
    kv_there = cross(kv_here)
    d_rows = [d_rows[0]] + [to_sp(d_low[k - 1], k) for k in others]
    pairs, ws = [own_pair, swap(for_sib)], [packed, packed_sib]
    packed_far = [
        small(
            pack_far_kernel,
            "pack_far",
            low(*packed.shape),
            piece,
            cross(piece),
            kv,
            pos=pos,
            deps=(kv_here,),
        )
        for piece, kv in zip(x_pieces, kv_far)
    ]
    grads = [grads[0]] + [to_sp(grads[k], k) for k in others]
    far_sib = [attend_far(pos, True, normed, out_cotangent, w, ()) for w in packed_far]

    vmem = pl.BlockSpec(memory_space=pltpu.VMEM)
    smem = pl.BlockSpec(memory_space=pltpu.SMEM)
    grant = pltpu.CompilerParams(vmem_limit_bytes=VMEM_LIMIT)
    passed = len(far_sib)
    dkv_rows, d_red, *far_sib = pl.pallas_call(
        lambda *refs: back_kernel(n_sp, *refs[: 5 + n_sp], *refs[5 + n_sp + passed :][:2]),
        in_specs=[smem] + [vmem] * (4 + n_sp) + [ANY] * passed,
        out_specs=[vmem] * 2 + [ANY] * passed,
        out_shape=[low(blocks, 2 * feats), low(blocks, width)]
        + [low(*pair.shape) for pair in far_sib],
        input_output_aliases={5 + n_sp + k: 2 + k for k in range(passed)},
        compiler_params=grant,
        cost_estimate=cost(1 << 28, 1 << 21),
        name="back",
    )(pos, key_weight, value_weight, kv_here, kv_there, *d_rows, *far_sib)
    d_far = [to_hd(d_red, 2 * k) for k in range(1, n_x)]
    near = to_xor(dkv_rows, 1)
    for w, pair in zip(packed_far, far_sib):
        mine = attend_far(pos, False, normed, out_cotangent, w, (d_red, pairs[1]))
        pairs += [mine, swap(pair)]
        ws += [w, swap(w)]
    d_mine, d_other, dkv_all = pl.pallas_call(
        lambda pos_ref, *refs: fold_kernel(pos_ref, *refs[: n_x + 2], *refs[n_x + 3 :]),
        in_specs=[smem] + [vmem] * (n_x + 2) + [ANY],
        out_specs=[vmem] * 3,
        out_shape=[
            wide(blocks // 2, width),
            low(blocks // 2, width),
            low(2 * blocks, 2 * feats),
        ],
        scratch_shapes=[pltpu.VMEM((blocks, width), F32)],
        compiler_params=grant,
        cost_estimate=cost(1 << 28, 1 << 21),
        name="fold",
    )(pos, d_red, *d_far, near, dkv_rows, pairs[-2])
    bit = 2
    while bit < n_sp:
        dkv_all = jnp.concatenate([dkv_all, to_xor(dkv_all, bit)])
        bit *= 2
    parts = [d_mine, swap(d_other)]
    branch, other, d_heads = model_rows(pos, width, pairs, ws, n_hd, (d_other,))
    place = (1 - c) * own
    branch = lax.dynamic_update_slice_in_dim(branch, swap(other), place, 0)
    input_grad, other = input_rows(
        pos,
        norm_gain,
        reduce_gain,
        tokens,
        r_unit,
        r_inverse,
        d_heads,
        parts,
        n_hd,
        (dkv_all, *grads[1:]),
    )
    input_grad = lax.dynamic_update_slice_in_dim(input_grad, swap(other), place, 0)
    query_grad, out_grad = small(
        grad_sum_kernel, "grad_sum", [wide(depth, feats)] * 2, *grads, deps=(other,)
    )
    key_grad, value_grad = small(
        functools.partial(kv_grad_kernel, n_sp, grad_factor),
        "kv_grad",
        [wide(depth, feats)] * 2,
        reduced_cols,
        dkv_all,
        pos=pos,
        deps=(other,),
    )
    return (branch, input_grad, query_grad, key_grad, value_grad, out_grad)


def solution(mesh):
    rows, whole, both = P(("scene", "sp"), None), P(), P("sp", "hd")
    out = P(("scene", "sp"), "hd")
    return jax.shard_map(
        on_device,
        mesh=mesh,
        in_specs=(rows, whole, whole, both, both, both, both, rows),
        out_specs=(out,) * 6,
        check_vma=False,
    )
```

```python
import functools
import jax
import jax.numpy as jnp
from jax import lax
from jax.experimental import pallas as pl
from jax.experimental.pallas import tpu as pltpu
from jax.sharding import PartitionSpec as P

HEAD_DIM = 64
POOL = 8
GRID_W = 128
EPS = 1e-06
BF = jnp.bfloat16
F32 = jnp.float32
VMEM_LIMIT = 24 * 1024 * 1024
NORM_LIMIT = 24 * 1024 * 1024
TURN_LIMIT = 58 * 1024 * 1024
ATTEND_LIMIT = 24 * 1024 * 1024

NN = (((1,), (0,)), ((), ()))
TN = (((0,), (0,)), ((), ()))
NT = (((1,), (1,)), ((), ()))


def mm(left, right, dims=NN):
    return lax.dot_general(left, right, dims, preferred_element_type=F32)


def cost(flops, moved):
    return pl.CostEstimate(flops=int(flops), bytes_accessed=int(moved), transcendentals=0)


ANY = pl.BlockSpec(memory_space=pl.ANY)


def after(kernel, inputs, deps):
    return lambda *refs: kernel(*refs[:inputs], *refs[inputs + deps :])


def params(axes=1, limit=VMEM_LIMIT):
    return pltpu.CompilerParams(
        dimension_semantics=("arbitrary",) * axes, vmem_limit_bytes=limit
    )


def norm_kernel(gain_ref, rgain_ref, tok_ref, normed_ref, red_ref, runit_ref, rinv_ref, pooled):
    row, col = pl.program_id(0), pl.program_id(1)
    cols, width = tok_ref.shape[1], tok_ref.shape[2]
    gain = gain_ref[...].astype(F32).reshape(1, 1, width)
    chunk = 2 * POOL
    sums = []
    for part in range(cols // chunk):
        at = slice(part * chunk, (part + 1) * chunk)
        v = tok_ref[:, at, :].astype(F32)
        d = v - jnp.mean(v, axis=-1, keepdims=True)
        inv = lax.rsqrt(jnp.mean(d * d, axis=-1, keepdims=True) + EPS)
        n = (d * inv * gain).astype(BF)
        normed_ref[:, at, :] = n
        acc = jnp.sum(n.astype(F32), axis=0)
        sums.append(jnp.sum(acc.reshape(2, POOL, width), axis=1))
    span = cols // POOL
    base = pl.multiple_of((row * pl.num_programs(1) + col) * span, span)
    pooled[pl.ds(base, span), :] = jnp.concatenate(sums, axis=0)

    @pl.when((row == pl.num_programs(0) - 1) & (col == pl.num_programs(1) - 1))
    def _():
        v = pooled[...] / (POOL * POOL)
        d = v - jnp.mean(v, axis=-1, keepdims=True)
        inv = lax.rsqrt(jnp.mean(d * d, axis=-1, keepdims=True) + EPS)
        unit = d * inv
        runit_ref[...] = unit
        rinv_ref[...] = jnp.broadcast_to(inv, rinv_ref.shape)
        red_ref[...] = (unit * rgain_ref[...].astype(F32).reshape(1, width)).astype(BF)


def norm_and_pool(tokens, norm_gain, reduce_gain, deps):
    count, width = tokens.shape
    grid_rows = count // GRID_W
    blocks = count // (POOL * POOL)
    cols = 64
    tok = pl.BlockSpec((POOL, cols, width), lambda i, j: (i, j, 0))
    whole = lambda shape: pl.BlockSpec(shape, lambda i, j: (0,) * len(shape))
    normed, reduced, unit, inverse = pl.pallas_call(
        after(norm_kernel, 3, len(deps)),
        grid=(grid_rows // POOL, GRID_W // cols),
        in_specs=[whole((width,)), whole((width,)), tok] + [ANY] * len(deps),
        out_specs=[tok, whole((blocks, width)), whole((blocks, width)), whole((blocks, 128))],
        out_shape=[
            jax.ShapeDtypeStruct((grid_rows, GRID_W, width), BF),
            jax.ShapeDtypeStruct((blocks, width), BF),
            jax.ShapeDtypeStruct((blocks, width), F32),
            jax.ShapeDtypeStruct((blocks, 128), F32),
        ],
        scratch_shapes=[pltpu.VMEM((blocks, width), F32)],
        compiler_params=params(2, NORM_LIMIT),
        cost_estimate=cost(40 * count * width, 10 * count * width),
        name="norm_pool",
    )(norm_gain, reduce_gain, tokens.reshape(grid_rows, GRID_W, width), *deps)
    return normed.reshape(count, width), reduced, unit, inverse


def spread_heads(w_ref, width, kbd, vbd, kbd_t, vbd_t):
    feats, blocks = w_ref.shape[1], w_ref.shape[2] - width
    row = lax.broadcasted_iota(jnp.int32, (feats, blocks), 0)
    k = w_ref[0, :, width:].astype(F32) * HEAD_DIM ** (-0.5)
    v = w_ref[1, :, width:].astype(F32)
    for head in range(feats // HEAD_DIM):
        mask = (row >= head * HEAD_DIM) & (row < (head + 1) * HEAD_DIM)
        lanes = slice(head * blocks, (head + 1) * blocks)
        kbd_t[:, lanes] = jnp.where(mask, k, 0.0).astype(BF)
        vbd_t[:, lanes] = jnp.where(mask, v, 0.0).astype(BF)
    kbd[...] = kbd_t[...].T
    vbd[...] = vbd_t[...].T


def attend_tile(x, y, w_ref, kbd, vbd, kbd_t, vbd_t):
    feats = w_ref.shape[1]
    heads = feats // HEAD_DIM
    blocks = kbd.shape[0] // heads
    q_t = mm(w_ref[0, :, : x.shape[1]], x, NT).astype(BF)
    da_t = mm(w_ref[1, :, : y.shape[1]], y, NT).astype(BF)
    scores = mm(kbd[...], q_t)
    d_chances = mm(vbd[...], da_t)
    low, d_low = [], []
    for head in range(heads):
        rows = slice(head * blocks, (head + 1) * blocks)
        s = scores[rows]
        e = jnp.exp(s - jnp.max(s, axis=0, keepdims=True))
        p = e * (1.0 / jnp.sum(e, axis=0, keepdims=True))
        dp = d_chances[rows]
        delta = jnp.sum(p * dp, axis=0, keepdims=True)
        low.append(p.astype(BF))
        d_low.append((p * (dp - delta)).astype(BF))
    low = jnp.concatenate(low, axis=0)
    d_low = jnp.concatenate(d_low, axis=0)
    attn_t = mm(vbd_t[...], low).astype(BF)
    dq_t = mm(kbd_t[...], d_low).astype(BF)
    return q_t, da_t, low, d_low, attn_t, dq_t


def head_mask(shape, head):
    lane = lax.broadcasted_iota(jnp.int32, shape, 1)
    return (lane >= head * HEAD_DIM) & (lane < (head + 1) * HEAD_DIM)


def head_scratch(heads, blocks, feats):
    return [
        pltpu.VMEM((heads * blocks, feats), BF),
        pltpu.VMEM((heads * blocks, feats), BF),
        pltpu.VMEM((feats, heads * blocks), BF),
        pltpu.VMEM((feats, heads * blocks), BF),
    ]


def attend_kernel(n_sp, grad_factor, pos_ref, x_ref, y_ref, w_ref, sib_ref, own_ref, *rest):
    step = pl.program_id(0)
    half = pl.num_programs(0) // 2
    feats, width = w_ref.shape[1], x_ref.shape[1]
    blocks = w_ref.shape[2] - width
    depth = width // n_sp
    grad_ref, dkv_ref, send_refs = rest[0], rest[1], rest[2 : n_sp + 1]
    heads_at = rest[n_sp + 1 : n_sp + 5]
    dk_acc, dv_acc, g_acc = rest[n_sp + 5 :]

    @pl.when(step == 0)
    def _():
        spread_heads(w_ref, width, *heads_at)
        dk_acc[...] = jnp.zeros_like(dk_acc)
        dv_acc[...] = jnp.zeros_like(dv_acc)
        g_acc[...] = jnp.zeros_like(g_acc)

    x, y = x_ref[...], y_ref[...]
    q_t, da_t, low, d_low, attn_t, dq_t = attend_tile(x, y, w_ref, *heads_at)

    dk_acc[...] += mm(d_low, q_t, NT)
    dv_acc[...] += mm(low, da_t, NT)
    g_acc[0] += mm(dq_t, x)
    g_acc[1] += mm(attn_t, y)

    @pl.when(step < half)
    def _():
        sib_ref[0] = attn_t
        sib_ref[1] = dq_t

    @pl.when(step >= half)
    def _():
        own_ref[0] = attn_t
        own_ref[1] = dq_t

    @pl.when(step == pl.num_programs(0) - 1)
    def _():
        z = pos_ref[0]
        dk = jnp.zeros((blocks, feats), F32)
        dv = jnp.zeros((blocks, feats), F32)
        for head in range(feats // HEAD_DIM):
            mask = head_mask((blocks, feats), head)
            rows = slice(head * blocks, (head + 1) * blocks)
            dk = dk + jnp.where(mask, dk_acc[rows, :], 0.0)
            dv = dv + jnp.where(mask, dv_acc[rows, :], 0.0)
        dk = dk * HEAD_DIM ** (-0.5)
        part = blocks // n_sp
        dkv = jnp.concatenate([dk, dv], axis=1)
        dkv_ref[...] = dkv[:part]
        for k in range(n_sp):
            for which in range(2):
                cuts = [g_acc[which, :, i * depth : (i + 1) * depth] for i in range(n_sp)]
                total = choose(lax.rem(z + k, n_sp), cuts) * grad_factor
                if k == 0:
                    grad_ref[which] = total
                else:
                    send_refs[k - 1][which * feats : (which + 1) * feats, :] = total.astype(BF)
            if k > 0:
                at = (n_sp - k) * part
                for j in range(2 * feats // depth):
                    send_refs[k - 1][2 * feats + j * part : 2 * feats + (j + 1) * part, :] = dkv[
                        at : at + part, j * depth : (j + 1) * depth
                    ].astype(BF)


def far_kernel(x_ref, y_ref, w_ref, out_ref, *heads_at):
    @pl.when(pl.program_id(0) == 0)
    def _():
        spread_heads(w_ref, x_ref.shape[1], *heads_at)

    out = attend_tile(x_ref[...], y_ref[...], w_ref, *heads_at)
    out_ref[0] = out[4]
    out_ref[1] = out[5]


def fixed(shape):
    return pl.BlockSpec(shape, lambda *i: (0,) * len(shape))


def attend(n_sp, pos, normed, cotangent, weights, grad_factor, deps):
    feats = weights.shape[1]
    count, width = normed.shape
    own = count // 2
    blocks = weights.shape[2] - width
    heads = feats // HEAD_DIM
    depth = width // n_sp
    tile = 256
    half = own // tile
    rows = pl.BlockSpec((tile, width), lambda i, p: (lax.rem(i + (1 - p[1]) * half, 2 * half), 0))
    sib = pl.BlockSpec((2, feats, tile), lambda i, p: (0, 0, jnp.minimum(i, half - 1)))
    mine = pl.BlockSpec((2, feats, tile), lambda i, p: (0, 0, jnp.maximum(i - half, 0)))
    g_shape, d_shape = (2, feats, depth), (blocks // n_sp, 2 * feats)
    p_shape = (2 * feats + blocks // n_sp * (2 * feats // depth), depth)
    out = pl.pallas_call(
        after(functools.partial(attend_kernel, n_sp, grad_factor), 4, len(deps)),
        grid_spec=pltpu.PrefetchScalarGridSpec(
            num_scalar_prefetch=1,
            grid=(2 * half,),
            in_specs=[rows, rows, fixed(weights.shape)] + [ANY] * len(deps),
            out_specs=[sib, mine, fixed(g_shape), fixed(d_shape)] + [fixed(p_shape)] * (n_sp - 1),
            scratch_shapes=head_scratch(heads, blocks, feats)
            + [
                pltpu.VMEM((heads * blocks, feats), F32),
                pltpu.VMEM((heads * blocks, feats), F32),
                pltpu.VMEM((2, feats, width), F32),
            ],
        ),
        out_shape=[
            jax.ShapeDtypeStruct((2, feats, own), BF),
            jax.ShapeDtypeStruct((2, feats, own), BF),
        ]
        + [jax.ShapeDtypeStruct(g_shape, F32), jax.ShapeDtypeStruct(d_shape, F32)]
        + [jax.ShapeDtypeStruct(p_shape, BF)] * (n_sp - 1),
        compiler_params=params(1, ATTEND_LIMIT),
        cost_estimate=cost(
            16 * count * width * feats + 24 * count * heads * blocks * feats, 8 * count * width
        ),
        name="attend_grads",
    )(pos, normed, cotangent, weights, *deps)
    return out[0], out[1], out[2], out[3], out[4:]


def attend_far(pos, sibling, normed, cotangent, weights, deps):
    feats = weights.shape[1]
    count, width = normed.shape
    own = count // 2
    blocks = weights.shape[2] - width
    heads = feats // HEAD_DIM
    tile = 256
    half = own // tile
    if sibling:
        rows = pl.BlockSpec((tile, width), lambda i, p: (i + (1 - p[1]) * half, 0))
    else:
        rows = pl.BlockSpec((tile, width), lambda i, p: (i + p[1] * half, 0))
    return pl.pallas_call(
        after(lambda pos_ref, *refs: far_kernel(*refs), 4, len(deps)),
        grid_spec=pltpu.PrefetchScalarGridSpec(
            num_scalar_prefetch=1,
            grid=(half,),
            in_specs=[rows, rows, fixed(weights.shape)] + [ANY] * len(deps),
            out_specs=pl.BlockSpec((2, feats, tile), lambda i, p: (0, 0, i)),
            scratch_shapes=head_scratch(heads, blocks, feats),
        ),
        out_shape=jax.ShapeDtypeStruct((2, feats, own), BF),
        compiler_params=params(1, ATTEND_LIMIT),
        cost_estimate=cost(own * width * feats, own * width),
        name="attend_far",
    )(pos, normed, cotangent, weights, *deps)


def rows_kernel(count, pos_ref, *refs):
    in_refs, refs = refs[:count], refs[count:]
    w_refs, (own_ref, sib_ref, heads_ref) = refs[:count], refs[count:]
    h = pos_ref[2]
    sib = h + 1 - 2 * lax.rem(h, 2)
    cols = own_ref.shape[1]
    rows = [ref[0].T for ref in in_refs]
    for ref, owner in ((own_ref, h), (sib_ref, sib)):
        lanes = pl.ds(pl.multiple_of(owner * cols, 128), cols)
        total = None
        for row, w_ref in zip(rows, w_refs):
            term = mm(row, w_ref[1, :, lanes]).astype(BF).astype(F32)
            total = term if total is None else total + term
        ref[...] = total.astype(BF)
    total = None
    for in_ref, w_ref in zip(in_refs, w_refs):
        term = mm(in_ref[1].T, w_ref[0, :, : heads_ref.shape[1]]).astype(BF).astype(F32)
        total = term if total is None else total + term
    heads_ref[...] = total


def model_rows(pos, width, pieces, weights, n_hd, deps):
    count = len(pieces)
    feats = pieces[0].shape[-2]
    own = pieces[0].shape[-1]
    cols = width // n_hd
    tile = 256
    steps = own // tile
    whole = lambda shape: pl.BlockSpec(shape, lambda i, p: (0,) * len(shape))
    t_spec = pl.BlockSpec((2, feats, tile), lambda i, p: (0, 0, i))
    return pl.pallas_call(
        after(functools.partial(rows_kernel, count), 2 * count + 1, len(deps)),
        grid_spec=pltpu.PrefetchScalarGridSpec(
            num_scalar_prefetch=1,
            grid=(steps,),
            in_specs=[t_spec] * count
            + [whole(w.shape) for w in weights]
            + [ANY] * len(deps),
            out_specs=[
                pl.BlockSpec((tile, cols), lambda i, p: (p[1] * steps + i, 0)),
                pl.BlockSpec((tile, cols), lambda i, p: (i, 0)),
                pl.BlockSpec((tile, width), lambda i, p: (i, 0)),
            ],
        ),
        out_shape=[
            jax.ShapeDtypeStruct((2 * own, cols), BF),
            jax.ShapeDtypeStruct((own, cols), BF),
            jax.ShapeDtypeStruct((own, width), F32),
        ],
        compiler_params=params(),
        cost_estimate=cost(4 * own * width * (width + 2 * cols), 12 * own * width),
        name="model_rows",
    )(pos, *pieces, *weights, *deps)


def input_kernel(count, pos_ref, gain_ref, rgain_ref, tok_ref, runit_ref, rinv_ref, heads_ref, *refs):
    d_refs, (own_ref, sib_ref, spread, u_ref) = refs[:count], refs[count:]
    width = tok_ref.shape[1]
    h = pos_ref[2]
    sib = h + 1 - 2 * lax.rem(h, 2)
    cols = own_ref.shape[1]

    @pl.when(pl.program_id(0) == 0)
    def _():
        groups = runit_ref.shape[0]
        total = d_refs[0][...].astype(F32)
        for ref in d_refs[1:]:
            total = total + ref[...].astype(F32)
        e = total * rgain_ref[...].astype(F32).reshape(1, width)
        unit = runit_ref[...]
        first = jnp.mean(e, axis=-1, keepdims=True)
        second = jnp.mean(e * unit, axis=-1, keepdims=True)
        d_pooled = rinv_ref[:, 0:1] * (e - first - unit * second) / (POOL * POOL)
        spread[...] = jnp.broadcast_to(d_pooled[:, None, :], (groups, POOL, width)).reshape(
            groups * POOL, width
        )

    gain = gain_ref[...].astype(F32).reshape(1, width)
    for part in range(tok_ref.shape[0] // GRID_W):
        at = slice(part * GRID_W, (part + 1) * GRID_W)
        v = tok_ref[at, :].astype(F32)
        d = v - jnp.mean(v, axis=-1, keepdims=True)
        inv = lax.rsqrt(jnp.mean(d * d, axis=-1, keepdims=True) + EPS)
        unit = d * inv
        e = (heads_ref[at, :] + spread[...]) * gain
        first = jnp.mean(e, axis=-1, keepdims=True)
        second = jnp.mean(e * unit, axis=-1, keepdims=True)
        u_ref[at, :] = inv * (e - first - unit * second)
    for ref, owner in ((own_ref, h), (sib_ref, sib)):
        ref[...] = u_ref[:, pl.ds(pl.multiple_of(owner * cols, 128), cols)].astype(BF)


def input_rows(pos, norm_gain, reduce_gain, tokens, unit, inverse, d_heads, parts, n_hd, deps):
    own, width = d_heads.shape
    cols = width // n_hd
    groups = parts[0].shape[0]
    tile = 256
    steps = own // tile
    whole = lambda shape: pl.BlockSpec(shape, lambda i, p: (0,) * len(shape))
    half = lambda shape: pl.BlockSpec(shape, lambda i, p: (p[1], 0))
    return pl.pallas_call(
        after(functools.partial(input_kernel, len(parts)), 7 + len(parts), len(deps)),
        grid_spec=pltpu.PrefetchScalarGridSpec(
            num_scalar_prefetch=1,
            grid=(steps,),
            in_specs=[
                whole((width,)),
                whole((width,)),
                pl.BlockSpec((tile, width), lambda i, p: (p[1] * steps + i, 0)),
                half((groups, width)),
                half((groups, 128)),
                pl.BlockSpec((tile, width), lambda i, p: (i, 0)),
            ]
            + [whole(part.shape) for part in parts]
            + [ANY] * len(deps),
            out_specs=[
                pl.BlockSpec((tile, cols), lambda i, p: (p[1] * steps + i, 0)),
                pl.BlockSpec((tile, cols), lambda i, p: (i, 0)),
            ],
            scratch_shapes=[
                pltpu.VMEM((groups * POOL, width), F32),
                pltpu.VMEM((tile, width), F32),
            ],
        ),
        out_shape=[
            jax.ShapeDtypeStruct((2 * own, cols), BF),
            jax.ShapeDtypeStruct((own, cols), BF),
        ],
        compiler_params=params(),
        cost_estimate=cost(40 * own * width, 16 * own * width),
        name="input_rows",
    )(
        pos,
        norm_gain,
        reduce_gain,
        tokens,
        unit,
        inverse,
        d_heads,
        *parts,
        *deps,
    )


def small(kernel, name, out_shape, *args, pos=None, deps=()):
    smem = [] if pos is None else [pl.BlockSpec(memory_space=pltpu.SMEM)]
    vmem = pl.BlockSpec(memory_space=pltpu.VMEM)
    many = isinstance(out_shape, list)
    return pl.pallas_call(
        after(kernel, len(smem) + len(args), len(deps)),
        in_specs=smem + [vmem] * len(args) + [ANY] * len(deps),
        out_specs=[vmem] * len(out_shape) if many else vmem,
        out_shape=out_shape,
        compiler_params=pltpu.CompilerParams(vmem_limit_bytes=VMEM_LIMIT),
        cost_estimate=cost(1 << 28, 1 << 21),
        name=name,
    )(*([] if pos is None else [pos]), *args, *deps)


def turn_kernel(q_ref, o_ref, out_ref, half_ref, tag_ref):
    tag_ref[...] = jnp.zeros_like(tag_ref)
    q, o = q_ref[...].T, o_ref[...].T
    out_ref[0] = q
    out_ref[1] = o
    half_ref[...] = jnp.where(lax.axis_index("scene") == 0, q, o)


def stack_kernel(n_sp, pos_ref, red_ref, *refs):
    pieces, far_ref, cut_refs = refs[: n_sp - 1], refs[n_sp - 1], refs[n_sp:]
    depth = far_ref.shape[2]
    z = pos_ref[0]
    for k, ref in enumerate(pieces):
        far_ref[k] = ref[...]
    parts = [red_ref[:, i * depth : (i + 1) * depth] for i in range(n_sp)]
    for k, ref in enumerate(cut_refs):
        ref[...] = choose(lax.rem(z + k, n_sp), parts)


def choose(index, values):
    result = values[0]
    for k in range(1, len(values)):
        result = jnp.where(index == k, values[k], result)
    return result


def place_pieces(z, pieces, out_ref, which):
    n_sp, depth = len(pieces), pieces[0].shape[1]
    for place in range(n_sp):
        index = lax.rem(z - place + n_sp, n_sp)
        out_ref[which, :, place * depth : (place + 1) * depth] = choose(index, pieces)


def pack_kernel(n_sp, pos_ref, own_ref, here_ref, there_ref, part_ref, *refs):
    parts, (out_ref, kv_ref) = refs[:-2], refs[-2:]
    feats, depth = own_ref.shape[1:]
    rows = part_ref.shape[0]
    blocks, width = rows // n_sp, depth * n_sp
    z, y = pos_ref[0], pos_ref[3]
    for which in range(2):
        pieces = [own_ref[which]] + [
            jnp.where(y == which, here_ref[k], there_ref[k]) for k in range(n_sp - 1)
        ]
        place_pieces(z, pieces, out_ref, which)
        lanes = slice(which * feats, (which + 1) * feats)
        sums = []
        for j in range(n_sp):
            total = part_ref[j * blocks : (j + 1) * blocks, lanes]
            for k, part in enumerate(parts, 1):
                at = (j - k) % n_sp
                total = total + part[at * blocks : (at + 1) * blocks, lanes].astype(F32)
            sums.append(total)
        kv = jnp.concatenate(sums, axis=0).T.astype(BF)
        out_ref[which, :, width:] = kv
        kv_ref[which] = kv


def pack_far_kernel(pos_ref, here_ref, there_ref, kv_ref, out_ref):
    n_sp, feats, depth = here_ref.shape
    z, y = pos_ref[0], pos_ref[3]
    for which in range(2):
        pieces = [jnp.where(y == which, here_ref[k], there_ref[k]) for k in range(n_sp)]
        place_pieces(z, pieces, out_ref, which)
        out_ref[which, :, n_sp * depth :] = kv_ref[which]


def project_kernel(k_ref, v_ref, own_ref, far_ref, *refs):
    red, (cols_ref, part_ref, low_ref, all_ref) = refs[:-4], refs[-4:]
    all_ref[0] = own_ref[...]
    all_ref[1:] = far_ref[...]
    feats = k_ref.shape[1]
    rows = jnp.concatenate([ref[...] for ref in red], axis=0)
    cols_ref[...] = rows
    for which, ref in ((0, k_ref), (1, v_ref)):
        lanes = slice(which * feats, (which + 1) * feats)
        part = mm(rows, ref[...])
        part_ref[:, lanes] = part
        low_ref[:, lanes] = part.astype(BF)


def back_kernel(n_sp, pos_ref, key_ref, value_ref, here_ref, there_ref, own_ref, *refs):
    parts, (low_ref, mine_ref, other_ref, d_red) = refs[: n_sp - 1], refs[n_sp - 1 :]
    blocks = own_ref.shape[0]
    depth, feats = key_ref.shape
    z, c, y = pos_ref[0], pos_ref[1], pos_ref[3]
    total = own_ref[...]
    for part in parts:
        rows = part[2 * feats :, :].astype(F32)
        total = total + jnp.concatenate(
            [rows[j * blocks : (j + 1) * blocks] for j in range(2 * feats // depth)], axis=1
        )
    low = total.astype(BF)
    low_ref[...] = low
    terms = [mm(low[:, :feats], key_ref[...], NT) + mm(low[:, feats:], value_ref[...], NT)]
    for k in range(n_sp - 1):
        here, there = here_ref[k], there_ref[k]
        key, value = jnp.where(y == 0, here, there), jnp.where(y == 0, there, here)
        terms.append(mm(low[:, :feats], key, NT) + mm(low[:, feats:], value, NT))
    for place in range(n_sp):
        index = lax.rem(z - place + n_sp, n_sp)
        d_red[:, place * depth : (place + 1) * depth] = choose(index, terms)
    half = blocks // 2
    mine_ref[...] = d_red[pl.ds(pl.multiple_of(c * half, half), half), :].astype(BF)
    other_ref[...] = d_red[pl.ds(pl.multiple_of((1 - c) * half, half), half), :].astype(BF)


def half_kernel(k_ref, v_ref, out_ref):
    out_ref[...] = jnp.where(lax.axis_index("scene") == 0, k_ref[...], v_ref[...])


def gather_kernel(*refs):
    for k, ref in enumerate(refs[:-1]):
        refs[-1][k] = ref[...]


def kv_grad_kernel(n_sp, grad_factor, pos_ref, red_ref, d_ref, key_ref, value_ref):
    feats = key_ref.shape[1]
    blocks = d_ref.shape[0] // n_sp
    z = pos_ref[0]
    both = None
    for j in range(n_sp):
        index = lax.rem(z - lax.bitwise_xor(z, j) + n_sp, n_sp)
        red = red_ref[pl.ds(pl.multiple_of(index * blocks, blocks), blocks), :]
        term = mm(red.T, d_ref[j * blocks : (j + 1) * blocks, :])
        both = term if both is None else both + term
    key_ref[...] = both[:, :feats] * grad_factor
    value_ref[...] = both[:, feats:] * grad_factor


def grad_sum_kernel(*refs):
    query_ref, out_ref = refs[-2:]
    for which, ref in ((0, query_ref), (1, out_ref)):
        total = refs[0][which]
        feats = total.shape[0]
        for part in refs[1:-2]:
            total = total + part[which * feats : (which + 1) * feats, :].astype(F32)
        ref[...] = total.T


def on_device(
    tokens,
    norm_gain,
    reduce_gain,
    query_weight,
    key_weight,
    value_weight,
    out_weight,
    out_cotangent,
):
    n_sp, n_hd = lax.axis_size("sp"), lax.axis_size("hd")
    n_x = n_hd // 2
    z, h, y = lax.axis_index("sp"), lax.axis_index("hd"), lax.axis_index("scene")
    c = h % 2
    depth, feats = query_weight.shape
    width = tokens.shape[1]
    own = tokens.shape[0] // 2
    grad_factor = float(2 * own * n_sp) ** (-0.5)
    pos = jnp.stack([z, c, h, y]).astype(jnp.int32)
    others = range(1, n_sp)

    def low(*shape):
        return jax.ShapeDtypeStruct(shape, BF)

    def wide(*shape):
        return jax.ShapeDtypeStruct(shape, F32)

    def to_sp(value, k):
        return lax.ppermute(value, "sp", [(i, (i + k) % n_sp) for i in range(n_sp)])

    def to_xor(value, bit):
        return lax.ppermute(value, "sp", [(i, i ^ bit) for i in range(n_sp)])

    def to_hd(value, k):
        return lax.ppermute(value, "hd", [(i, (i + k) % n_hd) for i in range(n_hd)])

    def swap(value):
        return lax.ppermute(value, "hd", [(i, i ^ 1) for i in range(n_hd)])

    def cross(value):
        return lax.ppermute(value, "scene", [(0, 1), (1, 0)])

    block = pl.BlockSpec((depth, feats), lambda i: (0, 0))
    shard, half, tag = pl.pallas_call(
        turn_kernel,
        grid=(1,),
        in_specs=[block, block],
        out_specs=[fixed((2, feats, depth)), fixed((feats, depth)), fixed((8, 128))],
        out_shape=[low(2, feats, depth), low(feats, depth), wide(8, 128)],
        compiler_params=params(1, TURN_LIMIT),
        name="turn",
    )(query_weight, out_weight)
    here = [to_sp(half, k) for k in others]
    normed, reduced, r_unit, r_inverse = norm_and_pool(tokens, norm_gain, reduce_gain, (tag,))
    blocks = reduced.shape[0]
    far3, *cuts = small(
        functools.partial(stack_kernel, n_sp),
        "stack",
        [low(n_sp - 1, feats, depth)] + [low(blocks, depth)] * n_sp,
        reduced,
        *here,
        pos=pos,
    )
    there3 = cross(far3)

    both = (blocks * n_sp, 2 * feats)
    reduced_cols, kv_part, kv_low, all4 = small(
        project_kernel,
        "project",
        [low(blocks * n_sp, depth), wide(*both), low(*both), low(n_sp, feats, depth)],
        key_weight,
        value_weight,
        half,
        far3,
        cuts[0],
        *[to_sp(cuts[k], k) for k in others],
    )
    x_pieces = [to_hd(all4, 2 * k) for k in range(1, n_x)]
    packed, kv_own = small(
        functools.partial(pack_kernel, n_sp),
        "pack",
        [low(2, feats, width + blocks * n_sp), low(2, feats, blocks * n_sp)],
        shard,
        far3,
        there3,
        kv_part,
        *[to_sp(kv_low, k) for k in others],
        pos=pos,
        deps=tuple(x_pieces),
    )

    kv_half = small(
        half_kernel, "half", low(depth, feats), key_weight, value_weight, deps=(packed,)
    )
    kv_here = [to_sp(kv_half, k) for k in others]
    kv_far = [to_hd(kv_own, 2 * k) for k in range(1, n_x)]

    for_sib, own_pair, grad_own, dkv_own, sends = attend(
        n_sp, pos, normed, out_cotangent, packed, grad_factor, (kv_half, *kv_far)
    )
    packed_sib = swap(packed)
    parts = [to_sp(sends[k - 1], k) for k in others]
    kv_here = small(
        gather_kernel, "gather", low(n_sp - 1, depth, feats), *kv_here, deps=(own_pair, packed_sib)
    )
    kv_there = cross(kv_here)
    pairs, ws = [own_pair, swap(for_sib)], [packed, packed_sib]
    packed_far = [
        small(
            pack_far_kernel,
            "pack_far",
            low(*packed.shape),
            piece,
            cross(piece),
            kv,
            pos=pos,
            deps=(kv_here,),
        )
        for piece, kv in zip(x_pieces, kv_far)
    ]
    far_sib = [attend_far(pos, True, normed, out_cotangent, w, ()) for w in packed_far]
    for w, pair in zip(packed_far, far_sib):
        mine = attend_far(pos, False, normed, out_cotangent, w, (pairs[1], *far_sib))
        pairs += [mine, swap(pair)]
        ws += [w, swap(w)]
    branch, other, d_heads = model_rows(pos, width, pairs, ws, n_hd, ())

    vmem = pl.BlockSpec(memory_space=pltpu.VMEM)
    dkv_rows, d_mine, d_other = pl.pallas_call(
        after(functools.partial(back_kernel, n_sp), 5 + n_sp, 1),
        in_specs=[pl.BlockSpec(memory_space=pltpu.SMEM)] + [vmem] * (4 + n_sp) + [ANY],
        out_specs=[vmem] * 3,
        out_shape=[low(blocks, 2 * feats), low(blocks // 2, width), low(blocks // 2, width)],
        scratch_shapes=[pltpu.VMEM((blocks, width), F32)],
        compiler_params=pltpu.CompilerParams(vmem_limit_bytes=VMEM_LIMIT),
        cost_estimate=cost(1 << 28, 1 << 21),
        name="back",
    )(pos, key_weight, value_weight, kv_here, kv_there, dkv_own, *parts, d_heads)
    d_parts = [d_mine] + [to_hd(d_other if k % 2 else d_mine, k) for k in range(1, n_hd)]
    dkv_all, bit = dkv_rows, 1
    while bit < n_sp:
        dkv_all = jnp.concatenate([dkv_all, to_xor(dkv_all, bit)])
        bit *= 2
    place = (1 - c) * own
    branch = lax.dynamic_update_slice_in_dim(branch, swap(other), place, 0)
    input_grad, other = input_rows(
        pos,
        norm_gain,
        reduce_gain,
        tokens,
        r_unit,
        r_inverse,
        d_heads,
        d_parts,
        n_hd,
        (),
    )
    input_grad = lax.dynamic_update_slice_in_dim(input_grad, swap(other), place, 0)
    query_grad, out_grad = small(
        grad_sum_kernel, "grad_sum", [wide(depth, feats)] * 2, grad_own, *parts, deps=(other,)
    )
    key_grad, value_grad = small(
        functools.partial(kv_grad_kernel, n_sp, grad_factor),
        "kv_grad",
        [wide(depth, feats)] * 2,
        reduced_cols,
        dkv_all,
        pos=pos,
        deps=(other,),
    )
    return (branch, input_grad, query_grad, key_grad, value_grad, out_grad)


def solution(mesh):
    rows, whole, both = P(("scene", "sp"), None), P(), P("sp", "hd")
    out = P(("scene", "sp"), "hd")
    return jax.shard_map(
        on_device,
        mesh=mesh,
        in_specs=(rows, whole, whole, both, both, both, both, rows),
        out_specs=(out,) * 6,
        check_vma=False,
    )
```

```python
import functools
import jax
import jax.numpy as jnp
from jax import lax
from jax.experimental import pallas as pl
from jax.experimental.pallas import tpu as pltpu
from jax.sharding import PartitionSpec as P

HEAD_DIM = 64
POOL = 8
GRID_W = 128
EPS = 1e-06
BF = jnp.bfloat16
F32 = jnp.float32
VMEM_LIMIT = 24 * 1024 * 1024
NORM_LIMIT = 24 * 1024 * 1024
TURN_LIMIT = 58 * 1024 * 1024
ATTEND_LIMIT = 24 * 1024 * 1024

NN = (((1,), (0,)), ((), ()))
TN = (((0,), (0,)), ((), ()))
NT = (((1,), (1,)), ((), ()))


def mm(left, right, dims=NN):
    return lax.dot_general(left, right, dims, preferred_element_type=F32)


def cost(flops, moved):
    return pl.CostEstimate(flops=int(flops), bytes_accessed=int(moved), transcendentals=0)


ANY = pl.BlockSpec(memory_space=pl.ANY)


def after(kernel, inputs, deps):
    return lambda *refs: kernel(*refs[:inputs], *refs[inputs + deps :])


def params(axes=1, limit=VMEM_LIMIT):
    return pltpu.CompilerParams(
        dimension_semantics=("arbitrary",) * axes, vmem_limit_bytes=limit
    )


def norm_kernel(gain_ref, rgain_ref, tok_ref, normed_ref, red_ref, runit_ref, rinv_ref, pooled):
    row, col = pl.program_id(0), pl.program_id(1)
    cols, width = tok_ref.shape[1], tok_ref.shape[2]
    gain = gain_ref[...].astype(F32).reshape(1, 1, width)
    chunk = 2 * POOL
    sums = []
    for part in range(cols // chunk):
        at = slice(part * chunk, (part + 1) * chunk)
        v = tok_ref[:, at, :].astype(F32)
        d = v - jnp.mean(v, axis=-1, keepdims=True)
        inv = lax.rsqrt(jnp.mean(d * d, axis=-1, keepdims=True) + EPS)
        n = (d * inv * gain).astype(BF)
        normed_ref[:, at, :] = n
        acc = jnp.sum(n.astype(F32), axis=0)
        sums.append(jnp.sum(acc.reshape(2, POOL, width), axis=1))
    span = cols // POOL
    base = pl.multiple_of((row * pl.num_programs(1) + col) * span, span)
    pooled[pl.ds(base, span), :] = jnp.concatenate(sums, axis=0)

    @pl.when((row == pl.num_programs(0) - 1) & (col == pl.num_programs(1) - 1))
    def _():
        v = pooled[...] / (POOL * POOL)
        d = v - jnp.mean(v, axis=-1, keepdims=True)
        inv = lax.rsqrt(jnp.mean(d * d, axis=-1, keepdims=True) + EPS)
        unit = d * inv
        runit_ref[...] = unit
        rinv_ref[...] = jnp.broadcast_to(inv, rinv_ref.shape)
        red_ref[...] = (unit * rgain_ref[...].astype(F32).reshape(1, width)).astype(BF)


def norm_and_pool(tokens, norm_gain, reduce_gain, deps):
    count, width = tokens.shape
    grid_rows = count // GRID_W
    blocks = count // (POOL * POOL)
    cols = 64
    tok = pl.BlockSpec((POOL, cols, width), lambda i, j: (i, j, 0))
    whole = lambda shape: pl.BlockSpec(shape, lambda i, j: (0,) * len(shape))
    normed, reduced, unit, inverse = pl.pallas_call(
        after(norm_kernel, 3, len(deps)),
        grid=(grid_rows // POOL, GRID_W // cols),
        in_specs=[whole((width,)), whole((width,)), tok] + [ANY] * len(deps),
        out_specs=[tok, whole((blocks, width)), whole((blocks, width)), whole((blocks, 128))],
        out_shape=[
            jax.ShapeDtypeStruct((grid_rows, GRID_W, width), BF),
            jax.ShapeDtypeStruct((blocks, width), BF),
            jax.ShapeDtypeStruct((blocks, width), F32),
            jax.ShapeDtypeStruct((blocks, 128), F32),
        ],
        scratch_shapes=[pltpu.VMEM((blocks, width), F32)],
        compiler_params=params(2, NORM_LIMIT),
        cost_estimate=cost(40 * count * width, 10 * count * width),
        name="norm_pool",
    )(norm_gain, reduce_gain, tokens.reshape(grid_rows, GRID_W, width), *deps)
    return normed.reshape(count, width), reduced, unit, inverse


def spread_heads(w_ref, width, kbd, vbd, kbd_t, vbd_t):
    feats, blocks = w_ref.shape[1], w_ref.shape[2] - width
    row = lax.broadcasted_iota(jnp.int32, (feats, blocks), 0)
    k = w_ref[0, :, width:].astype(F32) * HEAD_DIM ** (-0.5)
    v = w_ref[1, :, width:].astype(F32)
    for head in range(feats // HEAD_DIM):
        mask = (row >= head * HEAD_DIM) & (row < (head + 1) * HEAD_DIM)
        lanes = slice(head * blocks, (head + 1) * blocks)
        kbd_t[:, lanes] = jnp.where(mask, k, 0.0).astype(BF)
        vbd_t[:, lanes] = jnp.where(mask, v, 0.0).astype(BF)
    kbd[...] = kbd_t[...].T
    vbd[...] = vbd_t[...].T


def attend_tile(x, y, w_ref, kbd, vbd, kbd_t, vbd_t):
    feats = w_ref.shape[1]
    heads = feats // HEAD_DIM
    blocks = kbd.shape[0] // heads
    q_t = mm(w_ref[0, :, : x.shape[1]], x, NT).astype(BF)
    da_t = mm(w_ref[1, :, : y.shape[1]], y, NT).astype(BF)
    scores = mm(kbd[...], q_t)
    d_chances = mm(vbd[...], da_t)
    low, d_low = [], []
    for head in range(heads):
        rows = slice(head * blocks, (head + 1) * blocks)
        s = scores[rows]
        e = jnp.exp(s - jnp.max(s, axis=0, keepdims=True))
        p = e * (1.0 / jnp.sum(e, axis=0, keepdims=True))
        dp = d_chances[rows]
        delta = jnp.sum(p * dp, axis=0, keepdims=True)
        low.append(p.astype(BF))
        d_low.append((p * (dp - delta)).astype(BF))
    low = jnp.concatenate(low, axis=0)
    d_low = jnp.concatenate(d_low, axis=0)
    attn_t = mm(vbd_t[...], low).astype(BF)
    dq_t = mm(kbd_t[...], d_low).astype(BF)
    return q_t, da_t, low, d_low, attn_t, dq_t


def head_mask(shape, head):
    lane = lax.broadcasted_iota(jnp.int32, shape, 1)
    return (lane >= head * HEAD_DIM) & (lane < (head + 1) * HEAD_DIM)


def head_scratch(heads, blocks, feats):
    return [
        pltpu.VMEM((heads * blocks, feats), BF),
        pltpu.VMEM((heads * blocks, feats), BF),
        pltpu.VMEM((feats, heads * blocks), BF),
        pltpu.VMEM((feats, heads * blocks), BF),
    ]


def attend_kernel(n_sp, grad_factor, pos_ref, x_ref, y_ref, w_ref, sib_ref, own_ref, *rest):
    step = pl.program_id(0)
    half = pl.num_programs(0) // 2
    feats, width = w_ref.shape[1], x_ref.shape[1]
    blocks = w_ref.shape[2] - width
    depth = width // n_sp
    grad_ref, dkv_ref, send_refs = rest[0], rest[1], rest[2 : n_sp + 1]
    heads_at = rest[n_sp + 1 : n_sp + 5]
    dk_acc, dv_acc, g_acc = rest[n_sp + 5 :]

    @pl.when(step == 0)
    def _():
        spread_heads(w_ref, width, *heads_at)
        dk_acc[...] = jnp.zeros_like(dk_acc)
        dv_acc[...] = jnp.zeros_like(dv_acc)
        g_acc[...] = jnp.zeros_like(g_acc)

    x, y = x_ref[...], y_ref[...]
    q_t, da_t, low, d_low, attn_t, dq_t = attend_tile(x, y, w_ref, *heads_at)

    dk_acc[...] += mm(d_low, q_t, NT)
    dv_acc[...] += mm(low, da_t, NT)
    g_acc[0] += mm(dq_t, x)
    g_acc[1] += mm(attn_t, y)

    @pl.when(step < half)
    def _():
        sib_ref[0] = attn_t
        sib_ref[1] = dq_t

    @pl.when(step >= half)
    def _():
        own_ref[0] = attn_t
        own_ref[1] = dq_t

    @pl.when(step == pl.num_programs(0) - 1)
    def _():
        z = pos_ref[0]
        dk = jnp.zeros((blocks, feats), F32)
        dv = jnp.zeros((blocks, feats), F32)
        for head in range(feats // HEAD_DIM):
            mask = head_mask((blocks, feats), head)
            rows = slice(head * blocks, (head + 1) * blocks)
            dk = dk + jnp.where(mask, dk_acc[rows, :], 0.0)
            dv = dv + jnp.where(mask, dv_acc[rows, :], 0.0)
        dk = dk * HEAD_DIM ** (-0.5)
        part = blocks // n_sp
        dkv = jnp.concatenate([dk, dv], axis=1)
        dkv_ref[...] = dkv[:part]
        for k in range(n_sp):
            for which in range(2):
                cuts = [g_acc[which, :, i * depth : (i + 1) * depth] for i in range(n_sp)]
                total = choose(lax.rem(z + k, n_sp), cuts) * grad_factor
                if k == 0:
                    grad_ref[which] = total
                else:
                    send_refs[k - 1][which * feats : (which + 1) * feats, :] = total.astype(BF)
            if k > 0:
                at = (n_sp - k) * part
                for j in range(2 * feats // depth):
                    send_refs[k - 1][2 * feats + j * part : 2 * feats + (j + 1) * part, :] = dkv[
                        at : at + part, j * depth : (j + 1) * depth
                    ].astype(BF)


def far_kernel(x_ref, y_ref, w_ref, out_ref, *heads_at):
    @pl.when(pl.program_id(0) == 0)
    def _():
        spread_heads(w_ref, x_ref.shape[1], *heads_at)

    out = attend_tile(x_ref[...], y_ref[...], w_ref, *heads_at)
    out_ref[0] = out[4]
    out_ref[1] = out[5]


def fixed(shape):
    return pl.BlockSpec(shape, lambda *i: (0,) * len(shape))


def attend(n_sp, pos, normed, cotangent, weights, grad_factor, deps):
    feats = weights.shape[1]
    count, width = normed.shape
    own = count // 2
    blocks = weights.shape[2] - width
    heads = feats // HEAD_DIM
    depth = width // n_sp
    tile = 256
    half = own // tile
    rows = pl.BlockSpec((tile, width), lambda i, p: (lax.rem(i + (1 - p[1]) * half, 2 * half), 0))
    sib = pl.BlockSpec((2, feats, tile), lambda i, p: (0, 0, jnp.minimum(i, half - 1)))
    mine = pl.BlockSpec((2, feats, tile), lambda i, p: (0, 0, jnp.maximum(i - half, 0)))
    g_shape, d_shape = (2, feats, depth), (blocks // n_sp, 2 * feats)
    p_shape = (2 * feats + blocks // n_sp * (2 * feats // depth), depth)
    out = pl.pallas_call(
        after(functools.partial(attend_kernel, n_sp, grad_factor), 4, len(deps)),
        grid_spec=pltpu.PrefetchScalarGridSpec(
            num_scalar_prefetch=1,
            grid=(2 * half,),
            in_specs=[rows, rows, fixed(weights.shape)] + [ANY] * len(deps),
            out_specs=[sib, mine, fixed(g_shape), fixed(d_shape)] + [fixed(p_shape)] * (n_sp - 1),
            scratch_shapes=head_scratch(heads, blocks, feats)
            + [
                pltpu.VMEM((heads * blocks, feats), F32),
                pltpu.VMEM((heads * blocks, feats), F32),
                pltpu.VMEM((2, feats, width), F32),
            ],
        ),
        out_shape=[
            jax.ShapeDtypeStruct((2, feats, own), BF),
            jax.ShapeDtypeStruct((2, feats, own), BF),
        ]
        + [jax.ShapeDtypeStruct(g_shape, F32), jax.ShapeDtypeStruct(d_shape, F32)]
        + [jax.ShapeDtypeStruct(p_shape, BF)] * (n_sp - 1),
        compiler_params=params(1, ATTEND_LIMIT),
        cost_estimate=cost(
            16 * count * width * feats + 24 * count * heads * blocks * feats, 8 * count * width
        ),
        name="attend_grads",
    )(pos, normed, cotangent, weights, *deps)
    return out[0], out[1], out[2], out[3], out[4:]


def attend_far(pos, sibling, normed, cotangent, weights, deps):
    feats = weights.shape[1]
    count, width = normed.shape
    own = count // 2
    blocks = weights.shape[2] - width
    heads = feats // HEAD_DIM
    tile = 256
    half = own // tile
    if sibling:
        rows = pl.BlockSpec((tile, width), lambda i, p: (i + (1 - p[1]) * half, 0))
    else:
        rows = pl.BlockSpec((tile, width), lambda i, p: (i + p[1] * half, 0))
    return pl.pallas_call(
        after(lambda pos_ref, *refs: far_kernel(*refs), 4, len(deps)),
        grid_spec=pltpu.PrefetchScalarGridSpec(
            num_scalar_prefetch=1,
            grid=(half,),
            in_specs=[rows, rows, fixed(weights.shape)] + [ANY] * len(deps),
            out_specs=pl.BlockSpec((2, feats, tile), lambda i, p: (0, 0, i)),
            scratch_shapes=head_scratch(heads, blocks, feats),
        ),
        out_shape=jax.ShapeDtypeStruct((2, feats, own), BF),
        compiler_params=params(1, ATTEND_LIMIT),
        cost_estimate=cost(own * width * feats, own * width),
        name="attend_far",
    )(pos, normed, cotangent, weights, *deps)


def rows_kernel(count, pos_ref, *refs):
    in_refs, refs = refs[:count], refs[count:]
    w_refs, (own_ref, sib_ref, heads_ref) = refs[:count], refs[count:]
    h = pos_ref[2]
    sib = h + 1 - 2 * lax.rem(h, 2)
    cols = own_ref.shape[1]
    rows = [ref[0].T for ref in in_refs]
    for ref, owner in ((own_ref, h), (sib_ref, sib)):
        lanes = pl.ds(pl.multiple_of(owner * cols, 128), cols)
        total = None
        for row, w_ref in zip(rows, w_refs):
            term = mm(row, w_ref[1, :, lanes]).astype(BF).astype(F32)
            total = term if total is None else total + term
        ref[...] = total.astype(BF)
    total = None
    for in_ref, w_ref in zip(in_refs, w_refs):
        term = mm(in_ref[1].T, w_ref[0, :, : heads_ref.shape[1]]).astype(BF).astype(F32)
        total = term if total is None else total + term
    heads_ref[...] = total


def model_rows(pos, width, pieces, weights, n_hd, deps):
    count = len(pieces)
    feats = pieces[0].shape[-2]
    own = pieces[0].shape[-1]
    cols = width // n_hd
    tile = 256
    steps = own // tile
    whole = lambda shape: pl.BlockSpec(shape, lambda i, p: (0,) * len(shape))
    t_spec = pl.BlockSpec((2, feats, tile), lambda i, p: (0, 0, i))
    return pl.pallas_call(
        after(functools.partial(rows_kernel, count), 2 * count + 1, len(deps)),
        grid_spec=pltpu.PrefetchScalarGridSpec(
            num_scalar_prefetch=1,
            grid=(steps,),
            in_specs=[t_spec] * count
            + [whole(w.shape) for w in weights]
            + [ANY] * len(deps),
            out_specs=[
                pl.BlockSpec((tile, cols), lambda i, p: (p[1] * steps + i, 0)),
                pl.BlockSpec((tile, cols), lambda i, p: (i, 0)),
                pl.BlockSpec((tile, width), lambda i, p: (i, 0)),
            ],
        ),
        out_shape=[
            jax.ShapeDtypeStruct((2 * own, cols), BF),
            jax.ShapeDtypeStruct((own, cols), BF),
            jax.ShapeDtypeStruct((own, width), F32),
        ],
        compiler_params=params(),
        cost_estimate=cost(4 * own * width * (width + 2 * cols), 12 * own * width),
        name="model_rows",
    )(pos, *pieces, *weights, *deps)


def input_kernel(count, pos_ref, gain_ref, rgain_ref, tok_ref, runit_ref, rinv_ref, heads_ref, *refs):
    d_refs, (own_ref, sib_ref, spread, u_ref) = refs[:count], refs[count:]
    width = tok_ref.shape[1]
    h = pos_ref[2]
    sib = h + 1 - 2 * lax.rem(h, 2)
    cols = own_ref.shape[1]

    @pl.when(pl.program_id(0) == 0)
    def _():
        groups = runit_ref.shape[0]
        total = d_refs[0][...].astype(F32)
        for ref in d_refs[1:]:
            total = total + ref[...].astype(F32)
        e = total * rgain_ref[...].astype(F32).reshape(1, width)
        unit = runit_ref[...]
        first = jnp.mean(e, axis=-1, keepdims=True)
        second = jnp.mean(e * unit, axis=-1, keepdims=True)
        d_pooled = rinv_ref[:, 0:1] * (e - first - unit * second) / (POOL * POOL)
        spread[...] = jnp.broadcast_to(d_pooled[:, None, :], (groups, POOL, width)).reshape(
            groups * POOL, width
        )

    gain = gain_ref[...].astype(F32).reshape(1, width)
    for part in range(tok_ref.shape[0] // GRID_W):
        at = slice(part * GRID_W, (part + 1) * GRID_W)
        v = tok_ref[at, :].astype(F32)
        d = v - jnp.mean(v, axis=-1, keepdims=True)
        inv = lax.rsqrt(jnp.mean(d * d, axis=-1, keepdims=True) + EPS)
        unit = d * inv
        e = (heads_ref[at, :] + spread[...]) * gain
        first = jnp.mean(e, axis=-1, keepdims=True)
        second = jnp.mean(e * unit, axis=-1, keepdims=True)
        u_ref[at, :] = inv * (e - first - unit * second)
    for ref, owner in ((own_ref, h), (sib_ref, sib)):
        ref[...] = u_ref[:, pl.ds(pl.multiple_of(owner * cols, 128), cols)].astype(BF)


def input_rows(pos, norm_gain, reduce_gain, tokens, unit, inverse, d_heads, parts, n_hd, deps):
    own, width = d_heads.shape
    cols = width // n_hd
    groups = parts[0].shape[0]
    tile = 256
    steps = own // tile
    whole = lambda shape: pl.BlockSpec(shape, lambda i, p: (0,) * len(shape))
    half = lambda shape: pl.BlockSpec(shape, lambda i, p: (p[1], 0))
    return pl.pallas_call(
        after(functools.partial(input_kernel, len(parts)), 7 + len(parts), len(deps)),
        grid_spec=pltpu.PrefetchScalarGridSpec(
            num_scalar_prefetch=1,
            grid=(steps,),
            in_specs=[
                whole((width,)),
                whole((width,)),
                pl.BlockSpec((tile, width), lambda i, p: (p[1] * steps + i, 0)),
                half((groups, width)),
                half((groups, 128)),
                pl.BlockSpec((tile, width), lambda i, p: (i, 0)),
            ]
            + [whole(part.shape) for part in parts]
            + [ANY] * len(deps),
            out_specs=[
                pl.BlockSpec((tile, cols), lambda i, p: (p[1] * steps + i, 0)),
                pl.BlockSpec((tile, cols), lambda i, p: (i, 0)),
            ],
            scratch_shapes=[
                pltpu.VMEM((groups * POOL, width), F32),
                pltpu.VMEM((tile, width), F32),
            ],
        ),
        out_shape=[
            jax.ShapeDtypeStruct((2 * own, cols), BF),
            jax.ShapeDtypeStruct((own, cols), BF),
        ],
        compiler_params=params(),
        cost_estimate=cost(40 * own * width, 16 * own * width),
        name="input_rows",
    )(
        pos,
        norm_gain,
        reduce_gain,
        tokens,
        unit,
        inverse,
        d_heads,
        *parts,
        *deps,
    )


def small(kernel, name, out_shape, *args, pos=None, deps=()):
    smem = [] if pos is None else [pl.BlockSpec(memory_space=pltpu.SMEM)]
    vmem = pl.BlockSpec(memory_space=pltpu.VMEM)
    many = isinstance(out_shape, list)
    return pl.pallas_call(
        after(kernel, len(smem) + len(args), len(deps)),
        in_specs=smem + [vmem] * len(args) + [ANY] * len(deps),
        out_specs=[vmem] * len(out_shape) if many else vmem,
        out_shape=out_shape,
        compiler_params=pltpu.CompilerParams(vmem_limit_bytes=VMEM_LIMIT),
        cost_estimate=cost(1 << 28, 1 << 21),
        name=name,
    )(*([] if pos is None else [pos]), *args, *deps)


def turn_kernel(q_ref, o_ref, out_ref, half_ref, tag_ref):
    tag_ref[...] = jnp.zeros_like(tag_ref)
    q, o = q_ref[...].T, o_ref[...].T
    out_ref[0] = q
    out_ref[1] = o
    half_ref[...] = jnp.where(lax.axis_index("scene") == 0, q, o)


def stack_kernel(n_sp, pos_ref, red_ref, *refs):
    pieces, far_ref, cut_refs = refs[: n_sp - 1], refs[n_sp - 1], refs[n_sp:]
    depth = far_ref.shape[2]
    z = pos_ref[0]
    for k, ref in enumerate(pieces):
        far_ref[k] = ref[...]
    parts = [red_ref[:, i * depth : (i + 1) * depth] for i in range(n_sp)]
    for k, ref in enumerate(cut_refs):
        ref[...] = choose(lax.rem(z + k, n_sp), parts)


def choose(index, values):
    result = values[0]
    for k in range(1, len(values)):
        result = jnp.where(index == k, values[k], result)
    return result


def place_pieces(z, pieces, out_ref, which):
    n_sp, depth = len(pieces), pieces[0].shape[1]
    for place in range(n_sp):
        index = lax.rem(z - place + n_sp, n_sp)
        out_ref[which, :, place * depth : (place + 1) * depth] = choose(index, pieces)


def pack_kernel(n_sp, pos_ref, own_ref, here_ref, there_ref, part_ref, *refs):
    parts, (out_ref, kv_ref) = refs[:-2], refs[-2:]
    feats, depth = own_ref.shape[1:]
    rows = part_ref.shape[0]
    blocks, width = rows // n_sp, depth * n_sp
    z, y = pos_ref[0], pos_ref[3]
    for which in range(2):
        pieces = [own_ref[which]] + [
            jnp.where(y == which, here_ref[k], there_ref[k]) for k in range(n_sp - 1)
        ]
        place_pieces(z, pieces, out_ref, which)
        lanes = slice(which * feats, (which + 1) * feats)
        sums = []
        for j in range(n_sp):
            total = part_ref[j * blocks : (j + 1) * blocks, lanes]
            for k, part in enumerate(parts, 1):
                at = (j - k) % n_sp
                total = total + part[at * blocks : (at + 1) * blocks, lanes].astype(F32)
            sums.append(total)
        kv = jnp.concatenate(sums, axis=0).T.astype(BF)
        out_ref[which, :, width:] = kv
        kv_ref[which] = kv


def pack_far_kernel(pos_ref, here_ref, there_ref, kv_ref, out_ref):
    n_sp, feats, depth = here_ref.shape
    z, y = pos_ref[0], pos_ref[3]
    for which in range(2):
        pieces = [jnp.where(y == which, here_ref[k], there_ref[k]) for k in range(n_sp)]
        place_pieces(z, pieces, out_ref, which)
        out_ref[which, :, n_sp * depth :] = kv_ref[which]


def project_kernel(k_ref, v_ref, own_ref, far_ref, *refs):
    red, (cols_ref, part_ref, low_ref, all_ref) = refs[:-4], refs[-4:]
    all_ref[0] = own_ref[...]
    all_ref[1:] = far_ref[...]
    feats = k_ref.shape[1]
    rows = jnp.concatenate([ref[...] for ref in red], axis=0)
    cols_ref[...] = rows
    for which, ref in ((0, k_ref), (1, v_ref)):
        lanes = slice(which * feats, (which + 1) * feats)
        part = mm(rows, ref[...])
        part_ref[:, lanes] = part
        low_ref[:, lanes] = part.astype(BF)


def back_kernel(n_sp, pos_ref, key_ref, value_ref, here_ref, there_ref, own_ref, *refs):
    parts, (low_ref, mine_ref, other_ref, d_red) = refs[: n_sp - 1], refs[n_sp - 1 :]
    blocks = own_ref.shape[0]
    depth, feats = key_ref.shape
    z, c, y = pos_ref[0], pos_ref[1], pos_ref[3]
    total = own_ref[...]
    for part in parts:
        rows = part[2 * feats :, :].astype(F32)
        total = total + jnp.concatenate(
            [rows[j * blocks : (j + 1) * blocks] for j in range(2 * feats // depth)], axis=1
        )
    low = total.astype(BF)
    low_ref[...] = low
    terms = [mm(low[:, :feats], key_ref[...], NT) + mm(low[:, feats:], value_ref[...], NT)]
    for k in range(n_sp - 1):
        here, there = here_ref[k], there_ref[k]
        key, value = jnp.where(y == 0, here, there), jnp.where(y == 0, there, here)
        terms.append(mm(low[:, :feats], key, NT) + mm(low[:, feats:], value, NT))
    for place in range(n_sp):
        index = lax.rem(z - place + n_sp, n_sp)
        d_red[:, place * depth : (place + 1) * depth] = choose(index, terms)
    half = blocks // 2
    mine_ref[...] = d_red[pl.ds(pl.multiple_of(c * half, half), half), :].astype(BF)
    other_ref[...] = d_red[pl.ds(pl.multiple_of((1 - c) * half, half), half), :].astype(BF)


def half_kernel(k_ref, v_ref, out_ref):
    out_ref[...] = jnp.where(lax.axis_index("scene") == 0, k_ref[...], v_ref[...])


def gather_kernel(*refs):
    for k, ref in enumerate(refs[:-1]):
        refs[-1][k] = ref[...]


def kv_grad_kernel(n_sp, grad_factor, pos_ref, red_ref, d_ref, key_ref, value_ref):
    feats = key_ref.shape[1]
    blocks = d_ref.shape[0] // n_sp
    z = pos_ref[0]
    both = None
    for j in range(n_sp):
        index = lax.rem(z - lax.bitwise_xor(z, j) + n_sp, n_sp)
        red = red_ref[pl.ds(pl.multiple_of(index * blocks, blocks), blocks), :]
        term = mm(red.T, d_ref[j * blocks : (j + 1) * blocks, :])
        both = term if both is None else both + term
    key_ref[...] = both[:, :feats] * grad_factor
    value_ref[...] = both[:, feats:] * grad_factor


def grad_sum_kernel(*refs):
    query_ref, out_ref = refs[-2:]
    for which, ref in ((0, query_ref), (1, out_ref)):
        total = refs[0][which]
        feats = total.shape[0]
        for part in refs[1:-2]:
            total = total + part[which * feats : (which + 1) * feats, :].astype(F32)
        ref[...] = total.T


def on_device(
    tokens,
    norm_gain,
    reduce_gain,
    query_weight,
    key_weight,
    value_weight,
    out_weight,
    out_cotangent,
):
    n_sp, n_hd = lax.axis_size("sp"), lax.axis_size("hd")
    n_x = n_hd // 2
    z, h, y = lax.axis_index("sp"), lax.axis_index("hd"), lax.axis_index("scene")
    c = h % 2
    depth, feats = query_weight.shape
    width = tokens.shape[1]
    own = tokens.shape[0] // 2
    grad_factor = float(2 * own * n_sp) ** (-0.5)
    pos = jnp.stack([z, c, h, y]).astype(jnp.int32)
    others = range(1, n_sp)

    def low(*shape):
        return jax.ShapeDtypeStruct(shape, BF)

    def wide(*shape):
        return jax.ShapeDtypeStruct(shape, F32)

    def to_sp(value, k):
        return lax.ppermute(value, "sp", [(i, (i + k) % n_sp) for i in range(n_sp)])

    def to_xor(value, bit):
        return lax.ppermute(value, "sp", [(i, i ^ bit) for i in range(n_sp)])

    def to_hd(value, k):
        return lax.ppermute(value, "hd", [(i, (i + k) % n_hd) for i in range(n_hd)])

    def swap(value):
        return lax.ppermute(value, "hd", [(i, i ^ 1) for i in range(n_hd)])

    def cross(value):
        return lax.ppermute(value, "scene", [(0, 1), (1, 0)])

    block = pl.BlockSpec((depth, feats), lambda i: (0, 0))
    shard, half, tag = pl.pallas_call(
        turn_kernel,
        grid=(1,),
        in_specs=[block, block],
        out_specs=[fixed((2, feats, depth)), fixed((feats, depth)), fixed((8, 128))],
        out_shape=[low(2, feats, depth), low(feats, depth), wide(8, 128)],
        compiler_params=params(1, TURN_LIMIT),
        name="turn",
    )(query_weight, out_weight)
    here = [to_sp(half, k) for k in others]
    normed, reduced, r_unit, r_inverse = norm_and_pool(tokens, norm_gain, reduce_gain, (tag,))
    blocks = reduced.shape[0]
    far3, *cuts = small(
        functools.partial(stack_kernel, n_sp),
        "stack",
        [low(n_sp - 1, feats, depth)] + [low(blocks, depth)] * n_sp,
        reduced,
        *here,
        pos=pos,
    )
    there3 = cross(far3)

    both = (blocks * n_sp, 2 * feats)
    reduced_cols, kv_part, kv_low, all4 = small(
        project_kernel,
        "project",
        [low(blocks * n_sp, depth), wide(*both), low(*both), low(n_sp, feats, depth)],
        key_weight,
        value_weight,
        half,
        far3,
        cuts[0],
        *[to_sp(cuts[k], k) for k in others],
    )
    x_pieces = [to_hd(all4, 2 * k) for k in range(1, n_x)]
    packed, kv_own = small(
        functools.partial(pack_kernel, n_sp),
        "pack",
        [low(2, feats, width + blocks * n_sp), low(2, feats, blocks * n_sp)],
        shard,
        far3,
        there3,
        kv_part,
        *[to_sp(kv_low, k) for k in others],
        pos=pos,
        deps=tuple(x_pieces),
    )

    kv_half = small(
        half_kernel, "half", low(depth, feats), key_weight, value_weight, deps=(packed,)
    )
    kv_here = [to_sp(kv_half, k) for k in others]
    kv_far = [to_hd(kv_own, 2 * k) for k in range(1, n_x)]

    for_sib, own_pair, grad_own, dkv_own, sends = attend(
        n_sp, pos, normed, out_cotangent, packed, grad_factor, (kv_half, *kv_far)
    )
    packed_sib = swap(packed)
    parts = [to_sp(sends[k - 1], k) for k in others]
    kv_here = small(
        gather_kernel, "gather", low(n_sp - 1, depth, feats), *kv_here, deps=(own_pair, packed_sib)
    )
    kv_there = cross(kv_here)
    pairs, ws = [own_pair, swap(for_sib)], [packed, packed_sib]
    packed_far = [
        small(
            pack_far_kernel,
            "pack_far",
            low(*packed.shape),
            piece,
            cross(piece),
            kv,
            pos=pos,
            deps=(kv_here,),
        )
        for piece, kv in zip(x_pieces, kv_far)
    ]
    far_sib = [attend_far(pos, True, normed, out_cotangent, w, ()) for w in packed_far]
    for w, pair in zip(packed_far, far_sib):
        mine = attend_far(pos, False, normed, out_cotangent, w, (pairs[1], *far_sib))
        pairs += [mine, swap(pair)]
        ws += [w, swap(w)]
    branch, other, d_heads = model_rows(pos, width, pairs, ws, n_hd, ())

    vmem = pl.BlockSpec(memory_space=pltpu.VMEM)
    dkv_rows, d_mine, d_other = pl.pallas_call(
        after(functools.partial(back_kernel, n_sp), 5 + n_sp, 1),
        in_specs=[pl.BlockSpec(memory_space=pltpu.SMEM)] + [vmem] * (4 + n_sp) + [ANY],
        out_specs=[vmem] * 3,
        out_shape=[low(blocks, 2 * feats), low(blocks // 2, width), low(blocks // 2, width)],
        scratch_shapes=[pltpu.VMEM((blocks, width), F32)],
        compiler_params=pltpu.CompilerParams(vmem_limit_bytes=VMEM_LIMIT),
        cost_estimate=cost(1 << 28, 1 << 21),
        name="back",
    )(pos, key_weight, value_weight, kv_here, kv_there, dkv_own, *parts, d_heads)
    d_parts = [d_mine] + [to_hd(d_other if k % 2 else d_mine, k) for k in range(1, n_hd)]
    dkv_all, bit = dkv_rows, 1
    while bit < n_sp:
        dkv_all = jnp.concatenate([dkv_all, to_xor(dkv_all, bit)])
        bit *= 2
    place = (1 - c) * own
    branch = lax.dynamic_update_slice_in_dim(branch, swap(other), place, 0)
    input_grad, other = input_rows(
        pos,
        norm_gain,
        reduce_gain,
        tokens,
        r_unit,
        r_inverse,
        d_heads,
        d_parts,
        n_hd,
        (dkv_all,),
    )
    input_grad = lax.dynamic_update_slice_in_dim(input_grad, swap(other), place, 0)
    query_grad, out_grad = small(
        grad_sum_kernel, "grad_sum", [wide(depth, feats)] * 2, grad_own, *parts, deps=(other,)
    )
    key_grad, value_grad = small(
        functools.partial(kv_grad_kernel, n_sp, grad_factor),
        "kv_grad",
        [wide(depth, feats)] * 2,
        reduced_cols,
        dkv_all,
        pos=pos,
        deps=(other,),
    )
    return (branch, input_grad, query_grad, key_grad, value_grad, out_grad)


def solution(mesh):
    rows, whole, both = P(("scene", "sp"), None), P(), P("sp", "hd")
    out = P(("scene", "sp"), "hd")
    return jax.shard_map(
        on_device,
        mesh=mesh,
        in_specs=(rows, whole, whole, both, both, both, both, rows),
        out_specs=(out,) * 6,
        check_vma=False,
    )
```
